32 devices in a mesh: groups: 2 (over y), row: 16 (over z, x, core).
Axes of the slice: x: 2, y: 2, z: 4, core: 2. Of those that a mesh axis runs over, the one named last changes fastest.
Arguments:
- sigma_blocks: bfloat16 [2, 16, 5, 512, 512], P('groups', 'row'), parts along dimension 0, may hold values from -6 to 6
- first_panel: bfloat16 [2, 16, 512, 512], P('groups', 'row'), parts along dimension 0, may hold values from -0.0625 to 0.0625
- second_panel: bfloat16 [2, 16, 512, 512], P('groups', 'row'), parts along dimension 0, may hold values from -0.0625 to 0.0625
- lower_panel: bfloat16 [1024, 512], P('groups'), parts along dimension 0, may hold values from -0.25 to 0.25
- first_diag: float32 [1024, 512], P('groups'), parts along dimension 0, may hold values from -6 to 6
- second_diag: float32 [1024, 512], P('groups'), parts along dimension 0, may hold values from -6 to 6
- task_list: int32 [2, 16, 5], P('groups', 'row'), parts along dimension 0, may hold values from -2 to 2, as said below
- task_count: int32 [2, 16], P('groups', 'row'), parts along dimension 0, may hold values from 1 to 5, as said below
Outputs:
- column_first: bfloat16 [2, 16, 512, 512], P('groups', 'row'), parts along dimension 0
- block_first: float32 [1024, 512], P('groups'), parts along dimension 0
- block_link: float32 [1024, 512], P('groups'), parts along dimension 0
- column_second: bfloat16 [2, 16, 512, 512], P('groups', 'row'), parts along dimension 0
- block_second: float32 [1024, 512], P('groups'), parts along dimension 0
The draws below stay inside these ranges and needn't reach their ends.
There are 2 independent parts, one for each index of `groups`. The reference program is written for one: setup_inputs(seed, part) draws one part's arguments, and reference() takes and returns one part's arrays. A program takes and returns all parts, laid end to end along the dimension named above; each array names one. Nothing has to cross between parts.
Inputs may be any that keep to these rules, and one draw needn't show every extreme that they name: For slots s < task_count, block row i + task_list[i, s] lies in 0 to 15; the live offsets of a row are distinct, increasing, and include 0; slots from task_count on hold 0. `task_count`: some block row has all 5 couplings live and some has only its own.
All inputs are finite; a program needn't handle non-finite values.
Results may differ from the reference program's by a relative error of at most 0.0041.
Values may be sent and summed in bfloat16 or wider, within the bound.
No kernel may reach another device: no remote copies, remote signals or barrier semaphores. Data moves between devices by JAX's collectives and lax.ppermute only.
A program may use at most 64 MiB of HBM per device.

```python
import jax
import jax.numpy as jnp
from jax import lax

B = 512
SPAN = 2
SLOTS = 5
BR_DEV = 1
NBLK = 16
N_ROW = 16


def pattern(key):
    total_rows = BR_DEV * N_ROW
    coins = jax.random.randint(key, (total_rows, SLOTS), 0, 2)
    offsets = jnp.arange(SLOTS, dtype=jnp.int32) - SPAN
    rows_index = jnp.arange(total_rows, dtype=jnp.int32)[:, None]
    target = rows_index + offsets[None, :]
    inside = (target >= 0) & (target < total_rows)
    full_row = rows_index == total_rows // 2
    lone_row = rows_index == 0
    live = jnp.where(offsets[None, :] == 0, 1, jnp.where(full_row, 1, jnp.where(lone_row, 0, coins)))
    live = jnp.where(inside, live, 0)
    score = (1 - live) * SLOTS + jnp.arange(SLOTS, dtype=jnp.int32)[None, :]
    order = jnp.argsort(score, axis=1)
    listed = jnp.take_along_axis(jnp.broadcast_to(offsets[None, :], (total_rows, SLOTS)), order, axis=1)
    count = jnp.sum(live, axis=1)
    listed = jnp.where(jnp.arange(SLOTS, dtype=jnp.int32)[None, :] < count[:, None], listed, 0)
    return (listed.reshape((BR_DEV, N_ROW, SLOTS)).astype(jnp.int32), count.reshape((BR_DEV, N_ROW)).astype(jnp.int32))


def draw_task_list(key, part):
    listed, count = pattern(key)
    return listed


def draw_task_count(key, part):
    listed, count = pattern(key)
    return count


def block_scale(key, dims, cuts, least, top_value):
    def one(position, blocks):
        draws = jax.random.uniform(jax.random.fold_in(jax.random.fold_in(key, 6), position), (blocks,), jnp.float32, least / len(cuts), top_value / len(cuts))
        return jnp.repeat(jnp.exp(draws), dims[position] // blocks).reshape((-1,) + (1,) * (len(dims) - position - 1))

    level = one(*cuts[0])
    for cut in cuts[1:]:
        level = level * one(*cut)
    return level


def bell_draw(own_key, extent, scale, most, pieces=(), kind=jnp.bfloat16):
    factor_of = block_scale(own_key, extent, pieces, -0.22, 0.18) if pieces else 1.0
    values = jax.random.normal(own_key, extent, jnp.float32) * scale * factor_of
    return jnp.minimum(jnp.maximum(values, -most), most).astype(kind)


def setup_inputs(seed: int = 0, part: int = 0) -> dict:
    key_list = jax.random.split(jax.random.key(seed), 9)
    part_splits = jax.random.split(jax.random.fold_in(key_list[8], part), 9)
    sigma_blocks = bell_draw(part_splits[0], (BR_DEV, N_ROW, SLOTS, B, B), ((NBLK / SLOTS) ** 0.5), 6.0, ((1, 16),))
    first_panel = bell_draw(part_splits[1], (BR_DEV, N_ROW, B, B), (NBLK * B) ** -0.5, 0.0625, ((1, 16),))
    second_panel = bell_draw(part_splits[2], (BR_DEV, N_ROW, B, B), (NBLK * B) ** -0.5, 0.0625, ((1, 16),))
    lower_panel = bell_draw(part_splits[3], (B, B), B ** -0.5, 0.25)
    first_diag = bell_draw(part_splits[4], (B, B), 1.0, 6.0, (), jnp.float32)
    second_diag = bell_draw(part_splits[5], (B, B), 1.0, 6.0, (), jnp.float32)
    task_list = draw_task_list(jax.random.fold_in(jax.random.fold_in(key_list[8], part), 71), part)
    task_count = draw_task_count(jax.random.fold_in(jax.random.fold_in(key_list[8], part), 71), part)
    return {"sigma_blocks": sigma_blocks, "first_panel": first_panel, "second_panel": second_panel, "lower_panel": lower_panel, "first_diag": first_diag, "second_diag": second_diag, "task_list": task_list, "task_count": task_count}


def band_product(sigma_blocks, panel, task_list, task_count):
    total_rows = sigma_blocks.shape[0] * sigma_blocks.shape[1]
    slot_count = sigma_blocks.shape[2]
    width = sigma_blocks.shape[-1]
    blocks = sigma_blocks.reshape((total_rows, slot_count, width, width))
    panels = panel.reshape((total_rows, width, panel.shape[-1]))
    listed = task_list.reshape((total_rows, slot_count))
    counts = task_count.reshape((total_rows,))

    def one_row(block_index):
        target = jnp.clip(block_index + listed[block_index], 0, total_rows - 1).astype(jnp.int32)
        live = (jnp.arange(slot_count, dtype=jnp.int32) < counts[block_index]).astype(jnp.float32)
        chosen = panels[target].astype(jnp.float32)
        weighted = blocks[block_index].astype(jnp.float32) * live[:, None, None]
        return jnp.einsum('kab,kbc->ac', weighted, chosen)

    result = lax.map(one_row, jnp.arange(total_rows, dtype=jnp.int32))
    return result.reshape(panel.shape)


def reference(sigma_blocks, first_panel, second_panel, lower_panel, first_diag, second_diag, task_list, task_count):
    first_band = band_product(sigma_blocks, first_panel, task_list, task_count)
    column_first = (-first_band).astype(jnp.bfloat16)
    first_f = first_panel.astype(jnp.float32)
    second_f = second_panel.astype(jnp.float32)
    column_first_f = column_first.astype(jnp.float32)
    lower_f = lower_panel.astype(jnp.float32)
    block_first = first_diag - jnp.einsum('jnab,jnac->bc', first_f, column_first_f)
    cross = jnp.einsum('jnab,jnac->bc', column_first_f, second_f)
    link = jnp.dot(block_first, lower_f, precision=lax.Precision.HIGHEST) + cross
    block_link = -link
    second_band = band_product(sigma_blocks, second_panel, task_list, task_count)
    second_total = second_band + jnp.einsum('jnab,bc->jnac', column_first_f, lower_f)
    column_second = (-second_total).astype(jnp.bfloat16)
    block_second = second_diag + jnp.dot(lower_f.T, link, precision=lax.Precision.HIGHEST) - jnp.einsum('jnab,jnac->bc', second_f, column_second.astype(jnp.float32))
    return column_first, block_first, block_link, column_second, block_second
```

```python
import functools

import jax
import jax.numpy as jnp
from jax import lax
from jax.experimental import pallas as pl
from jax.experimental.pallas import tpu as pltpu
from jax.sharding import PartitionSpec as P

VMEM_BYTES = 40 * 1024 * 1024


def vmem_spec():
    return pl.BlockSpec(memory_space=pltpu.VMEM)


def smem_spec():
    return pl.BlockSpec(memory_space=pltpu.SMEM)


def call(body, outs, args, scalars, scratch, flops):
    moved = sum(a.size * a.dtype.itemsize for a in args) + sum(o.size * o.dtype.itemsize for o in outs)
    return pl.pallas_call(
        body,
        out_shape=outs,
        in_specs=[smem_spec()] * scalars + [vmem_spec()] * (len(args) - scalars),
        out_specs=[vmem_spec()] * len(outs),
        scratch_shapes=scratch,
        compiler_params=pltpu.CompilerParams(vmem_limit_bytes=VMEM_BYTES),
        cost_estimate=pl.CostEstimate(flops=flops, bytes_accessed=moved, transcendentals=0),
    )(*args)


def dot(a, b):
    return lax.dot_general(a, b, (((1,), (0,)), ((), ())), preferred_element_type=jnp.float32)


def dot_t(a, b):
    return lax.dot_general(a, b, (((0,), (0,)), ((), ())), preferred_element_type=jnp.float32)


def band(where_ref, list_ref, count_ref, sigma_ref, panels, acc_ref):
    member = where_ref[0] % 4
    across = jnp.where(member < 2, 2, -2)
    beside = jnp.where(member % 2 == 0, 1, -1)
    offsets = (0, beside, across, -across, -beside)
    acc_ref[...] = jnp.zeros_like(acc_ref)
    for offset, panel in zip(offsets, panels):
        slot = jnp.int32(0)
        live = jnp.int32(0)
        for s in range(sigma_ref.shape[0]):
            hit = (list_ref[s] == offset) & (s < count_ref[0])
            slot = jnp.where(hit, s, slot)
            live = jnp.where(hit, 1, live)

        @pl.when(live == 1)
        def _(slot=slot, panel=panel):
            acc_ref[...] += dot(sigma_ref[slot], panel[...])


def first_kernel(where_ref, list_ref, count_ref, sigma_ref, own, beside, across, far, rest, second_ref,
                 column_ref, parts_ref, acc_ref):
    band(where_ref, list_ref, count_ref, sigma_ref, (own, beside, across, far, rest), acc_ref)
    column = (-acc_ref[...]).astype(jnp.bfloat16)
    column_ref[...] = column
    chunks, _, rows, width = parts_ref.shape
    diag = -dot_t(own[...], column)
    parts_ref[:, 0] = diag.astype(jnp.bfloat16).reshape(chunks, rows, width)
    cross = dot_t(column, second_ref[...])
    parts_ref[:, 1] = cross.astype(jnp.bfloat16).reshape(chunks, rows, width)


def second_kernel(where_ref, list_ref, count_ref, sigma_ref, own, beside, across, far, rest, column_first_ref,
                  lower_ref, column_ref, parts_ref, acc_ref):
    band(where_ref, list_ref, count_ref, sigma_ref, (own, beside, across, far, rest), acc_ref)
    total = acc_ref[...] + dot(column_first_ref[...], lower_ref[...])
    column = (-total).astype(jnp.bfloat16)
    column_ref[...] = column
    chunks, rows, width = parts_ref.shape
    parts_ref[...] = (-dot_t(own[...], column)).astype(jnp.bfloat16).reshape(chunks, rows, width)


def split(value):
    high = value.astype(jnp.bfloat16)
    low = (value - high.astype(jnp.float32)).astype(jnp.bfloat16)
    return high, low


def final_kernel(sums_ref, second_sum_ref, lower_ref, first_diag_ref, second_diag_ref, first_ref, link_ref, second_ref):
    size = lower_ref.shape
    lower = lower_ref[...]
    block_first = first_diag_ref[...] + sums_ref[:, 0].astype(jnp.float32).reshape(size)
    first_ref[...] = block_first
    high, low = split(block_first)
    link = dot(high, lower) + dot(low, lower) + sums_ref[:, 1].astype(jnp.float32).reshape(size)
    link_ref[...] = -link
    high, low = split(link)
    second_ref[...] = (
        second_diag_ref[...]
        + dot_t(lower, high)
        + dot_t(lower, low)
        + second_sum_ref[...].astype(jnp.float32).reshape(size)
    )


def exchange(panel, member, devices):
    beside = lax.ppermute(panel, "row", [(i, i ^ 1) for i in range(devices)])
    across = lax.ppermute(panel, "row", [(i, i ^ 2) for i in range(devices)])
    hops = [(i, i + 4 if i % 4 < 2 else i - 4) for i in range(devices)]
    far = lax.ppermute(across, "row", [(a, b) for a, b in hops if 0 <= b < devices])
    give_across = (member == 0) | (member == 3)
    rest = lax.ppermute(jnp.where(give_across, across, far), "row", [(i, i ^ 1) for i in range(devices)])
    return beside, across, far, rest


def summed(parts):
    devices = parts.shape[0]
    mine = lax.all_to_all(parts, "row", 0, 0, tiled=True)
    total = jnp.sum(mine.astype(jnp.float32), axis=0).astype(jnp.bfloat16)
    return lax.all_to_all(jnp.broadcast_to(total[None], (devices,) + total.shape), "row", 0, 0, tiled=True)


def shards(sigma_blocks, first_panel, second_panel, lower_panel, first_diag, second_diag, task_list, task_count):
    devices = lax.axis_size("row")
    position = lax.axis_index("row").astype(jnp.int32)
    member = position % 4
    slots, size, width = sigma_blocks.shape[-3:]
    sigma = sigma_blocks.reshape((slots, size, width))
    first = first_panel.reshape((size, width))
    second = second_panel.reshape((size, width))
    where = position.reshape((1,))
    listed = task_list.reshape((slots,))
    count = task_count.reshape((1,))
    one = 2 * size * size * width
    rows = size // devices

    first_near = exchange(first, member, devices)
    second_near = exchange(second, member, devices)
    column_first, parts = call(
        first_kernel,
        [jax.ShapeDtypeStruct((size, width), jnp.bfloat16), jax.ShapeDtypeStruct((devices, 2, rows, width), jnp.bfloat16)],
        [where, listed, count, sigma, first, *first_near, second],
        3,
        [pltpu.VMEM((size, width), jnp.float32)],
        7 * one,
    )
    column_second, second_parts = call(
        second_kernel,
        [jax.ShapeDtypeStruct((size, width), jnp.bfloat16), jax.ShapeDtypeStruct((devices, rows, width), jnp.bfloat16)],
        [where, listed, count, sigma, second, *second_near, column_first, lower_panel],
        3,
        [pltpu.VMEM((size, width), jnp.float32)],
        7 * one,
    )
    sums = summed(parts)
    second_sum = summed(second_parts)
    wide = jax.ShapeDtypeStruct((size, width), jnp.float32)
    block_first, block_link, block_second = call(
        final_kernel,
        [wide] * 3,
        [sums, second_sum, lower_panel, first_diag, second_diag],
        0,
        [],
        4 * one,
    )
    shape = first_panel.shape
    return column_first.reshape(shape), block_first, block_link, column_second.reshape(shape), block_second


def solution(mesh):
    return jax.shard_map(
        shards,
        mesh=mesh,
        in_specs=(
            P("groups", "row", None, None, None),
            P("groups", "row", None, None),
            P("groups", "row", None, None),
            P("groups", None),
            P("groups", None),
            P("groups", None),
            P("groups", "row", None),
            P("groups", "row"),
        ),
        out_specs=(
            P("groups", "row", None, None),
            P("groups", None),
            P("groups", None),
            P("groups", "row", None, None),
            P("groups", None),
        ),
        check_vma=False,
    )
```

```python
import functools

import jax
import jax.numpy as jnp
from jax import lax
from jax.experimental import pallas as pl
from jax.experimental.pallas import tpu as pltpu
from jax.sharding import PartitionSpec as P

VMEM_BYTES = 40 * 1024 * 1024


def vmem_spec():
    return pl.BlockSpec(memory_space=pltpu.VMEM)


def smem_spec():
    return pl.BlockSpec(memory_space=pltpu.SMEM)


def call(body, outs, args, scalars, scratch, flops):
    moved = sum(a.size * a.dtype.itemsize for a in args) + sum(o.size * o.dtype.itemsize for o in outs)
    return pl.pallas_call(
        body,
        out_shape=outs,
        in_specs=[smem_spec()] * scalars + [vmem_spec()] * (len(args) - scalars),
        out_specs=[vmem_spec()] * len(outs),
        scratch_shapes=scratch,
        compiler_params=pltpu.CompilerParams(vmem_limit_bytes=VMEM_BYTES),
        cost_estimate=pl.CostEstimate(flops=flops, bytes_accessed=moved, transcendentals=0),
    )(*args)


def dot(a, b):
    return lax.dot_general(a, b, (((1,), (0,)), ((), ())), preferred_element_type=jnp.float32)


def dot_t(a, b):
    return lax.dot_general(a, b, (((0,), (0,)), ((), ())), preferred_element_type=jnp.float32)


def band(where_ref, list_ref, count_ref, sigma_ref, panels, acc_ref):
    member = where_ref[0] % 4
    across = jnp.where(member < 2, 2, -2)
    beside = jnp.where(member % 2 == 0, 1, -1)
    offsets = (0, beside, across, -across, -beside)
    acc_ref[...] = jnp.zeros_like(acc_ref)
    for offset, panel in zip(offsets, panels):
        slot = jnp.int32(0)
        live = jnp.int32(0)
        for s in range(sigma_ref.shape[0]):
            hit = (list_ref[s] == offset) & (s < count_ref[0])
            slot = jnp.where(hit, s, slot)
            live = jnp.where(hit, 1, live)

        @pl.when(live == 1)
        def _(slot=slot, panel=panel):
            acc_ref[...] += dot(sigma_ref[slot], panel[...])


def halves(value, where_ref, scratch_ref, give_ref, keep_ref, index):
    scratch_ref[...] = value
    half = value.shape[0] // 2
    core = where_ref[0] % 2
    keep_ref[index] = scratch_ref[pl.ds(pl.multiple_of(core * half, half), half)]
    give_ref[index] = scratch_ref[pl.ds(pl.multiple_of((1 - core) * half, half), half)].astype(jnp.bfloat16)


def first_kernel(where_ref, list_ref, count_ref, sigma_ref, own, beside, across, far, rest, second_ref,
                 column_ref, give_ref, keep_ref, acc_ref):
    band(where_ref, list_ref, count_ref, sigma_ref, (own, beside, across, far, rest), acc_ref)
    column = (-acc_ref[...]).astype(jnp.bfloat16)
    column_ref[...] = column
    halves(-dot_t(own[...], column), where_ref, acc_ref, give_ref, keep_ref, 0)
    halves(dot_t(column, second_ref[...]), where_ref, acc_ref, give_ref, keep_ref, 1)


def second_kernel(where_ref, list_ref, count_ref, sigma_ref, own, beside, across, far, rest, column_first_ref,
                  lower_ref, column_ref, give_ref, keep_ref, acc_ref):
    band(where_ref, list_ref, count_ref, sigma_ref, (own, beside, across, far, rest), acc_ref)
    total = acc_ref[...] + dot(column_first_ref[...], lower_ref[...])
    column = (-total).astype(jnp.bfloat16)
    column_ref[...] = column
    halves(-dot_t(own[...], column), where_ref, acc_ref, give_ref, keep_ref, 0)


def split(value):
    high = value.astype(jnp.bfloat16)
    low = (value - high.astype(jnp.float32)).astype(jnp.bfloat16)
    return high, low


def place(where_ref, mine_ref, other_ref, index, out_ref):
    half = mine_ref.shape[1]
    core = where_ref[0] % 2
    out_ref[pl.ds(pl.multiple_of(core * half, half), half)] = mine_ref[index].astype(jnp.float32)
    out_ref[pl.ds(pl.multiple_of((1 - core) * half, half), half)] = other_ref[index].astype(jnp.float32)


def link_kernel(where_ref, mine_ref, other_ref, lower_ref, first_diag_ref, second_diag_ref,
                first_ref, link_ref, base_ref, sum_ref):
    lower = lower_ref[...]
    place(where_ref, mine_ref, other_ref, 0, sum_ref)
    block_first = first_diag_ref[...] + sum_ref[...]
    first_ref[...] = block_first
    place(where_ref, mine_ref, other_ref, 1, sum_ref)
    high, low = split(block_first)
    link = dot(high, lower) + dot(low, lower) + sum_ref[...]
    link_ref[...] = -link
    high, low = split(link)
    base_ref[...] = second_diag_ref[...] + dot_t(lower, high) + dot_t(lower, low)


def last_kernel(where_ref, mine_ref, other_ref, base_ref, second_ref):
    place(where_ref, mine_ref, other_ref, 0, second_ref)
    second_ref[...] += base_ref[...]


def swapped(value, bit, devices):
    return lax.ppermute(value, "row", [(i, i ^ bit) for i in range(devices)])


def far_of(across, devices):
    hops = [(i, i + 4 if i % 4 < 2 else i - 4) for i in range(devices)]
    return lax.ppermute(across, "row", [(a, b) for a, b in hops if 0 <= b < devices])


def rest_of(across, far, member, devices):
    give_across = (member == 0) | (member == 3)
    return swapped(jnp.where(give_across, across, far), 1, devices)


def summed(give, keep, position, devices):
    total = keep + swapped(give, 1, devices).astype(jnp.float32)
    bits = [2 ** b for b in range(1, devices.bit_length() - 1)]
    for bit in bits:
        k, rows, width = total.shape
        pair = total.reshape((k, 2, rows // 2, width))
        mine = (position // bit) % 2
        give = lax.dynamic_index_in_dim(pair, 1 - mine, 1, keepdims=False).astype(jnp.bfloat16)
        keep = lax.dynamic_index_in_dim(pair, mine, 1, keepdims=False)
        total = keep + swapped(give, bit, devices).astype(jnp.float32)
    gathered = total.astype(jnp.bfloat16)
    for bit in bits[::-1]:
        other = swapped(gathered, bit, devices)
        mine = (position // bit) % 2
        low = jnp.where(mine == 0, gathered, other)
        high = jnp.where(mine == 0, other, gathered)
        gathered = jnp.concatenate([low, high], axis=1)
    return gathered, swapped(gathered, 1, devices)


def shards(sigma_blocks, first_panel, second_panel, lower_panel, first_diag, second_diag, task_list, task_count):
    devices = lax.axis_size("row")
    position = lax.axis_index("row").astype(jnp.int32)
    member = position % 4
    slots, size, width = sigma_blocks.shape[-3:]
    sigma = sigma_blocks.reshape((slots, size, width))
    first = first_panel.reshape((size, width))
    second = second_panel.reshape((size, width))
    where = position.reshape((1,))
    listed = task_list.reshape((slots,))
    count = task_count.reshape((1,))
    one = 2 * size * size * width
    half = size // 2
    narrow = jax.ShapeDtypeStruct((size, width), jnp.bfloat16)
    wide = jax.ShapeDtypeStruct((size, width), jnp.float32)
    scratch = [pltpu.VMEM((size, width), jnp.float32)]

    def parts(k):
        return [jax.ShapeDtypeStruct((k, half, width), t) for t in (jnp.bfloat16, jnp.float32)]

    across = swapped(first, 2, devices)
    beside = swapped(first, 1, devices)
    across, later = lax.optimization_barrier((across, second))
    far = far_of(across, devices)
    second_across = swapped(later, 2, devices)
    second_beside = swapped(later, 1, devices)
    rest = rest_of(across, far, member, devices)
    second_far = far_of(second_across, devices)
    second_rest = rest_of(second_across, second_far, member, devices)
    column_first, give, keep = call(
        first_kernel,
        [narrow] + parts(2),
        [where, listed, count, sigma, first, beside, across, far, rest, second],
        3,
        scratch,
        7 * one,
    )
    column_second, second_give, second_keep = call(
        second_kernel,
        [narrow] + parts(1),
        [where, listed, count, sigma, second, second_beside, second_across, second_far, second_rest,
         column_first, lower_panel],
        3,
        scratch,
        7 * one,
    )
    mine, other = summed(give, keep, position, devices)
    second_mine, second_other = summed(second_give, second_keep, position, devices)
    block_first, block_link, base = call(
        link_kernel, [wide] * 3, [where, mine, other, lower_panel, first_diag, second_diag], 1, scratch, 4 * one
    )
    (block_second,) = call(last_kernel, [wide], [where, second_mine, second_other, base], 1, [], size * width)
    shape = first_panel.shape
    return column_first.reshape(shape), block_first, block_link, column_second.reshape(shape), block_second


def solution(mesh):
    return jax.shard_map(
        shards,
        mesh=mesh,
        in_specs=(
            P("groups", "row", None, None, None),
            P("groups", "row", None, None),
            P("groups", "row", None, None),
            P("groups", None),
            P("groups", None),
            P("groups", None),
            P("groups", "row", None),
            P("groups", "row"),
        ),
        out_specs=(
            P("groups", "row", None, None),
            P("groups", None),
            P("groups", None),
            P("groups", "row", None, None),
            P("groups", None),
        ),
        check_vma=False,
    )
```

```python
import functools

import jax
import jax.numpy as jnp
from jax import lax
from jax.experimental import pallas as pl
from jax.experimental.pallas import tpu as pltpu
from jax.sharding import PartitionSpec as P

VMEM_BYTES = 24 * 1024 * 1024


def vmem_spec():
    return pl.BlockSpec(memory_space=pltpu.VMEM)


def smem_spec():
    return pl.BlockSpec(memory_space=pltpu.SMEM)


def call(body, outs, args, scalars, flops, scratch=()):
    moved = sum(a.size * a.dtype.itemsize for a in args) + sum(o.size * o.dtype.itemsize for o in outs)
    return pl.pallas_call(
        body,
        out_shape=outs,
        in_specs=[smem_spec()] * scalars + [vmem_spec()] * (len(args) - scalars),
        out_specs=[vmem_spec()] * len(outs),
        scratch_shapes=list(scratch),
        compiler_params=pltpu.CompilerParams(vmem_limit_bytes=VMEM_BYTES),
        cost_estimate=pl.CostEstimate(flops=flops, bytes_accessed=moved, transcendentals=0),
    )(*args)


def dot(a, b):
    return lax.dot_general(a, b, (((1,), (0,)), ((), ())), preferred_element_type=jnp.float32)


def dot_t(a, b):
    return lax.dot_general(a, b, (((0,), (0,)), ((), ())), preferred_element_type=jnp.float32)


def offsets_of(where_ref):
    member = where_ref[0] % 4
    across = jnp.where(member < 2, 2, -2)
    beside = jnp.where(member % 2 == 0, 1, -1)
    return jnp.int32(0), beside, across, -across, -beside


def add_products(list_ref, count_ref, sigma_ref, offset, pairs):
    slot = jnp.int32(0)
    live = jnp.int32(0)
    for s in range(sigma_ref.shape[0]):
        hit = (list_ref[s] == offset) & (s < count_ref[0])
        slot = jnp.where(hit, s, slot)
        live = jnp.where(hit, 1, live)

    @pl.when(live == 1)
    def _():
        for acc_ref, panel_ref in pairs:
            acc_ref[...] += dot(sigma_ref[slot], panel_ref[...])


def near_kernel(where_ref, list_ref, count_ref, sigma_ref, first, second, first_beside, second_beside,
                first_acc, second_acc, turned_ref):
    own, beside = offsets_of(where_ref)[:2]
    first_acc[...] = jnp.zeros_like(first_acc)
    second_acc[...] = jnp.zeros_like(second_acc)
    add_products(list_ref, count_ref, sigma_ref, own, ((first_acc, first), (second_acc, second)))
    add_products(list_ref, count_ref, sigma_ref, beside, ((first_acc, first_beside), (second_acc, second_beside)))
    size = first.shape[0]
    turned_ref[:size] = first[...].T
    turned_ref[size:] = second[...].T


def across_kernel(where_ref, list_ref, count_ref, sigma_ref, first_in, second_in, first_across, second_across,
                  first_acc, second_acc):
    first_acc[...] = first_in[...]
    second_acc[...] = second_in[...]
    across = offsets_of(where_ref)[2]
    add_products(list_ref, count_ref, sigma_ref, across, ((first_acc, first_across), (second_acc, second_across)))


def halves(value, where_ref, scratch_ref, give_ref, keep_ref, index):
    scratch_ref[...] = value
    half = value.shape[0] // 2
    core = where_ref[0] % 2
    keep_ref[index] = scratch_ref[pl.ds(pl.multiple_of(core * half, half), half)]
    give_ref[index] = scratch_ref[pl.ds(pl.multiple_of((1 - core) * half, half), half)].astype(jnp.bfloat16)


def first_kernel(where_ref, list_ref, count_ref, sigma_ref, acc_in, far, rest, turned_ref,
                 column_ref, give_ref, keep_ref, acc_ref):
    acc_ref[...] = acc_in[...]
    offsets = offsets_of(where_ref)
    add_products(list_ref, count_ref, sigma_ref, offsets[3], ((acc_ref, far),))
    add_products(list_ref, count_ref, sigma_ref, offsets[4], ((acc_ref, rest),))
    column = (-acc_ref[...]).astype(jnp.bfloat16)
    column_ref[...] = column
    size = column.shape[0]
    halves(-dot(turned_ref[:size], column), where_ref, acc_ref, give_ref, keep_ref, 0)
    halves(dot(turned_ref[size:], column), where_ref, acc_ref, give_ref, keep_ref, 1)


def lower_kernel(acc_in, column_ref, lower_ref, acc_ref):
    acc_ref[...] = acc_in[...] + dot(column_ref[...], lower_ref[...])


def second_kernel(where_ref, list_ref, count_ref, sigma_ref, acc_in, far, rest, turned_ref,
                  column_ref, give_ref, keep_ref, acc_ref):
    acc_ref[...] = acc_in[...]
    offsets = offsets_of(where_ref)
    add_products(list_ref, count_ref, sigma_ref, offsets[3], ((acc_ref, far),))
    add_products(list_ref, count_ref, sigma_ref, offsets[4], ((acc_ref, rest),))
    column = (-acc_ref[...]).astype(jnp.bfloat16)
    column_ref[...] = column
    size = column.shape[0]
    halves(-dot(turned_ref[size:], column), where_ref, acc_ref, give_ref, keep_ref, 0)


def split(value):
    high = value.astype(jnp.bfloat16)
    low = (value - high.astype(jnp.float32)).astype(jnp.bfloat16)
    return high, low


def place(where_ref, mine_ref, other_ref, index, out_ref):
    half = mine_ref.shape[1]
    core = where_ref[0] % 2
    out_ref[pl.ds(pl.multiple_of(core * half, half), half)] = mine_ref[index].astype(jnp.float32)
    out_ref[pl.ds(pl.multiple_of((1 - core) * half, half), half)] = other_ref[index].astype(jnp.float32)


def link_kernel(where_ref, mine_ref, other_ref, lower_ref, first_diag_ref, second_diag_ref,
                first_ref, link_ref, base_ref, sum_ref):
    lower = lower_ref[...]
    place(where_ref, mine_ref, other_ref, 0, sum_ref)
    block_first = first_diag_ref[...] + sum_ref[...]
    first_ref[...] = block_first
    place(where_ref, mine_ref, other_ref, 1, sum_ref)
    high, low = split(block_first)
    link = dot(high, lower) + dot(low, lower) + sum_ref[...].T
    link_ref[...] = -link
    high, low = split(link)
    base_ref[...] = second_diag_ref[...] + dot_t(lower, high) + dot_t(lower, low)


def last_kernel(where_ref, mine_ref, other_ref, base_ref, second_ref):
    place(where_ref, mine_ref, other_ref, 0, second_ref)
    second_ref[...] += base_ref[...]


def swapped(value, bit, devices):
    return lax.ppermute(value, "row", [(i, i ^ bit) for i in range(devices)])


def far_of(across, devices):
    hops = [(i, i + 4 if i % 4 < 2 else i - 4) for i in range(devices)]
    return lax.ppermute(across, "row", [(a, b) for a, b in hops if 0 <= b < devices])


def rest_of(across, far, member, devices):
    give_across = (member == 0) | (member == 3)
    return swapped(jnp.where(give_across, across, far), 1, devices)


def core_summed(give, keep, position, devices):
    return halved(keep + swapped(give, 1, devices).astype(jnp.float32), 2, position)


def halved(total, bit, position):
    k, rows, width = total.shape
    pair = total.reshape((k, 2, rows // 2, width))
    mine = (position // bit) % 2
    give = lax.dynamic_index_in_dim(pair, 1 - mine, 1, keepdims=False).astype(jnp.bfloat16)
    return give, lax.dynamic_index_in_dim(pair, mine, 1, keepdims=False)


def summed(give, keep, position, devices):
    bits = [2 ** b for b in range(1, devices.bit_length() - 1)]
    for bit in bits:
        total = keep + swapped(give, bit, devices).astype(jnp.float32)
        if bit != bits[-1]:
            give, keep = halved(total, 2 * bit, position)
    gathered = total.astype(jnp.bfloat16)
    for bit in bits[::-1]:
        other = swapped(gathered, bit, devices)
        mine = (position // bit) % 2
        low = jnp.where(mine == 0, gathered, other)
        high = jnp.where(mine == 0, other, gathered)
        gathered = jnp.concatenate([low, high], axis=1)
    return gathered, swapped(gathered, 1, devices)


def shards(sigma_blocks, first_panel, second_panel, lower_panel, first_diag, second_diag, task_list, task_count):
    devices = lax.axis_size("row")
    position = lax.axis_index("row").astype(jnp.int32)
    member = position % 4
    slots, size, width = sigma_blocks.shape[-3:]
    sigma = sigma_blocks.reshape((slots, size, width))
    first = first_panel.reshape((size, width))
    second = second_panel.reshape((size, width))
    where = position.reshape((1,))
    listed = task_list.reshape((slots,))
    count = task_count.reshape((1,))
    one = 2 * size * size * width
    half = size // 2
    narrow = jax.ShapeDtypeStruct((size, width), jnp.bfloat16)
    wide = jax.ShapeDtypeStruct((size, width), jnp.float32)
    scratch = [pltpu.VMEM((size, width), jnp.float32)]

    def parts(k):
        return [jax.ShapeDtypeStruct((k, half, width), t) for t in (jnp.bfloat16, jnp.float32)]

    scalars = [where, listed, count, sigma]
    across = swapped(first, 2, devices)
    beside = swapped(first, 1, devices)
    second_beside = swapped(second, 1, devices)
    first_acc, second_acc, turned = call(
        near_kernel,
        [wide, wide, jax.ShapeDtypeStruct((2 * size, width), jnp.bfloat16)],
        scalars + [first, second, beside, second_beside],
        3,
        4 * one,
    )
    across, later = lax.optimization_barrier((across, second))
    far = far_of(across, devices)
    second_across = swapped(later, 2, devices)
    rest = rest_of(across, far, member, devices)
    second_far = far_of(second_across, devices)
    first_acc, second_acc = call(
        across_kernel, [wide, wide], scalars + [first_acc, second_acc, across, second_across], 3, 2 * one
    )
    column_first, give, keep = call(
        first_kernel, [narrow] + parts(2), scalars + [first_acc, far, rest, turned], 3, 4 * one, scratch
    )
    give, second_across = lax.optimization_barrier((give, second_across))
    second_rest = rest_of(second_across, second_far, member, devices)
    give, keep = core_summed(give, keep, position, devices)
    (second_acc,) = call(lower_kernel, [wide], [second_acc, column_first, lower_panel], 0, one)
    give, second_rest = lax.optimization_barrier((give, second_rest))
    column_second, second_give, second_keep = call(
        second_kernel, [narrow] + parts(1), scalars + [second_acc, second_far, second_rest, turned], 3, 3 * one, scratch
    )
    mine, other = summed(give, keep, position, devices)
    second_give, second_keep = core_summed(second_give, second_keep, position, devices)
    second_mine, second_other = summed(second_give, second_keep, position, devices)
    block_first, block_link, base = call(
        link_kernel, [wide] * 3, [where, mine, other, lower_panel, first_diag, second_diag], 1, 4 * one, scratch
    )
    (block_second,) = call(last_kernel, [wide], [where, second_mine, second_other, base], 1, size * width)
    shape = first_panel.shape
    return column_first.reshape(shape), block_first, block_link, column_second.reshape(shape), block_second


def solution(mesh):
    return jax.shard_map(
        shards,
        mesh=mesh,
        in_specs=(
            P("groups", "row", None, None, None),
            P("groups", "row", None, None),
            P("groups", "row", None, None),
            P("groups", None),
            P("groups", None),
            P("groups", None),
            P("groups", "row", None),
            P("groups", "row"),
        ),
        out_specs=(
            P("groups", "row", None, None),
            P("groups", None),
            P("groups", None),
            P("groups", "row", None, None),
            P("groups", None),
        ),
        check_vma=False,
    )
```

```python
import functools

import jax
import jax.numpy as jnp
from jax import lax
from jax.experimental import pallas as pl
from jax.experimental.pallas import tpu as pltpu
from jax.sharding import PartitionSpec as P

VMEM_BYTES = 14 * 1024 * 1024


def call(body, outs, args, spaces, flops, scratch=()):
    kinds = {"s": pltpu.SMEM, "v": pltpu.VMEM, "h": pltpu.HBM}
    moved = sum(a.size * a.dtype.itemsize for a in args) + sum(o.size * o.dtype.itemsize for o in outs)
    return pl.pallas_call(
        body,
        out_shape=outs,
        in_specs=[pl.BlockSpec(memory_space=kinds[c]) for c in spaces],
        out_specs=[pl.BlockSpec(memory_space=pltpu.VMEM)] * len(outs),
        scratch_shapes=list(scratch),
        compiler_params=pltpu.CompilerParams(vmem_limit_bytes=VMEM_BYTES),
        cost_estimate=pl.CostEstimate(flops=flops, bytes_accessed=moved, transcendentals=0),
    )(*args)


def dot(a, b):
    return lax.dot_general(a, b, (((1,), (0,)), ((), ())), preferred_element_type=jnp.float32)


def dot_t(a, b):
    return lax.dot_general(a, b, (((0,), (0,)), ((), ())), preferred_element_type=jnp.float32)


def offsets_of(where_ref):
    member = where_ref[0] % 4
    across = jnp.where(member < 2, 2, -2)
    beside = jnp.where(member % 2 == 0, 1, -1)
    return jnp.int32(0), beside, across, -across, -beside


def near_kernel(where_ref, list_ref, count_ref, sigma_hbm, first_hbm, second_hbm, lower_hbm, first_beside, second_beside,
                first_acc, second_acc, turned_ref, sigma_ref, lower_ref, near_ref, first, second, sems):
    lives = []
    copies = []
    for index, offset in enumerate(offsets_of(where_ref)):
        slot = jnp.int32(0)
        live = jnp.int32(0)
        for s in range(sigma_hbm.shape[0]):
            hit = (list_ref[s] == offset) & (s < count_ref[0])
            slot = jnp.where(hit, s, slot)
            live = jnp.where(hit, 1, live)
        target = near_ref.at[index] if index < 2 else sigma_ref.at[index - 2]
        lives.append((live, target))
        copies.append(pltpu.make_async_copy(sigma_hbm.at[slot], target, sems.at[index]))
    copies.append(pltpu.make_async_copy(first_hbm, first, sems.at[5]))
    copies.append(pltpu.make_async_copy(second_hbm, second, sems.at[6]))
    copies.append(pltpu.make_async_copy(lower_hbm, lower_ref, sems.at[7]))
    for index in (0, 5, 6, 1, 2, 3, 4, 7):
        copies[index].start()

    def arrived(index):
        copies[index].wait()
        live, target = lives[index]

        @pl.when(live == 0)
        def _():
            target[...] = jnp.zeros(target.shape, target.dtype)

    copies[5].wait()
    copies[6].wait()
    arrived(0)
    first_acc[...] = dot(near_ref[0], first[...])
    second_acc[...] = dot(near_ref[0], second[...])
    size = first.shape[0]
    turned_ref[:size] = first[...].T
    turned_ref[size:] = second[...].T
    arrived(1)
    first_acc[...] += dot(near_ref[1], first_beside[...])
    second_acc[...] += dot(near_ref[1], second_beside[...])
    for index in (2, 3, 4):
        arrived(index)
    copies[7].wait()


def add_far(acc_ref, sigma_ref, index, parts):
    start = 0
    for part in parts:
        rows = part.shape[0]
        acc_ref[...] += dot(sigma_ref[index, :, start : start + rows], part[...])
        start += rows


def halves(value, where_ref, scratch_ref, give_ref, keep_ref, index):
    scratch_ref[...] = value
    half = value.shape[0] // 2
    core = where_ref[0] % 2
    keep_ref[index] = scratch_ref[pl.ds(pl.multiple_of(core * half, half), half)]
    give_ref[index] = scratch_ref[pl.ds(pl.multiple_of((1 - core) * half, half), half)].astype(jnp.bfloat16)


def first_kernel(where_ref, acc_in, across_0, across_1, far_0, far_1, rest, sigma_ref, turned_ref,
                 column_ref, again_ref, give_ref, keep_ref, acc_ref):
    acc_ref[...] = acc_in[...]
    add_far(acc_ref, sigma_ref, 0, (across_0, across_1))
    add_far(acc_ref, sigma_ref, 1, (far_0, far_1))
    add_far(acc_ref, sigma_ref, 2, (rest,))
    column = (-acc_ref[...]).astype(jnp.bfloat16)
    column_ref[...] = column
    again_ref[...] = column
    size = column.shape[0]
    halves(-dot(turned_ref[:size], column), where_ref, acc_ref, give_ref, keep_ref, 0)
    halves(dot(turned_ref[size:], column), where_ref, acc_ref, give_ref, keep_ref, 1)


def across_kernel(acc_in, column_ref, lower_ref, across_0, across_1, sigma_ref, acc_ref):
    acc_ref[...] = acc_in[...] + dot(column_ref[...], lower_ref[...])
    add_far(acc_ref, sigma_ref, 0, (across_0, across_1))


def second_kernel(where_ref, acc_in, far_0, far_1, rest, sigma_ref, turned_ref,
                  column_ref, give_ref, keep_ref, acc_ref):
    acc_ref[...] = acc_in[...]
    add_far(acc_ref, sigma_ref, 1, (far_0, far_1))
    add_far(acc_ref, sigma_ref, 2, (rest,))
    column = (-acc_ref[...]).astype(jnp.bfloat16)
    column_ref[...] = column
    size = column.shape[0]
    halves(-dot(turned_ref[size:], column), where_ref, acc_ref, give_ref, keep_ref, 0)


def split(value):
    high = value.astype(jnp.bfloat16)
    low = (value - high.astype(jnp.float32)).astype(jnp.bfloat16)
    return high, low


def place(where_ref, mine_ref, other_ref, index, out_ref):
    half = mine_ref.shape[1]
    core = where_ref[0] % 2
    out_ref[pl.ds(pl.multiple_of(core * half, half), half)] = mine_ref[index].astype(jnp.float32)
    out_ref[pl.ds(pl.multiple_of((1 - core) * half, half), half)] = other_ref[index].astype(jnp.float32)


def link_kernel(where_ref, mine_ref, other_ref, lower_ref, first_diag_ref, second_diag_ref,
                first_ref, link_ref, base_ref, sum_ref):
    lower = lower_ref[...]
    place(where_ref, mine_ref, other_ref, 0, sum_ref)
    block_first = first_diag_ref[...] + sum_ref[...]
    first_ref[...] = block_first
    place(where_ref, mine_ref, other_ref, 1, sum_ref)
    high, low = split(block_first)
    link = dot(high, lower) + dot(low, lower) + sum_ref[...].T
    link_ref[...] = -link
    high, low = split(link)
    base_ref[...] = second_diag_ref[...] + dot_t(lower, high) + dot_t(lower, low)


def last_kernel(where_ref, mine_ref, other_ref, base_ref, second_ref):
    place(where_ref, mine_ref, other_ref, 0, second_ref)
    second_ref[...] += base_ref[...]


def swapped(value, bit, devices):
    return lax.ppermute(value, "row", [(i, i ^ bit) for i in range(devices)])


def far_of(across, devices):
    hops = [(i, i + 4 if i % 4 < 2 else i - 4) for i in range(devices)]
    return lax.ppermute(across, "row", [(a, b) for a, b in hops if 0 <= b < devices])


def rest_of(across, far, member, devices):
    give_across = (member == 0) | (member == 3)
    pieces = [jnp.where(give_across, a, f) for a, f in zip(across, far)]
    return swapped(jnp.concatenate(pieces, axis=0), 1, devices)


def core_summed(give, keep, position, devices):
    return halved(keep + swapped(give, 1, devices).astype(jnp.float32), 2, position)


def halved(total, bit, position):
    k, rows, width = total.shape
    pair = total.reshape((k, 2, rows // 2, width))
    mine = (position // bit) % 2
    give = lax.dynamic_index_in_dim(pair, 1 - mine, 1, keepdims=False).astype(jnp.bfloat16)
    return give, lax.dynamic_index_in_dim(pair, mine, 1, keepdims=False)


def summed(give, keep, position, devices):
    bits = [2 ** b for b in range(1, devices.bit_length() - 1)]
    for bit in bits:
        total = keep + swapped(give, bit, devices).astype(jnp.float32)
        if bit != bits[-1]:
            give, keep = halved(total, 2 * bit, position)
    gathered = total.astype(jnp.bfloat16)
    for bit in bits[::-1]:
        other = swapped(gathered, bit, devices)
        mine = (position // bit) % 2
        low = jnp.where(mine == 0, gathered, other)
        high = jnp.where(mine == 0, other, gathered)
        gathered = jnp.concatenate([low, high], axis=1)
    return gathered, swapped(gathered, 1, devices)


def shards(sigma_blocks, first_panel, second_panel, lower_panel, first_diag, second_diag, task_list, task_count):
    devices = lax.axis_size("row")
    position = lax.axis_index("row").astype(jnp.int32)
    member = position % 4
    slots, size, width = sigma_blocks.shape[-3:]
    sigma = sigma_blocks.reshape((slots, size, width))
    first = first_panel.reshape((size, width))
    second = second_panel.reshape((size, width))
    where = position.reshape((1,))
    listed = task_list.reshape((slots,))
    count = task_count.reshape((1,))
    one = 2 * size * size * width
    half = size // 2
    narrow = jax.ShapeDtypeStruct((size, width), jnp.bfloat16)
    wide = jax.ShapeDtypeStruct((size, width), jnp.float32)
    scratch = [pltpu.VMEM((size, width), jnp.float32)]

    def parts(k):
        return [jax.ShapeDtypeStruct((k, half, width), t) for t in (jnp.bfloat16, jnp.float32)]

    barrier = lax.optimization_barrier

    across = [swapped(first[:half], 2, devices), swapped(first[half:], 2, devices)]
    beside = swapped(first, 1, devices)
    second_beside = swapped(second, 1, devices)
    first_acc, second_acc, turned, sorted_sigma, lower = call(
        near_kernel,
        [wide, wide, jax.ShapeDtypeStruct((2 * size, width), jnp.bfloat16),
         jax.ShapeDtypeStruct((3, size, width), jnp.bfloat16), narrow],
        [where, listed, count, sigma, first, second, lower_panel, beside, second_beside],
        "ssshhhhvv",
        4 * one,
        [pltpu.VMEM((2, size, width), jnp.bfloat16), pltpu.VMEM((size, width), jnp.bfloat16),
         pltpu.VMEM((size, width), jnp.bfloat16), pltpu.SemaphoreType.DMA((8,))],
    )
    across[0], turned, later_0 = barrier((across[0], turned, second[:half]))
    far = [far_of(across[0], devices)]
    second_across = [swapped(later_0, 2, devices)]
    across[1], later_1 = barrier((across[1], second[half:]))
    far.append(far_of(across[1], devices))
    second_across.append(swapped(later_1, 2, devices))
    far, second_across = barrier((far, second_across))
    rest = rest_of(across, far, member, devices)
    second_far = [far_of(piece, devices) for piece in second_across]
    column_first, column_again, give, keep = call(
        first_kernel,
        [narrow, narrow] + parts(2),
        [where, first_acc, *across, *far, rest, sorted_sigma, turned],
        "svvvvvvvv",
        5 * one,
        scratch,
    )
    give, second_across = barrier((give, second_across))
    second_rest = rest_of(second_across, second_far, member, devices)
    give, keep = core_summed(give, keep, position, devices)
    (second_acc,) = call(
        across_kernel, [wide], [second_acc, column_again, lower, *second_across, sorted_sigma], "vvvvvv", 2 * one
    )
    give, second_rest = barrier((give, second_rest))
    column_second, second_give, second_keep = call(
        second_kernel,
        [narrow] + parts(1),
        [where, second_acc, *second_far, second_rest, sorted_sigma, turned],
        "svvvvvv",
        3 * one,
        scratch,
    )
    mine, other = summed(give, keep, position, devices)
    second_give, second_keep = core_summed(second_give, second_keep, position, devices)
    second_mine, second_other = summed(second_give, second_keep, position, devices)
    block_first, block_link, base = call(
        link_kernel, [wide] * 3, [where, mine, other, lower, first_diag, second_diag], "svvvvv", 4 * one, scratch
    )
    (block_second,) = call(last_kernel, [wide], [where, second_mine, second_other, base], "svvv", size * width)
    shape = first_panel.shape
    return column_first.reshape(shape), block_first, block_link, column_second.reshape(shape), block_second


def solution(mesh):
    return jax.shard_map(
        shards,
        mesh=mesh,
        in_specs=(
            P("groups", "row", None, None, None),
            P("groups", "row", None, None),
            P("groups", "row", None, None),
            P("groups", None),
            P("groups", None),
            P("groups", None),
            P("groups", "row", None),
            P("groups", "row"),
        ),
        out_specs=(
            P("groups", "row", None, None),
            P("groups", None),
            P("groups", None),
            P("groups", "row", None, None),
            P("groups", None),
        ),
        check_vma=False,
    )
```

```python
import functools

import jax
import jax.numpy as jnp
from jax import lax
from jax.experimental import pallas as pl
from jax.experimental.pallas import tpu as pltpu
from jax.sharding import PartitionSpec as P

VMEM_BYTES = 14 * 1024 * 1024


def call(body, outs, args, spaces, flops, scratch=()):
    kinds = {"s": pltpu.SMEM, "v": pltpu.VMEM, "h": pltpu.HBM}
    moved = sum(a.size * a.dtype.itemsize for a in args) + sum(o.size * o.dtype.itemsize for o in outs)
    return pl.pallas_call(
        body,
        out_shape=outs,
        in_specs=[pl.BlockSpec(memory_space=kinds[c]) for c in spaces],
        out_specs=[pl.BlockSpec(memory_space=pltpu.VMEM)] * len(outs),
        scratch_shapes=list(scratch),
        compiler_params=pltpu.CompilerParams(vmem_limit_bytes=VMEM_BYTES),
        cost_estimate=pl.CostEstimate(flops=flops, bytes_accessed=moved, transcendentals=0),
    )(*args)


def dot(a, b):
    return lax.dot_general(a, b, (((1,), (0,)), ((), ())), preferred_element_type=jnp.float32)


def dot_t(a, b):
    return lax.dot_general(a, b, (((0,), (0,)), ((), ())), preferred_element_type=jnp.float32)


def offsets_of(where_ref):
    member = where_ref[0] % 4
    across = jnp.where(member < 2, 2, -2)
    beside = jnp.where(member % 2 == 0, 1, -1)
    return jnp.int32(0), beside, across, -across, -beside


def split_kernel(first_hbm, second_hbm, first_0, first_1, second_0, second_1, sems):
    half = first_0.shape[0]
    copies = [
        pltpu.make_async_copy(source.at[pl.ds(start, half)], target, sems.at[index])
        for index, (source, start, target) in enumerate(
            ((first_hbm, 0, first_0), (first_hbm, half, first_1), (second_hbm, 0, second_0), (second_hbm, half, second_1))
        )
    ]
    for copy in copies:
        copy.start()
    for copy in copies:
        copy.wait()


def near_kernel(where_ref, list_ref, count_ref, sigma_hbm, lower_hbm, first_0, first_1, second_0, second_1,
                first_beside, second_beside,
                first_acc, second_acc, turned_ref, sigma_ref, lower_ref, near_ref, sems):
    lives = []
    copies = []
    for index, offset in enumerate(offsets_of(where_ref)):
        slot = jnp.int32(0)
        live = jnp.int32(0)
        for s in range(sigma_hbm.shape[0]):
            hit = (list_ref[s] == offset) & (s < count_ref[0])
            slot = jnp.where(hit, s, slot)
            live = jnp.where(hit, 1, live)
        target = near_ref.at[index] if index < 2 else sigma_ref.at[index - 2]
        lives.append((live, target))
        copies.append(pltpu.make_async_copy(sigma_hbm.at[slot], target, sems.at[index]))
    copies.append(pltpu.make_async_copy(lower_hbm, lower_ref, sems.at[5]))
    for copy in copies:
        copy.start()

    def arrived(index):
        copies[index].wait()
        live, target = lives[index]

        @pl.when(live == 0)
        def _():
            target[...] = jnp.zeros(target.shape, target.dtype)

    half = first_0.shape[0]
    size = 2 * half
    turned_ref[:size, :half] = first_0[...].T
    turned_ref[:size, half:] = first_1[...].T
    turned_ref[size:, :half] = second_0[...].T
    turned_ref[size:, half:] = second_1[...].T
    arrived(0)
    first_acc[...] = jnp.zeros_like(first_acc)
    second_acc[...] = jnp.zeros_like(second_acc)
    add_far(first_acc, near_ref, 0, (first_0, first_1))
    add_far(second_acc, near_ref, 0, (second_0, second_1))
    arrived(1)
    add_far(first_acc, near_ref, 1, (first_beside,))
    add_far(second_acc, near_ref, 1, (second_beside,))
    for index in (2, 3, 4):
        arrived(index)
    copies[5].wait()


def add_far(acc_ref, sigma_ref, index, parts):
    start = 0
    for part in parts:
        rows = part.shape[0]
        acc_ref[...] += dot(sigma_ref[index, :, start : start + rows], part[...])
        start += rows


def halves(value, where_ref, scratch_ref, give_ref, keep_ref, index):
    scratch_ref[...] = value
    half = value.shape[0] // 2
    core = where_ref[0] % 2
    keep_ref[index] = scratch_ref[pl.ds(pl.multiple_of(core * half, half), half)]
    give_ref[index] = scratch_ref[pl.ds(pl.multiple_of((1 - core) * half, half), half)].astype(jnp.bfloat16)


def first_kernel(where_ref, acc_in, across_0, across_1, far_0, far_1, rest, sigma_ref, turned_ref,
                 column_ref, again_ref, give_ref, keep_ref, acc_ref):
    acc_ref[...] = acc_in[...]
    add_far(acc_ref, sigma_ref, 0, (across_0, across_1))
    add_far(acc_ref, sigma_ref, 1, (far_0, far_1))
    add_far(acc_ref, sigma_ref, 2, (rest,))
    column = (-acc_ref[...]).astype(jnp.bfloat16)
    column_ref[...] = column
    again_ref[...] = column
    size = column.shape[0]
    halves(-dot(turned_ref[:size], column), where_ref, acc_ref, give_ref, keep_ref, 0)
    halves(dot(turned_ref[size:], column), where_ref, acc_ref, give_ref, keep_ref, 1)


def across_kernel(acc_in, column_ref, lower_ref, across_0, across_1, sigma_ref, acc_ref):
    acc_ref[...] = acc_in[...] + dot(column_ref[...], lower_ref[...])
    add_far(acc_ref, sigma_ref, 0, (across_0, across_1))


def second_kernel(where_ref, acc_in, far_0, far_1, rest, sigma_ref, turned_ref,
                  column_ref, give_ref, keep_ref, acc_ref):
    acc_ref[...] = acc_in[...]
    add_far(acc_ref, sigma_ref, 1, (far_0, far_1))
    add_far(acc_ref, sigma_ref, 2, (rest,))
    column = (-acc_ref[...]).astype(jnp.bfloat16)
    column_ref[...] = column
    size = column.shape[0]
    halves(-dot(turned_ref[size:], column), where_ref, acc_ref, give_ref, keep_ref, 0)


def split(value):
    high = value.astype(jnp.bfloat16)
    low = (value - high.astype(jnp.float32)).astype(jnp.bfloat16)
    return high, low


def place(where_ref, mine_ref, other_ref, index, out_ref):
    half = mine_ref.shape[1]
    core = where_ref[0] % 2
    out_ref[pl.ds(pl.multiple_of(core * half, half), half)] = mine_ref[index].astype(jnp.float32)
    out_ref[pl.ds(pl.multiple_of((1 - core) * half, half), half)] = other_ref[index].astype(jnp.float32)


def link_kernel(where_ref, mine_ref, other_ref, lower_ref, first_diag_ref, second_diag_ref,
                first_ref, link_ref, base_ref, sum_ref):
    lower = lower_ref[...]
    place(where_ref, mine_ref, other_ref, 0, sum_ref)
    block_first = first_diag_ref[...] + sum_ref[...]
    first_ref[...] = block_first
    place(where_ref, mine_ref, other_ref, 1, sum_ref)
    high, low = split(block_first)
    link = dot(high, lower) + dot(low, lower) + sum_ref[...].T
    link_ref[...] = -link
    high, low = split(link)
    base_ref[...] = second_diag_ref[...] + dot_t(lower, high) + dot_t(lower, low)


def last_kernel(where_ref, mine_ref, other_ref, base_ref, second_ref):
    place(where_ref, mine_ref, other_ref, 0, second_ref)
    second_ref[...] += base_ref[...]


def swapped(value, bit, devices):
    return lax.ppermute(value, "row", [(i, i ^ bit) for i in range(devices)])


def far_of(across, devices):
    hops = [(i, i + 4 if i % 4 < 2 else i - 4) for i in range(devices)]
    return lax.ppermute(across, "row", [(a, b) for a, b in hops if 0 <= b < devices])


def rest_of(across, far, give_across, devices):
    pieces = [jnp.where(give_across, a, f) for a, f in zip(across, far)]
    return swapped(jnp.concatenate(pieces, axis=0), 1, devices)


def core_summed(give, keep, uppers, devices):
    return halved(keep + swapped(give, 1, devices).astype(jnp.float32), uppers[1])


def halved(total, upper):
    half = total.shape[1] // 2
    low, high = total[:, :half], total[:, half:]
    return jnp.where(upper, low, high).astype(jnp.bfloat16), jnp.where(upper, high, low)


def summed(give, keep, uppers, devices):
    count = len(uppers)
    for b in range(1, count):
        total = keep + swapped(give, 2 ** b, devices).astype(jnp.float32)
        if b + 1 < count:
            give, keep = halved(total, uppers[b + 1])
    gathered = total.astype(jnp.bfloat16)
    for b in range(count - 1, 0, -1):
        other = swapped(gathered, 2 ** b, devices)
        low = jnp.where(uppers[b], other, gathered)
        high = jnp.where(uppers[b], gathered, other)
        gathered = jnp.concatenate([low, high], axis=1)
    return gathered, swapped(gathered, 1, devices)


def shards(sigma_blocks, first_panel, second_panel, lower_panel, first_diag, second_diag, task_list, task_count):
    barrier = lax.optimization_barrier
    devices = lax.axis_size("row")
    position = lax.axis_index("row").astype(jnp.int32)
    slots, size, width = sigma_blocks.shape[-3:]
    sigma = sigma_blocks.reshape((slots, size, width))
    first = first_panel.reshape((size, width))
    second = second_panel.reshape((size, width))
    where = position.reshape((1,))
    bits = [(position >> b) & 1 for b in range(devices.bit_length() - 1)]
    uppers = [bit == 1 for bit in bits]
    give_across = bits[0] == bits[1]
    where, uppers, give_across, first, second = barrier((where, uppers, give_across, first, second))
    listed = task_list.reshape((slots,))
    count = task_count.reshape((1,))
    one = 2 * size * size * width
    half = size // 2
    narrow = jax.ShapeDtypeStruct((size, width), jnp.bfloat16)
    wide = jax.ShapeDtypeStruct((size, width), jnp.float32)
    scratch = [pltpu.VMEM((size, width), jnp.float32)]

    def parts(k):
        return [jax.ShapeDtypeStruct((k, half, width), t) for t in (jnp.bfloat16, jnp.float32)]

    piece = jax.ShapeDtypeStruct((half, width), jnp.bfloat16)
    pieces = call(split_kernel, [piece] * 4, [first, second], "hh", 1, [pltpu.SemaphoreType.DMA((4,))])
    across = [swapped(pieces[0], 2, devices), swapped(pieces[1], 2, devices)]
    beside = swapped(first, 1, devices)
    second_beside = swapped(second, 1, devices)
    first_acc, second_acc, turned, sorted_sigma, lower = call(
        near_kernel,
        [wide, wide, jax.ShapeDtypeStruct((2 * size, width), jnp.bfloat16),
         jax.ShapeDtypeStruct((3, size, width), jnp.bfloat16), narrow],
        [where, listed, count, sigma, lower_panel, *pieces, beside, second_beside],
        "ssshhvvvvvv",
        4 * one,
        [pltpu.VMEM((2, size, width), jnp.bfloat16), pltpu.SemaphoreType.DMA((6,))],
    )
    across[0], turned, later_0 = barrier((across[0], turned, pieces[2]))
    far = [far_of(across[0], devices)]
    second_across = [swapped(later_0, 2, devices)]
    across[1], later_1 = barrier((across[1], pieces[3]))
    far.append(far_of(across[1], devices))
    second_across.append(swapped(later_1, 2, devices))
    far, second_across = barrier((far, second_across))
    rest = rest_of(across, far, give_across, devices)
    second_far = [far_of(piece, devices) for piece in second_across]
    column_first, column_again, give, keep = call(
        first_kernel,
        [narrow, narrow] + parts(2),
        [where, first_acc, *across, *far, rest, sorted_sigma, turned],
        "svvvvvvvv",
        5 * one,
        scratch,
    )
    give, second_across = barrier((give, second_across))
    second_rest = rest_of(second_across, second_far, give_across, devices)
    give, keep = core_summed(give, keep, uppers, devices)
    (second_acc,) = call(
        across_kernel, [wide], [second_acc, column_again, lower, *second_across, sorted_sigma], "vvvvvv", 2 * one
    )
    give, second_rest = barrier((give, second_rest))
    column_second, second_give, second_keep = call(
        second_kernel,
        [narrow] + parts(1),
        [where, second_acc, *second_far, second_rest, sorted_sigma, turned],
        "svvvvvv",
        3 * one,
        scratch,
    )
    mine, other = summed(give, keep, uppers, devices)
    second_give, second_keep = core_summed(second_give, second_keep, uppers, devices)
    second_mine, second_other = summed(second_give, second_keep, uppers, devices)
    block_first, block_link, base = call(
        link_kernel, [wide] * 3, [where, mine, other, lower, first_diag, second_diag], "svvvvv", 4 * one, scratch
    )
    (block_second,) = call(last_kernel, [wide], [where, second_mine, second_other, base], "svvv", size * width)
    shape = first_panel.shape
    return column_first.reshape(shape), block_first, block_link, column_second.reshape(shape), block_second


def solution(mesh):
    return jax.shard_map(
        shards,
        mesh=mesh,
        in_specs=(
            P("groups", "row", None, None, None),
            P("groups", "row", None, None),
            P("groups", "row", None, None),
            P("groups", None),
            P("groups", None),
            P("groups", None),
            P("groups", "row", None),
            P("groups", "row"),
        ),
        out_specs=(
            P("groups", "row", None, None),
            P("groups", None),
            P("groups", None),
            P("groups", "row", None, None),
            P("groups", None),
        ),
        check_vma=False,
    )
```

```python
import functools

import jax
import jax.numpy as jnp
from jax import lax
from jax.experimental import pallas as pl
from jax.experimental.pallas import tpu as pltpu
from jax.sharding import PartitionSpec as P

VMEM_BYTES = 14 * 1024 * 1024


def call(body, outs, args, spaces, flops, scratch=()):
    kinds = {"s": pltpu.SMEM, "v": pltpu.VMEM, "h": pltpu.HBM}
    moved = sum(a.size * a.dtype.itemsize for a in args) + sum(o.size * o.dtype.itemsize for o in outs)
    return pl.pallas_call(
        body,
        out_shape=outs,
        in_specs=[pl.BlockSpec(memory_space=kinds[c]) for c in spaces],
        out_specs=[pl.BlockSpec(memory_space=pltpu.VMEM)] * len(outs),
        scratch_shapes=list(scratch),
        compiler_params=pltpu.CompilerParams(vmem_limit_bytes=VMEM_BYTES),
        cost_estimate=pl.CostEstimate(flops=flops, bytes_accessed=moved, transcendentals=0),
    )(*args)


def dot(a, b):
    return lax.dot_general(a, b, (((1,), (0,)), ((), ())), preferred_element_type=jnp.float32)


def dot_t(a, b):
    return lax.dot_general(a, b, (((0,), (0,)), ((), ())), preferred_element_type=jnp.float32)


def offsets_of(where_ref):
    member = where_ref[0] % 4
    across = jnp.where(member < 2, 2, -2)
    beside = jnp.where(member % 2 == 0, 1, -1)
    return jnp.int32(0), beside, across, -across, -beside


def near_kernel(where_ref, list_ref, count_ref, sigma_hbm, lower_hbm, first, second,
                first_beside, second_beside,
                first_acc, second_acc, turned_ref, sigma_ref, lower_ref, near_ref, sems):
    lives = []
    copies = []
    for index, offset in enumerate(offsets_of(where_ref)):
        slot = jnp.int32(0)
        live = jnp.int32(0)
        for s in range(sigma_hbm.shape[0]):
            hit = (list_ref[s] == offset) & (s < count_ref[0])
            slot = jnp.where(hit, s, slot)
            live = jnp.where(hit, 1, live)
        target = near_ref.at[index] if index < 2 else sigma_ref.at[index - 2]
        lives.append((live, target))
        copies.append(pltpu.make_async_copy(sigma_hbm.at[slot], target, sems.at[index]))
    copies.append(pltpu.make_async_copy(lower_hbm, lower_ref, sems.at[5]))
    for copy in copies:
        copy.start()

    def arrived(index):
        copies[index].wait()
        live, target = lives[index]

        @pl.when(live == 0)
        def _():
            target[...] = jnp.zeros(target.shape, target.dtype)

    size = first.shape[0]
    turned_ref[:size] = first[...].T
    turned_ref[size:] = second[...].T
    arrived(0)
    first_acc[...] = dot(near_ref[0], first[...])
    second_acc[...] = dot(near_ref[0], second[...])
    arrived(1)
    first_acc[...] += dot(near_ref[1], first_beside[...])
    second_acc[...] += dot(near_ref[1], second_beside[...])
    for index in (2, 3, 4):
        arrived(index)
    copies[5].wait()


def halves(value, where_ref, scratch_ref, give_ref, keep_ref, index):
    scratch_ref[...] = value
    half = value.shape[0] // 2
    core = where_ref[0] % 2
    keep_ref[index] = scratch_ref[pl.ds(pl.multiple_of(core * half, half), half)]
    give_ref[index] = scratch_ref[pl.ds(pl.multiple_of((1 - core) * half, half), half)].astype(jnp.bfloat16)


def first_kernel(where_ref, acc_in, across, far, rest, sigma_ref, turned_ref,
                 column_ref, again_ref, give_ref, keep_ref, acc_ref):
    acc_ref[...] = acc_in[...]
    acc_ref[...] += dot(sigma_ref[0], across[...])
    acc_ref[...] += dot(sigma_ref[1], far[...])
    acc_ref[...] += dot(sigma_ref[2], rest[...])
    column = (-acc_ref[...]).astype(jnp.bfloat16)
    column_ref[...] = column
    again_ref[...] = column
    size = column.shape[0]
    halves(-dot(turned_ref[:size], column), where_ref, acc_ref, give_ref, keep_ref, 0)
    halves(dot(turned_ref[size:], column), where_ref, acc_ref, give_ref, keep_ref, 1)


def across_kernel(acc_in, column_ref, lower_ref, across, sigma_ref, acc_ref):
    acc_ref[...] = acc_in[...] + dot(column_ref[...], lower_ref[...])
    acc_ref[...] += dot(sigma_ref[0], across[...])


def second_kernel(where_ref, acc_in, far, rest, sigma_ref, turned_ref,
                  column_ref, give_ref, keep_ref, acc_ref):
    acc_ref[...] = acc_in[...]
    acc_ref[...] += dot(sigma_ref[1], far[...])
    acc_ref[...] += dot(sigma_ref[2], rest[...])
    column = (-acc_ref[...]).astype(jnp.bfloat16)
    column_ref[...] = column
    size = column.shape[0]
    halves(-dot(turned_ref[size:], column), where_ref, acc_ref, give_ref, keep_ref, 0)


def split(value):
    high = value.astype(jnp.bfloat16)
    low = (value - high.astype(jnp.float32)).astype(jnp.bfloat16)
    return high, low


def place(where_ref, mine_ref, other_ref, index, out_ref):
    half = mine_ref.shape[1]
    core = where_ref[0] % 2
    out_ref[pl.ds(pl.multiple_of(core * half, half), half)] = mine_ref[index].astype(jnp.float32)
    out_ref[pl.ds(pl.multiple_of((1 - core) * half, half), half)] = other_ref[index].astype(jnp.float32)


def link_kernel(where_ref, mine_ref, other_ref, lower_ref, first_diag_ref, second_diag_ref,
                first_ref, link_ref, base_ref, sum_ref):
    lower = lower_ref[...]
    place(where_ref, mine_ref, other_ref, 0, sum_ref)
    block_first = first_diag_ref[...] + sum_ref[...]
    first_ref[...] = block_first
    place(where_ref, mine_ref, other_ref, 1, sum_ref)
    high, low = split(block_first)
    link = dot(high, lower) + dot(low, lower) + sum_ref[...].T
    link_ref[...] = -link
    high, low = split(link)
    base_ref[...] = second_diag_ref[...] + dot_t(lower, high) + dot_t(lower, low)


def last_kernel(where_ref, mine_ref, other_ref, base_ref, second_ref):
    place(where_ref, mine_ref, other_ref, 0, second_ref)
    second_ref[...] += base_ref[...]


def swapped(value, bit, devices):
    return lax.ppermute(value, "row", [(i, i ^ bit) for i in range(devices)])


def far_of(across, devices):
    hops = [(i, (i + (4 if i % 4 < 2 else -4)) % devices) for i in range(devices)]
    return lax.ppermute(across, "row", hops)


def rest_of(across, far, give_across, devices):
    return swapped(jnp.where(give_across, across, far), 1, devices)


def core_summed(give, keep, uppers, devices):
    return halved(keep + swapped(give, 1, devices).astype(jnp.float32), uppers[1])


def chip_summed(give, keep, devices):
    return keep + swapped(give, 2, devices).astype(jnp.float32)


def halved(total, upper):
    half = total.shape[1] // 2
    low, high = total[:, :half], total[:, half:]
    return jnp.where(upper, low, high).astype(jnp.bfloat16), jnp.where(upper, high, low)


def summed(total, uppers, devices):
    count = len(uppers)
    for b in range(2, count):
        give, keep = halved(total, uppers[b])
        total = keep + swapped(give, 2 ** b, devices).astype(jnp.float32)
    gathered = total.astype(jnp.bfloat16)
    for b in range(count - 1, 0, -1):
        other = swapped(gathered, 2 ** b, devices)
        low = jnp.where(uppers[b], other, gathered)
        high = jnp.where(uppers[b], gathered, other)
        gathered = jnp.concatenate([low, high], axis=1)
    return gathered, swapped(gathered, 1, devices)


def shards(sigma_blocks, first_panel, second_panel, lower_panel, first_diag, second_diag, task_list, task_count):
    barrier = lax.optimization_barrier
    devices = lax.axis_size("row")
    position = lax.axis_index("row").astype(jnp.int32)
    slots, size, width = sigma_blocks.shape[-3:]
    sigma = sigma_blocks.reshape((slots, size, width))
    first = first_panel.reshape((size, width))
    second = second_panel.reshape((size, width))
    where = position.reshape((1,))
    bits = [(position >> b) & 1 for b in range(devices.bit_length() - 1)]
    uppers = [bit == 1 for bit in bits]
    give_across = bits[0] == bits[1]
    where, uppers, give_across, first, second = barrier((where, uppers, give_across, first, second))
    listed = task_list.reshape((slots,))
    count = task_count.reshape((1,))
    one = 2 * size * size * width
    half = size // 2
    narrow = jax.ShapeDtypeStruct((size, width), jnp.bfloat16)
    wide = jax.ShapeDtypeStruct((size, width), jnp.float32)
    scratch = [pltpu.VMEM((size, width), jnp.float32)]

    def parts(k):
        return [jax.ShapeDtypeStruct((k, half, width), t) for t in (jnp.bfloat16, jnp.float32)]

    across = swapped(first, 2, devices)
    second_across = swapped(second, 2, devices)
    beside = swapped(first, 1, devices)
    second_beside = swapped(second, 1, devices)
    first_acc, second_acc, turned, sorted_sigma, lower = call(
        near_kernel,
        [wide, wide, jax.ShapeDtypeStruct((2 * size, width), jnp.bfloat16),
         jax.ShapeDtypeStruct((3, size, width), jnp.bfloat16), narrow],
        [where, listed, count, sigma, lower_panel, first, second, beside, second_beside],
        "ssshhvvvv",
        4 * one,
        [pltpu.VMEM((2, size, width), jnp.bfloat16), pltpu.SemaphoreType.DMA((6,))],
    )
    across, turned = barrier((across, turned))
    far = far_of(across, devices)
    far, second_across = barrier((far, second_across))
    second_far = far_of(second_across, devices)
    rest = rest_of(across, far, give_across, devices)
    column_first, column_again, give, keep = call(
        first_kernel,
        [narrow, narrow] + parts(2),
        [where, first_acc, across, far, rest, sorted_sigma, turned],
        "svvvvvv",
        5 * one,
        scratch,
    )
    give, keep = core_summed(give, keep, uppers, devices)
    give, second_across = barrier((give, second_across))
    second_rest = rest_of(second_across, second_far, give_across, devices)
    total = chip_summed(give, keep, devices)
    (second_acc,) = call(
        across_kernel, [wide], [second_acc, column_again, lower, second_across, sorted_sigma], "vvvvv", 2 * one
    )
    total, second_rest = barrier((total, second_rest))
    column_second, second_give, second_keep = call(
        second_kernel,
        [narrow] + parts(1),
        [where, second_acc, second_far, second_rest, sorted_sigma, turned],
        "svvvvv",
        3 * one,
        scratch,
    )
    mine, other = summed(total, uppers, devices)
    second_give, second_keep = core_summed(second_give, second_keep, uppers, devices)
    second_total = chip_summed(second_give, second_keep, devices)
    second_mine, second_other = summed(second_total, uppers, devices)
    block_first, block_link, base = call(
        link_kernel, [wide] * 3, [where, mine, other, lower, first_diag, second_diag], "svvvvv", 4 * one, scratch
    )
    (block_second,) = call(last_kernel, [wide], [where, second_mine, second_other, base], "svvv", size * width)
    shape = first_panel.shape
    return column_first.reshape(shape), block_first, block_link, column_second.reshape(shape), block_second


def solution(mesh):
    return jax.shard_map(
        shards,
        mesh=mesh,
        in_specs=(
            P("groups", "row", None, None, None),
            P("groups", "row", None, None),
            P("groups", "row", None, None),
            P("groups", None),
            P("groups", None),
            P("groups", None),
            P("groups", "row", None),
            P("groups", "row"),
        ),
        out_specs=(
            P("groups", "row", None, None),
            P("groups", None),
            P("groups", None),
            P("groups", "row", None, None),
            P("groups", None),
        ),
        check_vma=False,
    )
```

```python
import functools

import jax
import jax.numpy as jnp
from jax import lax
from jax.experimental import pallas as pl
from jax.experimental.pallas import tpu as pltpu
from jax.sharding import PartitionSpec as P

VMEM_BYTES = 14 * 1024 * 1024


def call(body, outs, args, spaces, flops, scratch=()):
    kinds = {"s": pltpu.SMEM, "v": pltpu.VMEM, "h": pltpu.HBM}
    moved = sum(a.size * a.dtype.itemsize for a in args) + sum(o.size * o.dtype.itemsize for o in outs)
    return pl.pallas_call(
        body,
        out_shape=outs,
        in_specs=[pl.BlockSpec(memory_space=kinds[c]) for c in spaces],
        out_specs=[pl.BlockSpec(memory_space=pltpu.VMEM)] * len(outs),
        scratch_shapes=list(scratch),
        compiler_params=pltpu.CompilerParams(vmem_limit_bytes=VMEM_BYTES),
        cost_estimate=pl.CostEstimate(flops=flops, bytes_accessed=moved, transcendentals=0),
    )(*args)


def dot(a, b):
    return lax.dot_general(a, b, (((1,), (0,)), ((), ())), preferred_element_type=jnp.float32)


def dot_t(a, b):
    return lax.dot_general(a, b, (((0,), (0,)), ((), ())), preferred_element_type=jnp.float32)


def offsets_of(where_ref):
    member = where_ref[0] % 4
    across = jnp.where(member < 2, 2, -2)
    beside = jnp.where(member % 2 == 0, 1, -1)
    return jnp.int32(0), beside, across, -across, -beside


def near_kernel(where_ref, list_ref, count_ref, sigma_hbm, lower_hbm, first, second,
                first_beside, second_beside,
                first_acc, second_acc, turned_ref, sigma_ref, lower_ref, near_ref, sems):
    lives = []
    copies = []
    for index, offset in enumerate(offsets_of(where_ref)):
        slot = jnp.int32(0)
        live = jnp.int32(0)
        for s in range(sigma_hbm.shape[0]):
            hit = (list_ref[s] == offset) & (s < count_ref[0])
            slot = jnp.where(hit, s, slot)
            live = jnp.where(hit, 1, live)
        target = near_ref.at[index] if index < 2 else sigma_ref.at[index - 2]
        lives.append((live, target))
        copies.append(pltpu.make_async_copy(sigma_hbm.at[slot], target, sems.at[index]))
    copies.append(pltpu.make_async_copy(lower_hbm, lower_ref, sems.at[5]))
    for copy in copies:
        copy.start()

    def arrived(index):
        copies[index].wait()
        live, target = lives[index]

        @pl.when(live == 0)
        def _():
            target[...] = jnp.zeros(target.shape, target.dtype)

    size = first.shape[0]
    turned_ref[:size] = first[...].T
    turned_ref[size:] = second[...].T
    arrived(0)
    first_acc[...] = dot(near_ref[0], first[...])
    second_acc[...] = dot(near_ref[0], second[...])
    arrived(1)
    first_acc[...] += dot(near_ref[1], first_beside[...])
    second_acc[...] += dot(near_ref[1], second_beside[...])
    for index in (2, 3, 4):
        arrived(index)
    copies[5].wait()


def halves(value, where_ref, scratch_ref, give_ref, keep_ref, index):
    scratch_ref[...] = value
    half = value.shape[0] // 2
    core = where_ref[0] % 2
    keep_ref[index] = scratch_ref[pl.ds(pl.multiple_of(core * half, half), half)]
    give_ref[index] = scratch_ref[pl.ds(pl.multiple_of((1 - core) * half, half), half)].astype(jnp.bfloat16)


def first_kernel(where_ref, acc_in, across, far, rest, sigma_ref, turned_ref,
                 column_ref, again_ref, give_ref, keep_ref, acc_ref):
    acc_ref[...] = acc_in[...]
    acc_ref[...] += dot(sigma_ref[0], across[...])
    acc_ref[...] += dot(sigma_ref[1], far[...])
    acc_ref[...] += dot(sigma_ref[2], rest[...])
    column = (-acc_ref[...]).astype(jnp.bfloat16)
    column_ref[...] = column
    again_ref[...] = column
    size = column.shape[0]
    halves(-dot(turned_ref[:size], column), where_ref, acc_ref, give_ref, keep_ref, 0)
    halves(dot(turned_ref[size:], column), where_ref, acc_ref, give_ref, keep_ref, 1)


def across_kernel(acc_in, column_ref, lower_ref, across, sigma_ref, acc_ref):
    acc_ref[...] = acc_in[...] + dot(column_ref[...], lower_ref[...])
    acc_ref[...] += dot(sigma_ref[0], across[...])


def second_kernel(where_ref, acc_in, far, rest, sigma_ref, turned_ref,
                  column_ref, give_ref, keep_ref, acc_ref):
    acc_ref[...] = acc_in[...]
    acc_ref[...] += dot(sigma_ref[1], far[...])
    acc_ref[...] += dot(sigma_ref[2], rest[...])
    column = (-acc_ref[...]).astype(jnp.bfloat16)
    column_ref[...] = column
    size = column.shape[0]
    halves(-dot(turned_ref[size:], column), where_ref, acc_ref, give_ref, keep_ref, 0)


def split(value):
    high = value.astype(jnp.bfloat16)
    low = (value - high.astype(jnp.float32)).astype(jnp.bfloat16)
    return high, low


def place(where_ref, mine_ref, other_ref, index, out_ref):
    half = mine_ref.shape[1]
    core = where_ref[0] % 2
    out_ref[pl.ds(pl.multiple_of(core * half, half), half)] = mine_ref[index].astype(jnp.float32)
    out_ref[pl.ds(pl.multiple_of((1 - core) * half, half), half)] = other_ref[index].astype(jnp.float32)


def link_kernel(where_ref, mine_ref, other_ref, lower_ref, first_diag_ref, second_diag_ref,
                first_ref, link_ref, base_ref, sum_ref):
    lower = lower_ref[...]
    place(where_ref, mine_ref, other_ref, 0, sum_ref)
    block_first = first_diag_ref[...] + sum_ref[...]
    first_ref[...] = block_first
    place(where_ref, mine_ref, other_ref, 1, sum_ref)
    high, low = split(block_first)
    link = dot(high, lower) + dot(low, lower) + sum_ref[...].T
    link_ref[...] = -link
    high, low = split(link)
    base_ref[...] = second_diag_ref[...] + dot_t(lower, high) + dot_t(lower, low)


def last_kernel(where_ref, mine_ref, other_ref, base_ref, second_ref):
    place(where_ref, mine_ref, other_ref, 0, second_ref)
    second_ref[...] += base_ref[...]


def swapped(value, bit, devices):
    return lax.ppermute(value, "row", [(i, i ^ bit) for i in range(devices)])


def far_of(across, devices):
    hops = [(i, (i + (4 if i % 4 < 2 else -4)) % devices) for i in range(devices)]
    return lax.ppermute(across, "row", hops)


def rest_of(across, far, give_across, devices):
    return swapped(jnp.where(give_across, across, far), 1, devices)


def core_summed(give, keep, uppers, devices):
    return halved(keep + swapped(give, 1, devices).astype(jnp.float32), uppers[1])


def chip_summed(give, keep, devices):
    return keep + swapped(give, 2, devices).astype(jnp.float32)


def halved(total, upper):
    half = total.shape[1] // 2
    low, high = total[:, :half], total[:, half:]
    return jnp.where(upper, low, high).astype(jnp.bfloat16), jnp.where(upper, high, low)


def summed(total, uppers, devices):
    count = len(uppers)
    for b in range(2, count):
        give, keep = halved(total, uppers[b])
        total = keep + swapped(give, 2 ** b, devices).astype(jnp.float32)
    gathered = total.astype(jnp.bfloat16)
    for b in range(count - 1, 0, -1):
        other = swapped(gathered, 2 ** b, devices)
        low = jnp.where(uppers[b], other, gathered)
        high = jnp.where(uppers[b], gathered, other)
        gathered = jnp.concatenate([low, high], axis=1)
    return gathered, swapped(gathered, 1, devices)


def shards(sigma_blocks, first_panel, second_panel, lower_panel, first_diag, second_diag, task_list, task_count):
    barrier = lax.optimization_barrier
    devices = lax.axis_size("row")
    position = lax.axis_index("row").astype(jnp.int32)
    slots, size, width = sigma_blocks.shape[-3:]
    sigma = sigma_blocks.reshape((slots, size, width))
    first = first_panel.reshape((size, width))
    second = second_panel.reshape((size, width))
    where = position.reshape((1,))
    bits = [(position >> b) & 1 for b in range(devices.bit_length() - 1)]
    uppers = [bit == 1 for bit in bits]
    give_across = bits[0] == bits[1]
    where, uppers, give_across, first, second = barrier((where, uppers, give_across, first, second))
    listed = task_list.reshape((slots,))
    count = task_count.reshape((1,))
    one = 2 * size * size * width
    half = size // 2
    narrow = jax.ShapeDtypeStruct((size, width), jnp.bfloat16)
    wide = jax.ShapeDtypeStruct((size, width), jnp.float32)
    scratch = [pltpu.VMEM((size, width), jnp.float32)]

    def parts(k):
        return [jax.ShapeDtypeStruct((k, half, width), t) for t in (jnp.bfloat16, jnp.float32)]

    across = swapped(first, 2, devices)
    second_across = swapped(second, 2, devices)
    beside = swapped(first, 1, devices)
    second_beside = swapped(second, 1, devices)
    first_acc, second_acc, turned, sorted_sigma, lower = call(
        near_kernel,
        [wide, wide, jax.ShapeDtypeStruct((2 * size, width), jnp.bfloat16),
         jax.ShapeDtypeStruct((3, size, width), jnp.bfloat16), narrow],
        [where, listed, count, sigma, lower_panel, first, second, beside, second_beside],
        "ssshhvvvv",
        4 * one,
        [pltpu.VMEM((2, size, width), jnp.bfloat16), pltpu.SemaphoreType.DMA((6,))],
    )
    across, turned = barrier((across, turned))
    far = far_of(across, devices)
    far, second_across = barrier((far, second_across))
    second_far = far_of(second_across, devices)
    rest = rest_of(across, far, give_across, devices)
    column_first, column_again, give, keep = call(
        first_kernel,
        [narrow, narrow] + parts(2),
        [where, first_acc, across, far, rest, sorted_sigma, turned],
        "svvvvvv",
        5 * one,
        scratch,
    )
    give, second_across = barrier((give, second_across))
    give, keep = core_summed(give, keep, uppers, devices)
    second_rest = rest_of(second_across, second_far, give_across, devices)
    total = chip_summed(give, keep, devices)
    (second_acc,) = call(
        across_kernel, [wide], [second_acc, column_again, lower, second_across, sorted_sigma], "vvvvv", 2 * one
    )
    column_second, second_give, second_keep = call(
        second_kernel,
        [narrow] + parts(1),
        [where, second_acc, second_far, second_rest, sorted_sigma, turned],
        "svvvvv",
        3 * one,
        scratch,
    )
    second_give, total = barrier((second_give, total))
    second_give, second_keep = core_summed(second_give, second_keep, uppers, devices)
    mine, other = summed(total, uppers, devices)
    second_total = chip_summed(second_give, second_keep, devices)
    second_mine, second_other = summed(second_total, uppers, devices)
    block_first, block_link, base = call(
        link_kernel, [wide] * 3, [where, mine, other, lower, first_diag, second_diag], "svvvvv", 4 * one, scratch
    )
    (block_second,) = call(last_kernel, [wide], [where, second_mine, second_other, base], "svvv", size * width)
    shape = first_panel.shape
    return column_first.reshape(shape), block_first, block_link, column_second.reshape(shape), block_second


def solution(mesh):
    return jax.shard_map(
        shards,
        mesh=mesh,
        in_specs=(
            P("groups", "row", None, None, None),
            P("groups", "row", None, None),
            P("groups", "row", None, None),
            P("groups", None),
            P("groups", None),
            P("groups", None),
            P("groups", "row", None),
            P("groups", "row"),
        ),
        out_specs=(
            P("groups", "row", None, None),
            P("groups", None),
            P("groups", None),
            P("groups", "row", None, None),
            P("groups", None),
        ),
        check_vma=False,
    )
```

```python
import functools

import jax
import jax.numpy as jnp
from jax import lax
from jax.experimental import pallas as pl
from jax.experimental.pallas import tpu as pltpu
from jax.sharding import PartitionSpec as P

VMEM_BYTES = 14 * 1024 * 1024


def call(body, outs, args, spaces, flops, scratch=()):
    kinds = {"s": pltpu.SMEM, "v": pltpu.VMEM, "h": pltpu.HBM}
    moved = sum(a.size * a.dtype.itemsize for a in args) + sum(o.size * o.dtype.itemsize for o in outs)
    return pl.pallas_call(
        body,
        out_shape=outs,
        in_specs=[pl.BlockSpec(memory_space=kinds[c]) for c in spaces],
        out_specs=[pl.BlockSpec(memory_space=pltpu.VMEM)] * len(outs),
        scratch_shapes=list(scratch),
        compiler_params=pltpu.CompilerParams(vmem_limit_bytes=VMEM_BYTES),
        cost_estimate=pl.CostEstimate(flops=flops, bytes_accessed=moved, transcendentals=0),
    )(*args)


def dot(a, b):
    return lax.dot_general(a, b, (((1,), (0,)), ((), ())), preferred_element_type=jnp.float32)


def dot_t(a, b):
    return lax.dot_general(a, b, (((0,), (0,)), ((), ())), preferred_element_type=jnp.float32)


def offsets_of(where_ref):
    member = where_ref[0] % 4
    across = jnp.where(member < 2, 2, -2)
    beside = jnp.where(member % 2 == 0, 1, -1)
    return jnp.int32(0), beside, across, -across, -beside


def near_kernel(where_ref, list_ref, count_ref, sigma_hbm, lower_hbm, first, second,
                first_beside, second_beside,
                first_acc, second_acc, turned_ref, sigma_ref, lower_ref, near_ref, sems):
    lives = []
    copies = []
    for index, offset in enumerate(offsets_of(where_ref)):
        slot = jnp.int32(0)
        live = jnp.int32(0)
        for s in range(sigma_hbm.shape[0]):
            hit = (list_ref[s] == offset) & (s < count_ref[0])
            slot = jnp.where(hit, s, slot)
            live = jnp.where(hit, 1, live)
        target = near_ref.at[index] if index < 2 else sigma_ref.at[index - 2]
        lives.append((live, target))
        copies.append(pltpu.make_async_copy(sigma_hbm.at[slot], target, sems.at[index]))
    copies.append(pltpu.make_async_copy(lower_hbm, lower_ref, sems.at[5]))
    for copy in copies:
        copy.start()

    def arrived(index):
        copies[index].wait()
        live, target = lives[index]

        @pl.when(live == 0)
        def _():
            target[...] = jnp.zeros(target.shape, target.dtype)

    size = first.shape[0]
    turned_ref[:size] = first[...].T
    turned_ref[size:] = second[...].T
    arrived(0)
    first_acc[...] = dot(near_ref[0], first[...])
    second_acc[...] = dot(near_ref[0], second[...])
    arrived(1)
    first_acc[...] += dot(near_ref[1], first_beside[...])
    second_acc[...] += dot(near_ref[1], second_beside[...])
    for index in (2, 3, 4):
        arrived(index)
    copies[5].wait()


def halves(value, where_ref, scratch_ref, give_ref, keep_ref, index):
    scratch_ref[...] = value
    half = value.shape[0] // 2
    core = where_ref[0] % 2
    keep_ref[index] = scratch_ref[pl.ds(pl.multiple_of(core * half, half), half)]
    give_ref[index] = scratch_ref[pl.ds(pl.multiple_of((1 - core) * half, half), half)].astype(jnp.bfloat16)


def first_kernel(where_ref, acc_in, across, far, rest, sigma_ref, turned_ref,
                 column_ref, again_ref, give_ref, keep_ref, acc_ref):
    acc_ref[...] = acc_in[...]
    acc_ref[...] += dot(sigma_ref[0], across[...])
    acc_ref[...] += dot(sigma_ref[1], far[...])
    acc_ref[...] += dot(sigma_ref[2], rest[...])
    column = (-acc_ref[...]).astype(jnp.bfloat16)
    column_ref[...] = column
    again_ref[...] = column
    size = column.shape[0]
    halves(-dot(turned_ref[:size], column), where_ref, acc_ref, give_ref, keep_ref, 0)
    halves(dot(turned_ref[size:], column), where_ref, acc_ref, give_ref, keep_ref, 1)


def across_kernel(acc_in, column_ref, lower_ref, across, sigma_ref, acc_ref):
    acc_ref[...] = acc_in[...] + dot(column_ref[...], lower_ref[...])
    acc_ref[...] += dot(sigma_ref[0], across[...])


def second_kernel(where_ref, acc_in, far_0, far_1, rest, sigma_ref, turned_ref,
                  column_ref, give_ref, keep_ref, acc_ref):
    half = far_0.shape[0]
    acc_ref[...] = acc_in[...]
    acc_ref[...] += dot(sigma_ref[1, :, :half], far_0[...])
    acc_ref[...] += dot(sigma_ref[1, :, half:], far_1[...])
    acc_ref[...] += dot(sigma_ref[2], rest[...])
    column = (-acc_ref[...]).astype(jnp.bfloat16)
    column_ref[...] = column
    size = column.shape[0]
    halves(-dot(turned_ref[size:], column), where_ref, acc_ref, give_ref, keep_ref, 0)


def split(value):
    high = value.astype(jnp.bfloat16)
    low = (value - high.astype(jnp.float32)).astype(jnp.bfloat16)
    return high, low


def place(where_ref, mine_ref, other_ref, index, out_ref):
    half = mine_ref.shape[1]
    core = where_ref[0] % 2
    out_ref[pl.ds(pl.multiple_of(core * half, half), half)] = mine_ref[index].astype(jnp.float32)
    out_ref[pl.ds(pl.multiple_of((1 - core) * half, half), half)] = other_ref[index].astype(jnp.float32)


def link_kernel(where_ref, mine_ref, other_ref, lower_ref, first_diag_ref, second_diag_ref,
                first_ref, link_ref, base_ref, sum_ref):
    lower = lower_ref[...]
    place(where_ref, mine_ref, other_ref, 0, sum_ref)
    block_first = first_diag_ref[...] + sum_ref[...]
    first_ref[...] = block_first
    place(where_ref, mine_ref, other_ref, 1, sum_ref)
    high, low = split(block_first)
    link = dot(high, lower) + dot(low, lower) + sum_ref[...].T
    link_ref[...] = -link
    high, low = split(link)
    base_ref[...] = second_diag_ref[...] + dot_t(lower, high) + dot_t(lower, low)


def last_kernel(where_ref, mine_ref, other_ref, base_ref, second_ref):
    place(where_ref, mine_ref, other_ref, 0, second_ref)
    second_ref[...] += base_ref[...]


def swapped(value, bit, devices):
    return lax.ppermute(value, "row", [(i, i ^ bit) for i in range(devices)])


def far_of(across, devices):
    hops = [(i, (i + (4 if i % 4 < 2 else -4)) % devices) for i in range(devices)]
    return lax.ppermute(across, "row", hops)


def rest_of(across, far, give_across, devices):
    rows = across.shape[0] // len(far)
    pieces = [jnp.where(give_across, across[i * rows : (i + 1) * rows], piece) for i, piece in enumerate(far)]
    return swapped(jnp.concatenate(pieces, axis=0), 1, devices)


def core_summed(give, keep, uppers, devices):
    return halved(keep + swapped(give, 1, devices).astype(jnp.float32), uppers[1])


def chip_summed(give, keep, devices):
    return keep + swapped(give, 2, devices).astype(jnp.float32)


def halved(total, upper):
    half = total.shape[1] // 2
    low, high = total[:, :half], total[:, half:]
    return jnp.where(upper, low, high).astype(jnp.bfloat16), jnp.where(upper, high, low)


def summed(total, uppers, devices):
    last = len(uppers) - 1
    for b in range(2, last):
        give, keep = halved(total, uppers[b])
        total = keep + swapped(give, 2 ** b, devices).astype(jnp.float32)
    own = total.astype(jnp.bfloat16)
    gathered = (own.astype(jnp.float32) + swapped(own, 2 ** last, devices).astype(jnp.float32)).astype(jnp.bfloat16)
    for b in range(last - 1, 0, -1):
        other = swapped(gathered, 2 ** b, devices)
        low = jnp.where(uppers[b], other, gathered)
        high = jnp.where(uppers[b], gathered, other)
        gathered = jnp.concatenate([low, high], axis=1)
    return gathered, swapped(gathered, 1, devices)


def shards(sigma_blocks, first_panel, second_panel, lower_panel, first_diag, second_diag, task_list, task_count):
    barrier = lax.optimization_barrier
    devices = lax.axis_size("row")
    position = lax.axis_index("row").astype(jnp.int32)
    slots, size, width = sigma_blocks.shape[-3:]
    sigma = sigma_blocks.reshape((slots, size, width))
    first = first_panel.reshape((size, width))
    second = second_panel.reshape((size, width))
    where = position.reshape((1,))
    bits = [(position >> b) & 1 for b in range(devices.bit_length() - 1)]
    uppers = [bit == 1 for bit in bits]
    give_across = bits[0] == bits[1]
    where, uppers, give_across, first, second = barrier((where, uppers, give_across, first, second))
    listed = task_list.reshape((slots,))
    count = task_count.reshape((1,))
    one = 2 * size * size * width
    half = size // 2
    narrow = jax.ShapeDtypeStruct((size, width), jnp.bfloat16)
    wide = jax.ShapeDtypeStruct((size, width), jnp.float32)
    scratch = [pltpu.VMEM((size, width), jnp.float32)]

    def parts(k):
        return [jax.ShapeDtypeStruct((k, half, width), t) for t in (jnp.bfloat16, jnp.float32)]

    across = swapped(first, 2, devices)
    second_across = swapped(second, 2, devices)
    beside = swapped(first, 1, devices)
    second_beside = swapped(second, 1, devices)
    first_acc, second_acc, turned, sorted_sigma, lower = call(
        near_kernel,
        [wide, wide, jax.ShapeDtypeStruct((2 * size, width), jnp.bfloat16),
         jax.ShapeDtypeStruct((3, size, width), jnp.bfloat16), narrow],
        [where, listed, count, sigma, lower_panel, first, second, beside, second_beside],
        "ssshhvvvv",
        4 * one,
        [pltpu.VMEM((2, size, width), jnp.bfloat16), pltpu.SemaphoreType.DMA((6,))],
    )
    across, turned = barrier((across, turned))
    far = far_of(across, devices)
    far, second_across = barrier((far, second_across))
    second_far = [far_of(second_across[:half], devices), far_of(second_across[half:], devices)]
    rest = rest_of(across, [far], give_across, devices)
    column_first, column_again, give, keep = call(
        first_kernel,
        [narrow, narrow] + parts(2),
        [where, first_acc, across, far, rest, sorted_sigma, turned],
        "svvvvvv",
        5 * one,
        scratch,
    )
    give, second_far[0] = barrier((give, second_far[0]))
    give, keep = core_summed(give, keep, uppers, devices)
    total = chip_summed(give, keep, devices)
    total, second_across = barrier((total, second_across))
    second_rest = rest_of(second_across, second_far, give_across, devices)
    (second_acc,) = call(
        across_kernel, [wide], [second_acc, column_again, lower, second_across, sorted_sigma], "vvvvv", 2 * one
    )
    column_second, second_give, second_keep = call(
        second_kernel,
        [narrow] + parts(1),
        [where, second_acc, *second_far, second_rest, sorted_sigma, turned],
        "svvvvvv",
        3 * one,
        scratch,
    )
    second_give, second_keep = core_summed(second_give, second_keep, uppers, devices)
    mine, other = summed(total, uppers, devices)
    second_total = chip_summed(second_give, second_keep, devices)
    second_mine, second_other = summed(second_total, uppers, devices)
    block_first, block_link, base = call(
        link_kernel, [wide] * 3, [where, mine, other, lower, first_diag, second_diag], "svvvvv", 4 * one, scratch
    )
    (block_second,) = call(last_kernel, [wide], [where, second_mine, second_other, base], "svvv", size * width)
    shape = first_panel.shape
    return column_first.reshape(shape), block_first, block_link, column_second.reshape(shape), block_second


def solution(mesh):
    return jax.shard_map(
        shards,
        mesh=mesh,
        in_specs=(
            P("groups", "row", None, None, None),
            P("groups", "row", None, None),
            P("groups", "row", None, None),
            P("groups", None),
            P("groups", None),
            P("groups", None),
            P("groups", "row", None),
            P("groups", "row"),
        ),
        out_specs=(
            P("groups", "row", None, None),
            P("groups", None),
            P("groups", None),
            P("groups", "row", None, None),
            P("groups", None),
        ),
        check_vma=False,
    )
```

```python
import functools

import jax
import jax.numpy as jnp
from jax import lax
from jax.experimental import pallas as pl
from jax.experimental.pallas import tpu as pltpu
from jax.sharding import PartitionSpec as P

VMEM_BYTES = 14 * 1024 * 1024


def call(body, outs, args, spaces, flops, scratch=()):
    kinds = {"s": pltpu.SMEM, "v": pltpu.VMEM, "h": pltpu.HBM}
    moved = sum(a.size * a.dtype.itemsize for a in args) + sum(o.size * o.dtype.itemsize for o in outs)
    return pl.pallas_call(
        body,
        out_shape=outs,
        in_specs=[pl.BlockSpec(memory_space=kinds[c]) for c in spaces],
        out_specs=[pl.BlockSpec(memory_space=pltpu.VMEM)] * len(outs),
        scratch_shapes=list(scratch),
        compiler_params=pltpu.CompilerParams(vmem_limit_bytes=VMEM_BYTES),
        cost_estimate=pl.CostEstimate(flops=flops, bytes_accessed=moved, transcendentals=0),
    )(*args)


def dot(a, b):
    return lax.dot_general(a, b, (((1,), (0,)), ((), ())), preferred_element_type=jnp.float32)


def dot_t(a, b):
    return lax.dot_general(a, b, (((0,), (0,)), ((), ())), preferred_element_type=jnp.float32)


def offsets_of(where_ref):
    member = where_ref[0] % 4
    across = jnp.where(member < 2, 2, -2)
    beside = jnp.where(member % 2 == 0, 1, -1)
    return jnp.int32(0), beside, across, -across, -beside


def near_kernel(where_ref, list_ref, count_ref, sigma_hbm, lower_hbm, first, second,
                first_beside, second_beside,
                first_acc, second_acc, turned_ref, sigma_ref, lower_ref, near_ref, sems):
    lives = []
    copies = []
    for index, offset in enumerate(offsets_of(where_ref)):
        slot = jnp.int32(0)
        live = jnp.int32(0)
        for s in range(sigma_hbm.shape[0]):
            hit = (list_ref[s] == offset) & (s < count_ref[0])
            slot = jnp.where(hit, s, slot)
            live = jnp.where(hit, 1, live)
        target = near_ref.at[index] if index < 2 else sigma_ref.at[index - 2]
        lives.append((live, target))
        copies.append(pltpu.make_async_copy(sigma_hbm.at[slot], target, sems.at[index]))
    copies.append(pltpu.make_async_copy(lower_hbm, lower_ref, sems.at[5]))
    for copy in copies:
        copy.start()

    def arrived(index):
        copies[index].wait()
        live, target = lives[index]

        @pl.when(live == 0)
        def _():
            target[...] = jnp.zeros(target.shape, target.dtype)

    size = first.shape[0]
    turned_ref[:size] = first[...].T
    turned_ref[size:] = second[...].T
    arrived(0)
    first_acc[...] = dot(near_ref[0], first[...])
    second_acc[...] = dot(near_ref[0], second[...])
    arrived(1)
    first_acc[...] += dot(near_ref[1], first_beside[...])
    second_acc[...] += dot(near_ref[1], second_beside[...])
    for index in (2, 3, 4):
        arrived(index)
    copies[5].wait()


def halves(value, where_ref, scratch_ref, give_ref, keep_ref, index):
    scratch_ref[...] = value
    half = value.shape[0] // 2
    core = where_ref[0] % 2
    keep_ref[index] = scratch_ref[pl.ds(pl.multiple_of(core * half, half), half)]
    give_ref[index] = scratch_ref[pl.ds(pl.multiple_of((1 - core) * half, half), half)].astype(jnp.bfloat16)


def first_kernel(where_ref, acc_in, across, far, rest, sigma_ref, turned_ref,
                 column_ref, again_ref, give_ref, keep_ref, acc_ref):
    acc_ref[...] = acc_in[...]
    acc_ref[...] += dot(sigma_ref[0], across[...])
    acc_ref[...] += dot(sigma_ref[1], far[...])
    acc_ref[...] += dot(sigma_ref[2], rest[...])
    column = (-acc_ref[...]).astype(jnp.bfloat16)
    column_ref[...] = column
    again_ref[...] = column
    size = column.shape[0]
    halves(-dot(turned_ref[:size], column), where_ref, acc_ref, give_ref, keep_ref, 0)
    halves(dot(turned_ref[size:], column), where_ref, acc_ref, give_ref, keep_ref, 1)


def across_kernel(acc_in, column_ref, lower_ref, across, sigma_ref, acc_ref):
    acc_ref[...] = acc_in[...] + dot(column_ref[...], lower_ref[...])
    acc_ref[...] += dot(sigma_ref[0], across[...])


def second_kernel(where_ref, acc_in, far, rest, sigma_ref, turned_ref,
                  column_ref, give_ref, keep_ref, acc_ref):
    acc_ref[...] = acc_in[...]
    acc_ref[...] += dot(sigma_ref[1], far[...])
    acc_ref[...] += dot(sigma_ref[2], rest[...])
    column = (-acc_ref[...]).astype(jnp.bfloat16)
    column_ref[...] = column
    size = column.shape[0]
    halves(-dot(turned_ref[size:], column), where_ref, acc_ref, give_ref, keep_ref, 0)


def split(value):
    high = value.astype(jnp.bfloat16)
    low = (value - high.astype(jnp.float32)).astype(jnp.bfloat16)
    return high, low


def place(where_ref, mine_ref, other_ref, index, out_ref):
    half = mine_ref.shape[1]
    core = where_ref[0] % 2
    out_ref[pl.ds(pl.multiple_of(core * half, half), half)] = mine_ref[index].astype(jnp.float32)
    out_ref[pl.ds(pl.multiple_of((1 - core) * half, half), half)] = other_ref[index].astype(jnp.float32)


def link_kernel(where_ref, mine_ref, other_ref, lower_ref, first_diag_ref, second_diag_ref,
                first_ref, link_ref, base_ref, sum_ref):
    lower = lower_ref[...]
    place(where_ref, mine_ref, other_ref, 0, sum_ref)
    block_first = first_diag_ref[...] + sum_ref[...]
    first_ref[...] = block_first
    place(where_ref, mine_ref, other_ref, 1, sum_ref)
    high, low = split(block_first)
    link = dot(high, lower) + dot(low, lower) + sum_ref[...].T
    link_ref[...] = -link
    high, low = split(link)
    base_ref[...] = second_diag_ref[...] + dot_t(lower, high) + dot_t(lower, low)


def last_kernel(where_ref, mine_ref, other_ref, base_ref, second_ref):
    place(where_ref, mine_ref, other_ref, 0, second_ref)
    second_ref[...] += base_ref[...]


def swapped(value, bit, devices):
    return lax.ppermute(value, "row", [(i, i ^ bit) for i in range(devices)])


def far_of(across, devices):
    hops = [(i, i + 4 if i % 4 < 2 else i - 4) for i in range(devices)]
    return lax.ppermute(across, "row", [(a, b) for a, b in hops if 0 <= b < devices])


def rest_of(across, far, give_across, devices):
    rows = across.shape[0] // len(far)
    pieces = [jnp.where(give_across, across[i * rows : (i + 1) * rows], piece) for i, piece in enumerate(far)]
    return swapped(jnp.concatenate(pieces, axis=0), 1, devices)


def core_summed(give, keep, uppers, devices):
    return halved(keep + swapped(give, 1, devices).astype(jnp.float32), uppers[1])


def chip_summed(give, keep, devices):
    return keep + swapped(give, 2, devices).astype(jnp.float32)


def halved(total, upper):
    half = total.shape[1] // 2
    low, high = total[:, :half], total[:, half:]
    return jnp.where(upper, low, high).astype(jnp.bfloat16), jnp.where(upper, high, low)


def summed(total, uppers, devices):
    last = len(uppers) - 1
    for b in range(2, last):
        give, keep = halved(total, uppers[b])
        total = keep + swapped(give, 2 ** b, devices).astype(jnp.float32)
    own = total.astype(jnp.bfloat16)
    gathered = (own.astype(jnp.float32) + swapped(own, 2 ** last, devices).astype(jnp.float32)).astype(jnp.bfloat16)
    for b in range(last - 1, 0, -1):
        other = swapped(gathered, 2 ** b, devices)
        low = jnp.where(uppers[b], other, gathered)
        high = jnp.where(uppers[b], gathered, other)
        gathered = jnp.concatenate([low, high], axis=1)
    return gathered, swapped(gathered, 1, devices)


def shards(sigma_blocks, first_panel, second_panel, lower_panel, first_diag, second_diag, task_list, task_count):
    barrier = lax.optimization_barrier
    devices = lax.axis_size("row")
    position = lax.axis_index("row").astype(jnp.int32)
    slots, size, width = sigma_blocks.shape[-3:]
    sigma = sigma_blocks.reshape((slots, size, width))
    first = first_panel.reshape((size, width))
    second = second_panel.reshape((size, width))
    where = position.reshape((1,))
    bits = [(position >> b) & 1 for b in range(devices.bit_length() - 1)]
    uppers = [bit == 1 for bit in bits]
    give_across = bits[0] == bits[1]
    where, uppers, give_across, first, second = barrier((where, uppers, give_across, first, second))
    listed = task_list.reshape((slots,))
    count = task_count.reshape((1,))
    one = 2 * size * size * width
    half = size // 2
    narrow = jax.ShapeDtypeStruct((size, width), jnp.bfloat16)
    wide = jax.ShapeDtypeStruct((size, width), jnp.float32)
    scratch = [pltpu.VMEM((size, width), jnp.float32)]

    def parts(k):
        return [jax.ShapeDtypeStruct((k, half, width), t) for t in (jnp.bfloat16, jnp.float32)]

    across = swapped(first, 2, devices)
    second_across = swapped(second, 2, devices)
    beside = swapped(first, 1, devices)
    second_beside = swapped(second, 1, devices)
    first_acc, second_acc, turned, sorted_sigma, lower = call(
        near_kernel,
        [wide, wide, jax.ShapeDtypeStruct((2 * size, width), jnp.bfloat16),
         jax.ShapeDtypeStruct((3, size, width), jnp.bfloat16), narrow],
        [where, listed, count, sigma, lower_panel, first, second, beside, second_beside],
        "ssshhvvvv",
        4 * one,
        [pltpu.VMEM((2, size, width), jnp.bfloat16), pltpu.SemaphoreType.DMA((6,))],
    )
    across, turned = barrier((across, turned))
    far = far_of(across, devices)
    far, second_across = barrier((far, second_across))
    second_far = far_of(second_across, devices)
    rest = rest_of(across, [far], give_across, devices)
    column_first, column_again, give, keep = call(
        first_kernel,
        [narrow, narrow] + parts(2),
        [where, first_acc, across, far, rest, sorted_sigma, turned],
        "svvvvvv",
        5 * one,
        scratch,
    )
    give, second_across = barrier((give, second_across))
    give, keep = core_summed(give, keep, uppers, devices)
    second_rest = rest_of(second_across, [second_far], give_across, devices)
    total = chip_summed(give, keep, devices)
    (second_acc,) = call(
        across_kernel, [wide], [second_acc, column_again, lower, second_across, sorted_sigma], "vvvvv", 2 * one
    )
    column_second, second_give, second_keep = call(
        second_kernel,
        [narrow] + parts(1),
        [where, second_acc, second_far, second_rest, sorted_sigma, turned],
        "svvvvv",
        3 * one,
        scratch,
    )
    second_give, total = barrier((second_give, total))
    second_give, second_keep = core_summed(second_give, second_keep, uppers, devices)
    mine, other = summed(total, uppers, devices)
    second_total = chip_summed(second_give, second_keep, devices)
    second_mine, second_other = summed(second_total, uppers, devices)
    block_first, block_link, base = call(
        link_kernel, [wide] * 3, [where, mine, other, lower, first_diag, second_diag], "svvvvv", 4 * one, scratch
    )
    (block_second,) = call(last_kernel, [wide], [where, second_mine, second_other, base], "svvv", size * width)
    shape = first_panel.shape
    return column_first.reshape(shape), block_first, block_link, column_second.reshape(shape), block_second


def solution(mesh):
    return jax.shard_map(
        shards,
        mesh=mesh,
        in_specs=(
            P("groups", "row", None, None, None),
            P("groups", "row", None, None),
            P("groups", "row", None, None),
            P("groups", None),
            P("groups", None),
            P("groups", None),
            P("groups", "row", None),
            P("groups", "row"),
        ),
        out_specs=(
            P("groups", "row", None, None),
            P("groups", None),
            P("groups", None),
            P("groups", "row", None, None),
            P("groups", None),
        ),
        check_vma=False,
    )
```

```python
import functools

import jax
import jax.numpy as jnp
from jax import lax
from jax.experimental import pallas as pl
from jax.experimental.pallas import tpu as pltpu
from jax.sharding import PartitionSpec as P

VMEM_BYTES = 14 * 1024 * 1024


def call(body, outs, args, spaces, flops, scratch=()):
    kinds = {"s": pltpu.SMEM, "v": pltpu.VMEM, "h": pltpu.HBM}
    moved = sum(a.size * a.dtype.itemsize for a in args) + sum(o.size * o.dtype.itemsize for o in outs)
    return pl.pallas_call(
        body,
        out_shape=outs,
        in_specs=[pl.BlockSpec(memory_space=kinds[c]) for c in spaces],
        out_specs=[pl.BlockSpec(memory_space=pltpu.VMEM)] * len(outs),
        scratch_shapes=list(scratch),
        compiler_params=pltpu.CompilerParams(vmem_limit_bytes=VMEM_BYTES),
        cost_estimate=pl.CostEstimate(flops=flops, bytes_accessed=moved, transcendentals=0),
    )(*args)


def dot(a, b):
    return lax.dot_general(a, b, (((1,), (0,)), ((), ())), preferred_element_type=jnp.float32)


def dot_t(a, b):
    return lax.dot_general(a, b, (((0,), (0,)), ((), ())), preferred_element_type=jnp.float32)


def offsets_of(where_ref):
    member = where_ref[0] % 4
    across = jnp.where(member < 2, 2, -2)
    beside = jnp.where(member % 2 == 0, 1, -1)
    return jnp.int32(0), beside, across, -across, -beside


def split_kernel(panel_hbm, low, high, sems):
    half = low.shape[0]
    copies = [
        pltpu.make_async_copy(panel_hbm.at[pl.ds(index * half, half)], target, sems.at[index])
        for index, target in enumerate((low, high))
    ]
    for copy in copies:
        copy.start()
    for copy in copies:
        copy.wait()


def near_kernel(where_ref, list_ref, count_ref, sigma_hbm, lower_hbm, first_0, first_1, second,
                first_beside, second_beside,
                first_acc, second_acc, turned_ref, sigma_ref, lower_ref, near_ref, sems):
    lives = []
    copies = []
    for index, offset in enumerate(offsets_of(where_ref)):
        slot = jnp.int32(0)
        live = jnp.int32(0)
        for s in range(sigma_hbm.shape[0]):
            hit = (list_ref[s] == offset) & (s < count_ref[0])
            slot = jnp.where(hit, s, slot)
            live = jnp.where(hit, 1, live)
        target = near_ref.at[index] if index < 2 else sigma_ref.at[index - 2]
        lives.append((live, target))
        copies.append(pltpu.make_async_copy(sigma_hbm.at[slot], target, sems.at[index]))
    copies.append(pltpu.make_async_copy(lower_hbm, lower_ref, sems.at[5]))
    for copy in copies:
        copy.start()

    def arrived(index):
        copies[index].wait()
        live, target = lives[index]

        @pl.when(live == 0)
        def _():
            target[...] = jnp.zeros(target.shape, target.dtype)

    half = first_0.shape[0]
    size = 2 * half
    turned_ref[:size, :half] = first_0[...].T
    turned_ref[:size, half:] = first_1[...].T
    turned_ref[size:] = second[...].T
    arrived(0)
    first_acc[...] = dot(near_ref[0, :, :half], first_0[...])
    first_acc[...] += dot(near_ref[0, :, half:], first_1[...])
    second_acc[...] = dot(near_ref[0], second[...])
    arrived(1)
    first_acc[...] += dot(near_ref[1], first_beside[...])
    second_acc[...] += dot(near_ref[1], second_beside[...])
    for index in (2, 3, 4):
        arrived(index)
    copies[5].wait()


def halves(value, where_ref, scratch_ref, give_ref, keep_ref, index):
    scratch_ref[...] = value
    half = value.shape[0] // 2
    core = where_ref[0] % 2
    keep_ref[index] = scratch_ref[pl.ds(pl.multiple_of(core * half, half), half)]
    give_ref[index] = scratch_ref[pl.ds(pl.multiple_of((1 - core) * half, half), half)].astype(jnp.bfloat16)


def first_kernel(where_ref, acc_in, across_0, across_1, far_0, far_1, rest, sigma_ref, turned_ref,
                 column_ref, again_ref, give_ref, keep_ref, acc_ref):
    half = far_0.shape[0]
    acc_ref[...] = acc_in[...]
    acc_ref[...] += dot(sigma_ref[0, :, :half], across_0[...])
    acc_ref[...] += dot(sigma_ref[0, :, half:], across_1[...])
    acc_ref[...] += dot(sigma_ref[1, :, :half], far_0[...])
    acc_ref[...] += dot(sigma_ref[1, :, half:], far_1[...])
    acc_ref[...] += dot(sigma_ref[2], rest[...])
    column = (-acc_ref[...]).astype(jnp.bfloat16)
    column_ref[...] = column
    again_ref[...] = column
    size = column.shape[0]
    halves(-dot(turned_ref[:size], column), where_ref, acc_ref, give_ref, keep_ref, 0)
    halves(dot(turned_ref[size:], column), where_ref, acc_ref, give_ref, keep_ref, 1)


def across_kernel(acc_in, column_ref, lower_ref, across, sigma_ref, acc_ref):
    acc_ref[...] = acc_in[...] + dot(column_ref[...], lower_ref[...])
    acc_ref[...] += dot(sigma_ref[0], across[...])


def second_kernel(where_ref, acc_in, far, rest, sigma_ref, turned_ref,
                  column_ref, give_ref, keep_ref, acc_ref):
    acc_ref[...] = acc_in[...]
    acc_ref[...] += dot(sigma_ref[1], far[...])
    acc_ref[...] += dot(sigma_ref[2], rest[...])
    column = (-acc_ref[...]).astype(jnp.bfloat16)
    column_ref[...] = column
    size = column.shape[0]
    halves(-dot(turned_ref[size:], column), where_ref, acc_ref, give_ref, keep_ref, 0)


def split(value):
    high = value.astype(jnp.bfloat16)
    low = (value - high.astype(jnp.float32)).astype(jnp.bfloat16)
    return high, low


def place(where_ref, mine_ref, other_ref, index, out_ref):
    half = mine_ref.shape[1]
    core = where_ref[0] % 2
    out_ref[pl.ds(pl.multiple_of(core * half, half), half)] = mine_ref[index].astype(jnp.float32)
    out_ref[pl.ds(pl.multiple_of((1 - core) * half, half), half)] = other_ref[index].astype(jnp.float32)


def link_kernel(where_ref, mine_ref, other_ref, lower_ref, first_diag_ref, second_diag_ref,
                first_ref, link_ref, base_ref, sum_ref):
    lower = lower_ref[...]
    place(where_ref, mine_ref, other_ref, 0, sum_ref)
    block_first = first_diag_ref[...] + sum_ref[...]
    first_ref[...] = block_first
    place(where_ref, mine_ref, other_ref, 1, sum_ref)
    high, low = split(block_first)
    link = dot(high, lower) + dot(low, lower) + sum_ref[...].T
    link_ref[...] = -link
    high, low = split(link)
    base_ref[...] = second_diag_ref[...] + dot_t(lower, high) + dot_t(lower, low)


def last_kernel(where_ref, mine_ref, other_ref, base_ref, second_ref):
    place(where_ref, mine_ref, other_ref, 0, second_ref)
    second_ref[...] += base_ref[...]


def swapped(value, bit, devices):
    return lax.ppermute(value, "row", [(i, i ^ bit) for i in range(devices)])


def far_of(across, devices):
    hops = [(i, i + 4 if i % 4 < 2 else i - 4) for i in range(devices)]
    return lax.ppermute(across, "row", [(a, b) for a, b in hops if 0 <= b < devices])


def rest_of(across, far, give_across, devices):
    pieces = [jnp.where(give_across, a, f) for a, f in zip(across, far)]
    return swapped(jnp.concatenate(pieces, axis=0), 1, devices)


def core_summed(give, keep, uppers, devices):
    return halved(keep + swapped(give, 1, devices).astype(jnp.float32), uppers[1])


def chip_summed(give, keep, devices):
    return keep + swapped(give, 2, devices).astype(jnp.float32)


def halved(total, upper):
    half = total.shape[1] // 2
    low, high = total[:, :half], total[:, half:]
    return jnp.where(upper, low, high).astype(jnp.bfloat16), jnp.where(upper, high, low)


def summed(total, uppers, devices):
    last = len(uppers) - 1
    for b in range(2, last):
        give, keep = halved(total, uppers[b])
        total = keep + swapped(give, 2 ** b, devices).astype(jnp.float32)
    own = total.astype(jnp.bfloat16)
    gathered = (own.astype(jnp.float32) + swapped(own, 2 ** last, devices).astype(jnp.float32)).astype(jnp.bfloat16)
    for b in range(last - 1, 0, -1):
        other = swapped(gathered, 2 ** b, devices)
        low = jnp.where(uppers[b], other, gathered)
        high = jnp.where(uppers[b], gathered, other)
        gathered = jnp.concatenate([low, high], axis=1)
    return gathered, swapped(gathered, 1, devices)


def shards(sigma_blocks, first_panel, second_panel, lower_panel, first_diag, second_diag, task_list, task_count):
    barrier = lax.optimization_barrier
    devices = lax.axis_size("row")
    position = lax.axis_index("row").astype(jnp.int32)
    slots, size, width = sigma_blocks.shape[-3:]
    sigma = sigma_blocks.reshape((slots, size, width))
    first = first_panel.reshape((size, width))
    second = second_panel.reshape((size, width))
    where = position.reshape((1,))
    bits = [(position >> b) & 1 for b in range(devices.bit_length() - 1)]
    uppers = [bit == 1 for bit in bits]
    give_across = bits[0] == bits[1]
    where, uppers, give_across, first, second = barrier((where, uppers, give_across, first, second))
    listed = task_list.reshape((slots,))
    count = task_count.reshape((1,))
    one = 2 * size * size * width
    half = size // 2
    narrow = jax.ShapeDtypeStruct((size, width), jnp.bfloat16)
    wide = jax.ShapeDtypeStruct((size, width), jnp.float32)
    scratch = [pltpu.VMEM((size, width), jnp.float32)]

    def parts(k):
        return [jax.ShapeDtypeStruct((k, half, width), t) for t in (jnp.bfloat16, jnp.float32)]

    piece = jax.ShapeDtypeStruct((half, width), jnp.bfloat16)
    pieces = call(split_kernel, [piece] * 2, [first], "h", 1, [pltpu.SemaphoreType.DMA((2,))])
    across = [swapped(part, 2, devices) for part in pieces]
    second_across = swapped(second, 2, devices)
    beside = swapped(first, 1, devices)
    second_beside = swapped(second, 1, devices)
    first_acc, second_acc, turned, sorted_sigma, lower = call(
        near_kernel,
        [wide, wide, jax.ShapeDtypeStruct((2 * size, width), jnp.bfloat16),
         jax.ShapeDtypeStruct((3, size, width), jnp.bfloat16), narrow],
        [where, listed, count, sigma, lower_panel, *pieces, second, beside, second_beside],
        "ssshhvvvvv",
        4 * one,
        [pltpu.VMEM((2, size, width), jnp.bfloat16), pltpu.SemaphoreType.DMA((6,))],
    )
    across[1], turned = barrier((across[1], turned))
    far = [far_of(part, devices) for part in across]
    second_far = far_of(second_across, devices)
    far, second_across = barrier((far, second_across))
    rest = rest_of(across, far, give_across, devices)
    column_first, column_again, give, keep = call(
        first_kernel,
        [narrow, narrow] + parts(2),
        [where, first_acc, *across, *far, rest, sorted_sigma, turned],
        "svvvvvvvv",
        5 * one,
        scratch,
    )
    give, second_across = barrier((give, second_across))
    give, keep = core_summed(give, keep, uppers, devices)
    second_rest = rest_of([second_across], [second_far], give_across, devices)
    total = chip_summed(give, keep, devices)
    (second_acc,) = call(
        across_kernel, [wide], [second_acc, column_again, lower, second_across, sorted_sigma], "vvvvv", 2 * one
    )
    column_second, second_give, second_keep = call(
        second_kernel,
        [narrow] + parts(1),
        [where, second_acc, second_far, second_rest, sorted_sigma, turned],
        "svvvvv",
        3 * one,
        scratch,
    )
    second_give, total = barrier((second_give, total))
    second_give, second_keep = core_summed(second_give, second_keep, uppers, devices)
    mine, other = summed(total, uppers, devices)
    second_total = chip_summed(second_give, second_keep, devices)
    second_mine, second_other = summed(second_total, uppers, devices)
    block_first, block_link, base = call(
        link_kernel, [wide] * 3, [where, mine, other, lower, first_diag, second_diag], "svvvvv", 4 * one, scratch
    )
    (block_second,) = call(last_kernel, [wide], [where, second_mine, second_other, base], "svvv", size * width)
    shape = first_panel.shape
    return column_first.reshape(shape), block_first, block_link, column_second.reshape(shape), block_second


def solution(mesh):
    return jax.shard_map(
        shards,
        mesh=mesh,
        in_specs=(
            P("groups", "row", None, None, None),
            P("groups", "row", None, None),
            P("groups", "row", None, None),
            P("groups", None),
            P("groups", None),
            P("groups", None),
            P("groups", "row", None),
            P("groups", "row"),
        ),
        out_specs=(
            P("groups", "row", None, None),
            P("groups", None),
            P("groups", None),
            P("groups", "row", None, None),
            P("groups", None),
        ),
        check_vma=False,
    )
```

```python
import functools

import jax
import jax.numpy as jnp
from jax import lax
from jax.experimental import pallas as pl
from jax.experimental.pallas import tpu as pltpu
from jax.sharding import PartitionSpec as P

VMEM_BYTES = 14 * 1024 * 1024


def call(body, outs, args, spaces, flops, scratch=()):
    kinds = {"s": pltpu.SMEM, "v": pltpu.VMEM, "h": pltpu.HBM}
    moved = sum(a.size * a.dtype.itemsize for a in args) + sum(o.size * o.dtype.itemsize for o in outs)
    return pl.pallas_call(
        body,
        out_shape=outs,
        in_specs=[pl.BlockSpec(memory_space=kinds[c]) for c in spaces],
        out_specs=[pl.BlockSpec(memory_space=pltpu.VMEM)] * len(outs),
        scratch_shapes=list(scratch),
        compiler_params=pltpu.CompilerParams(vmem_limit_bytes=VMEM_BYTES),
        cost_estimate=pl.CostEstimate(flops=flops, bytes_accessed=moved, transcendentals=0),
    )(*args)


def dot(a, b):
    return lax.dot_general(a, b, (((1,), (0,)), ((), ())), preferred_element_type=jnp.float32)


def dot_t(a, b):
    return lax.dot_general(a, b, (((0,), (0,)), ((), ())), preferred_element_type=jnp.float32)


def offsets_of(where_ref):
    member = where_ref[0] % 4
    across = jnp.where(member < 2, 2, -2)
    beside = jnp.where(member % 2 == 0, 1, -1)
    return jnp.int32(0), beside, across, -across, -beside


def split_kernel(panel_hbm, low, high, sems):
    half = low.shape[0]
    copies = [
        pltpu.make_async_copy(panel_hbm.at[pl.ds(index * half, half)], target, sems.at[index])
        for index, target in enumerate((low, high))
    ]
    for copy in copies:
        copy.start()
    for copy in copies:
        copy.wait()


def near_kernel(where_ref, list_ref, count_ref, sigma_hbm, lower_hbm, first_0, first_1, second,
                first_beside, second_beside,
                first_acc, second_acc, turned_ref, sigma_ref, lower_ref, near_ref, sems):
    lives = []
    copies = []
    for index, offset in enumerate(offsets_of(where_ref)):
        slot = jnp.int32(0)
        live = jnp.int32(0)
        for s in range(sigma_hbm.shape[0]):
            hit = (list_ref[s] == offset) & (s < count_ref[0])
            slot = jnp.where(hit, s, slot)
            live = jnp.where(hit, 1, live)
        target = near_ref.at[index] if index < 2 else sigma_ref.at[index - 2]
        lives.append((live, target))
        copies.append(pltpu.make_async_copy(sigma_hbm.at[slot], target, sems.at[index]))
    copies.append(pltpu.make_async_copy(lower_hbm, lower_ref, sems.at[5]))
    for copy in copies:
        copy.start()

    def arrived(index):
        copies[index].wait()
        live, target = lives[index]

        @pl.when(live == 0)
        def _():
            target[...] = jnp.zeros(target.shape, target.dtype)

    half = first_0.shape[0]
    size = 2 * half
    turned_ref[:size, :half] = first_0[...].T
    turned_ref[:size, half:] = first_1[...].T
    turned_ref[size:] = second[...].T
    arrived(0)
    first_acc[...] = dot(near_ref[0, :, :half], first_0[...])
    first_acc[...] += dot(near_ref[0, :, half:], first_1[...])
    second_acc[...] = dot(near_ref[0], second[...])
    arrived(1)
    first_acc[...] += dot(near_ref[1], first_beside[...])
    second_acc[...] += dot(near_ref[1], second_beside[...])
    for index in (2, 3, 4):
        arrived(index)
    copies[5].wait()


def halves(value, where_ref, scratch_ref, give_ref, keep_ref, index):
    scratch_ref[...] = value
    half = value.shape[0] // 2
    core = where_ref[0] % 2
    keep_ref[index] = scratch_ref[pl.ds(pl.multiple_of(core * half, half), half)]
    give_ref[index] = scratch_ref[pl.ds(pl.multiple_of((1 - core) * half, half), half)].astype(jnp.bfloat16)


def first_kernel(where_ref, acc_in, across_0, across_1, far_0, far_1, rest, sigma_ref, turned_ref,
                 column_ref, again_ref, give_ref, keep_ref, acc_ref):
    half = far_0.shape[0]
    acc_ref[...] = acc_in[...]
    acc_ref[...] += dot(sigma_ref[0, :, :half], across_0[...])
    acc_ref[...] += dot(sigma_ref[0, :, half:], across_1[...])
    acc_ref[...] += dot(sigma_ref[1, :, :half], far_0[...])
    acc_ref[...] += dot(sigma_ref[1, :, half:], far_1[...])
    acc_ref[...] += dot(sigma_ref[2], rest[...])
    column = (-acc_ref[...]).astype(jnp.bfloat16)
    column_ref[...] = column
    again_ref[...] = column
    size = column.shape[0]
    halves(-dot(turned_ref[:size], column), where_ref, acc_ref, give_ref, keep_ref, 0)
    halves(dot(turned_ref[size:], column), where_ref, acc_ref, give_ref, keep_ref, 1)


def across_kernel(acc_in, column_ref, lower_ref, across, sigma_ref, acc_ref):
    acc_ref[...] = acc_in[...] + dot(column_ref[...], lower_ref[...])
    acc_ref[...] += dot(sigma_ref[0], across[...])


def second_kernel(where_ref, acc_in, far, rest, sigma_ref, turned_ref,
                  column_ref, give_ref, keep_ref, acc_ref):
    acc_ref[...] = acc_in[...]
    acc_ref[...] += dot(sigma_ref[1], far[...])
    acc_ref[...] += dot(sigma_ref[2], rest[...])
    column = (-acc_ref[...]).astype(jnp.bfloat16)
    column_ref[...] = column
    size = column.shape[0]
    halves(-dot(turned_ref[size:], column), where_ref, acc_ref, give_ref, keep_ref, 0)


def split(value):
    high = value.astype(jnp.bfloat16)
    low = (value - high.astype(jnp.float32)).astype(jnp.bfloat16)
    return high, low


def place(where_ref, mine_ref, other_ref, index, out_ref):
    half = mine_ref.shape[1]
    core = where_ref[0] % 2
    out_ref[pl.ds(pl.multiple_of(core * half, half), half)] = mine_ref[index].astype(jnp.float32)
    out_ref[pl.ds(pl.multiple_of((1 - core) * half, half), half)] = other_ref[index].astype(jnp.float32)


def link_kernel(where_ref, mine_ref, other_ref, lower_ref, first_diag_ref, second_diag_ref,
                first_ref, link_ref, base_ref, sum_ref):
    lower = lower_ref[...]
    place(where_ref, mine_ref, other_ref, 0, sum_ref)
    block_first = first_diag_ref[...] + sum_ref[...]
    first_ref[...] = block_first
    place(where_ref, mine_ref, other_ref, 1, sum_ref)
    high, low = split(block_first)
    link = dot(high, lower) + dot(low, lower) + sum_ref[...].T
    link_ref[...] = -link
    high, low = split(link)
    base_ref[...] = second_diag_ref[...] + dot_t(lower, high) + dot_t(lower, low)


def last_kernel(where_ref, mine_ref, other_ref, base_ref, second_ref):
    place(where_ref, mine_ref, other_ref, 0, second_ref)
    second_ref[...] += base_ref[...]


def swapped(value, bit, devices):
    return lax.ppermute(value, "row", [(i, i ^ bit) for i in range(devices)])


def far_of(across, devices, closed=False):
    hops = [(i, i + 4 if i % 4 < 2 else i - 4) for i in range(devices)]
    pairs = [(a, b if 0 <= b < devices else a ^ 2) for a, b in hops]
    if not closed:
        pairs = [(a, b) for a, b in hops if 0 <= b < devices]
    return lax.ppermute(across, "row", pairs)


def rest_of(across, far, give_across, devices):
    pieces = [jnp.where(give_across, a, f) for a, f in zip(across, far)]
    return swapped(jnp.concatenate(pieces, axis=0), 1, devices)


def core_summed(give, keep, uppers, devices):
    return halved(keep + swapped(give, 1, devices).astype(jnp.float32), uppers[1])


def chip_summed(give, keep, devices):
    return keep + swapped(give, 2, devices).astype(jnp.float32)


def halved(total, upper):
    half = total.shape[1] // 2
    low, high = total[:, :half], total[:, half:]
    return jnp.where(upper, low, high).astype(jnp.bfloat16), jnp.where(upper, high, low)


def summed(total, uppers, devices):
    last = len(uppers) - 1
    for b in range(2, last):
        give, keep = halved(total, uppers[b])
        total = keep + swapped(give, 2 ** b, devices).astype(jnp.float32)
    own = total.astype(jnp.bfloat16)
    gathered = (own.astype(jnp.float32) + swapped(own, 2 ** last, devices).astype(jnp.float32)).astype(jnp.bfloat16)
    for b in range(last - 1, 0, -1):
        other = swapped(gathered, 2 ** b, devices)
        low = jnp.where(uppers[b], other, gathered)
        high = jnp.where(uppers[b], gathered, other)
        gathered = jnp.concatenate([low, high], axis=1)
    return gathered, swapped(gathered, 1, devices)


def shards(sigma_blocks, first_panel, second_panel, lower_panel, first_diag, second_diag, task_list, task_count):
    barrier = lax.optimization_barrier
    devices = lax.axis_size("row")
    position = lax.axis_index("row").astype(jnp.int32)
    slots, size, width = sigma_blocks.shape[-3:]
    sigma = sigma_blocks.reshape((slots, size, width))
    first = first_panel.reshape((size, width))
    second = second_panel.reshape((size, width))
    where = position.reshape((1,))
    bits = [(position >> b) & 1 for b in range(devices.bit_length() - 1)]
    uppers = [bit == 1 for bit in bits]
    give_across = bits[0] == bits[1]
    where, uppers, give_across, first, second = barrier((where, uppers, give_across, first, second))
    listed = task_list.reshape((slots,))
    count = task_count.reshape((1,))
    one = 2 * size * size * width
    half = size // 2
    narrow = jax.ShapeDtypeStruct((size, width), jnp.bfloat16)
    wide = jax.ShapeDtypeStruct((size, width), jnp.float32)
    scratch = [pltpu.VMEM((size, width), jnp.float32)]

    def parts(k):
        return [jax.ShapeDtypeStruct((k, half, width), t) for t in (jnp.bfloat16, jnp.float32)]

    piece = jax.ShapeDtypeStruct((half, width), jnp.bfloat16)
    pieces = call(split_kernel, [piece] * 2, [first], "h", 1, [pltpu.SemaphoreType.DMA((2,))])
    across = [swapped(part, 2, devices) for part in pieces]
    second_across = swapped(second, 2, devices)
    beside = swapped(first, 1, devices)
    second_beside = swapped(second, 1, devices)
    first_acc, second_acc, turned, sorted_sigma, lower = call(
        near_kernel,
        [wide, wide, jax.ShapeDtypeStruct((2 * size, width), jnp.bfloat16),
         jax.ShapeDtypeStruct((3, size, width), jnp.bfloat16), narrow],
        [where, listed, count, sigma, lower_panel, *pieces, second, beside, second_beside],
        "ssshhvvvvv",
        4 * one,
        [pltpu.VMEM((2, size, width), jnp.bfloat16), pltpu.SemaphoreType.DMA((6,))],
    )
    far = [far_of(part, devices) for part in across]
    second_far = far_of(second_across, devices, closed=True)
    far, second_across, turned = barrier((far, second_across, turned))
    rest = rest_of(across, far, give_across, devices)
    column_first, column_again, give, keep = call(
        first_kernel,
        [narrow, narrow] + parts(2),
        [where, first_acc, *across, *far, rest, sorted_sigma, turned],
        "svvvvvvvv",
        5 * one,
        scratch,
    )
    give, second_across = barrier((give, second_across))
    give, keep = core_summed(give, keep, uppers, devices)
    second_rest = rest_of([second_across], [second_far], give_across, devices)
    total = chip_summed(give, keep, devices)
    (second_acc,) = call(
        across_kernel, [wide], [second_acc, column_again, lower, second_across, sorted_sigma], "vvvvv", 2 * one
    )
    column_second, second_give, second_keep = call(
        second_kernel,
        [narrow] + parts(1),
        [where, second_acc, second_far, second_rest, sorted_sigma, turned],
        "svvvvv",
        3 * one,
        scratch,
    )
    second_give, total = barrier((second_give, total))
    second_give, second_keep = core_summed(second_give, second_keep, uppers, devices)
    mine, other = summed(total, uppers, devices)
    second_total = chip_summed(second_give, second_keep, devices)
    second_mine, second_other = summed(second_total, uppers, devices)
    block_first, block_link, base = call(
        link_kernel, [wide] * 3, [where, mine, other, lower, first_diag, second_diag], "svvvvv", 4 * one, scratch
    )
    (block_second,) = call(last_kernel, [wide], [where, second_mine, second_other, base], "svvv", size * width)
    shape = first_panel.shape
    return column_first.reshape(shape), block_first, block_link, column_second.reshape(shape), block_second


def solution(mesh):
    return jax.shard_map(
        shards,
        mesh=mesh,
        in_specs=(
            P("groups", "row", None, None, None),
            P("groups", "row", None, None),
            P("groups", "row", None, None),
            P("groups", None),
            P("groups", None),
            P("groups", None),
            P("groups", "row", None),
            P("groups", "row"),
        ),
        out_specs=(
            P("groups", "row", None, None),
            P("groups", None),
            P("groups", None),
            P("groups", "row", None, None),
            P("groups", None),
        ),
        check_vma=False,
    )
```

```python
import functools

import jax
import jax.numpy as jnp
from jax import lax
from jax.experimental import pallas as pl
from jax.experimental.pallas import tpu as pltpu
from jax.sharding import PartitionSpec as P

VMEM_BYTES = 14 * 1024 * 1024


def call(body, outs, args, spaces, flops, scratch=()):
    kinds = {"s": pltpu.SMEM, "v": pltpu.VMEM, "h": pltpu.HBM}
    moved = sum(a.size * a.dtype.itemsize for a in args) + sum(o.size * o.dtype.itemsize for o in outs)
    return pl.pallas_call(
        body,
        out_shape=outs,
        in_specs=[pl.BlockSpec(memory_space=kinds[c]) for c in spaces],
        out_specs=[pl.BlockSpec(memory_space=pltpu.VMEM)] * len(outs),
        scratch_shapes=list(scratch),
        compiler_params=pltpu.CompilerParams(vmem_limit_bytes=VMEM_BYTES),
        cost_estimate=pl.CostEstimate(flops=flops, bytes_accessed=moved, transcendentals=0),
    )(*args)


def dot(a, b):
    return lax.dot_general(a, b, (((1,), (0,)), ((), ())), preferred_element_type=jnp.float32)


def dot_t(a, b):
    return lax.dot_general(a, b, (((0,), (0,)), ((), ())), preferred_element_type=jnp.float32)


def offsets_of(where_ref):
    member = where_ref[0] % 4
    across = jnp.where(member < 2, 2, -2)
    beside = jnp.where(member % 2 == 0, 1, -1)
    return jnp.int32(0), beside, across, -across, -beside


def split_kernel(panel_hbm, low, high, sems):
    half = low.shape[0]
    copies = [
        pltpu.make_async_copy(panel_hbm.at[pl.ds(index * half, half)], target, sems.at[index])
        for index, target in enumerate((low, high))
    ]
    for copy in copies:
        copy.start()
    for copy in copies:
        copy.wait()


def near_kernel(where_ref, list_ref, count_ref, sigma_hbm, lower_hbm, first_0, first_1, second,
                first_beside, second_beside,
                first_acc, second_acc, turned_ref, sigma_ref, lower_ref, near_ref, sems):
    lives = []
    copies = []
    for index, offset in enumerate(offsets_of(where_ref)):
        slot = jnp.int32(0)
        live = jnp.int32(0)
        for s in range(sigma_hbm.shape[0]):
            hit = (list_ref[s] == offset) & (s < count_ref[0])
            slot = jnp.where(hit, s, slot)
            live = jnp.where(hit, 1, live)
        target = near_ref.at[index] if index < 2 else sigma_ref.at[index - 2]
        lives.append((live, target))
        copies.append(pltpu.make_async_copy(sigma_hbm.at[slot], target, sems.at[index]))
    copies.append(pltpu.make_async_copy(lower_hbm, lower_ref, sems.at[5]))
    for copy in copies:
        copy.start()

    def arrived(index):
        copies[index].wait()
        live, target = lives[index]

        @pl.when(live == 0)
        def _():
            target[...] = jnp.zeros(target.shape, target.dtype)

    half = first_0.shape[0]
    size = 2 * half
    turned_ref[:size, :half] = first_0[...].T
    turned_ref[:size, half:] = first_1[...].T
    turned_ref[size:] = second[...].T
    arrived(0)
    first_acc[...] = dot(near_ref[0, :, :half], first_0[...])
    first_acc[...] += dot(near_ref[0, :, half:], first_1[...])
    second_acc[...] = dot(near_ref[0], second[...])
    arrived(1)
    first_acc[...] += dot(near_ref[1], first_beside[...])
    second_acc[...] += dot(near_ref[1], second_beside[...])
    for index in (2, 3, 4):
        arrived(index)
    copies[5].wait()


def halves(value, where_ref, scratch_ref, give_ref, keep_ref, index):
    scratch_ref[...] = value
    half = value.shape[0] // 2
    core = where_ref[0] % 2
    keep_ref[index] = scratch_ref[pl.ds(pl.multiple_of(core * half, half), half)]
    give_ref[index] = scratch_ref[pl.ds(pl.multiple_of((1 - core) * half, half), half)].astype(jnp.bfloat16)


def first_kernel(where_ref, acc_in, across_0, across_1, far_0, far_1, rest, sigma_ref, turned_ref,
                 column_ref, again_ref, give_ref, keep_ref, acc_ref):
    half = far_0.shape[0]
    acc_ref[...] = acc_in[...]
    acc_ref[...] += dot(sigma_ref[0, :, :half], across_0[...])
    acc_ref[...] += dot(sigma_ref[0, :, half:], across_1[...])
    acc_ref[...] += dot(sigma_ref[1, :, :half], far_0[...])
    acc_ref[...] += dot(sigma_ref[1, :, half:], far_1[...])
    acc_ref[...] += dot(sigma_ref[2], rest[...])
    column = (-acc_ref[...]).astype(jnp.bfloat16)
    column_ref[...] = column
    again_ref[...] = column
    size = column.shape[0]
    halves(-dot(turned_ref[:size], column), where_ref, acc_ref, give_ref, keep_ref, 0)
    halves(dot(turned_ref[size:], column), where_ref, acc_ref, give_ref, keep_ref, 1)


def across_kernel(acc_in, column_ref, lower_ref, across, sigma_ref, acc_ref):
    acc_ref[...] = acc_in[...] + dot(column_ref[...], lower_ref[...])
    acc_ref[...] += dot(sigma_ref[0], across[...])


def second_kernel(where_ref, acc_in, far_0, far_1, rest, sigma_ref, turned_ref,
                  column_ref, give_ref, keep_ref, acc_ref):
    rows = far_0.shape[0]
    acc_ref[...] = acc_in[...]
    acc_ref[...] += dot(sigma_ref[1, :, :rows], far_0[...])
    acc_ref[...] += dot(sigma_ref[1, :, rows:], far_1[...])
    acc_ref[...] += dot(sigma_ref[2], rest[...])
    column = (-acc_ref[...]).astype(jnp.bfloat16)
    column_ref[...] = column
    size = column.shape[0]
    halves(-dot(turned_ref[size:], column), where_ref, acc_ref, give_ref, keep_ref, 0)


def split(value):
    high = value.astype(jnp.bfloat16)
    low = (value - high.astype(jnp.float32)).astype(jnp.bfloat16)
    return high, low


def place(where_ref, mine_ref, other_ref, index, out_ref):
    half = mine_ref.shape[1]
    core = where_ref[0] % 2
    out_ref[pl.ds(pl.multiple_of(core * half, half), half)] = mine_ref[index].astype(jnp.float32)
    out_ref[pl.ds(pl.multiple_of((1 - core) * half, half), half)] = other_ref[index].astype(jnp.float32)


def link_kernel(where_ref, mine_ref, other_ref, lower_ref, first_diag_ref, second_diag_ref,
                first_ref, link_ref, base_ref, sum_ref):
    lower = lower_ref[...]
    place(where_ref, mine_ref, other_ref, 0, sum_ref)
    block_first = first_diag_ref[...] + sum_ref[...]
    first_ref[...] = block_first
    place(where_ref, mine_ref, other_ref, 1, sum_ref)
    high, low = split(block_first)
    link = dot(high, lower) + dot(low, lower) + sum_ref[...].T
    link_ref[...] = -link
    high, low = split(link)
    base_ref[...] = second_diag_ref[...] + dot_t(lower, high) + dot_t(lower, low)


def last_kernel(where_ref, mine_ref, other_ref, base_ref, second_ref):
    place(where_ref, mine_ref, other_ref, 0, second_ref)
    second_ref[...] += base_ref[...]


def swapped(value, bit, devices):
    return lax.ppermute(value, "row", [(i, i ^ bit) for i in range(devices)])


def far_of(across, devices, closed=False):
    hops = [(i, i + 4 if i % 4 < 2 else i - 4) for i in range(devices)]
    pairs = [(a, b if 0 <= b < devices else a ^ 2) for a, b in hops]
    if not closed:
        pairs = [(a, b) for a, b in hops if 0 <= b < devices]
    return lax.ppermute(across, "row", pairs)


def rest_of(across, far, give_across, devices):
    pieces = [jnp.where(give_across, a, f) for a, f in zip(across, far)]
    return swapped(jnp.concatenate(pieces, axis=0), 1, devices)


def core_summed(give, keep, uppers, devices):
    return halved(keep + swapped(give, 1, devices).astype(jnp.float32), uppers[1])


def chip_summed(give, keep, devices):
    return keep + swapped(give, 2, devices).astype(jnp.float32)


def halved(total, upper):
    half = total.shape[1] // 2
    low, high = total[:, :half], total[:, half:]
    return jnp.where(upper, low, high).astype(jnp.bfloat16), jnp.where(upper, high, low)


def summed(total, uppers, devices):
    last = len(uppers) - 1
    for b in range(2, last):
        give, keep = halved(total, uppers[b])
        total = keep + swapped(give, 2 ** b, devices).astype(jnp.float32)
    own = total.astype(jnp.bfloat16)
    gathered = (own.astype(jnp.float32) + swapped(own, 2 ** last, devices).astype(jnp.float32)).astype(jnp.bfloat16)
    for b in range(last - 1, 0, -1):
        other = swapped(gathered, 2 ** b, devices)
        low = jnp.where(uppers[b], other, gathered)
        high = jnp.where(uppers[b], gathered, other)
        gathered = jnp.concatenate([low, high], axis=1)
    return gathered, swapped(gathered, 1, devices)


def shards(sigma_blocks, first_panel, second_panel, lower_panel, first_diag, second_diag, task_list, task_count):
    barrier = lax.optimization_barrier
    devices = lax.axis_size("row")
    position = lax.axis_index("row").astype(jnp.int32)
    slots, size, width = sigma_blocks.shape[-3:]
    sigma = sigma_blocks.reshape((slots, size, width))
    first = first_panel.reshape((size, width))
    second = second_panel.reshape((size, width))
    where = position.reshape((1,))
    bits = [(position >> b) & 1 for b in range(devices.bit_length() - 1)]
    uppers = [bit == 1 for bit in bits]
    give_across = bits[0] == bits[1]
    where, uppers, give_across, first, second = barrier((where, uppers, give_across, first, second))
    listed = task_list.reshape((slots,))
    count = task_count.reshape((1,))
    one = 2 * size * size * width
    half = size // 2
    narrow = jax.ShapeDtypeStruct((size, width), jnp.bfloat16)
    wide = jax.ShapeDtypeStruct((size, width), jnp.float32)
    scratch = [pltpu.VMEM((size, width), jnp.float32)]

    def parts(k):
        return [jax.ShapeDtypeStruct((k, half, width), t) for t in (jnp.bfloat16, jnp.float32)]

    piece = jax.ShapeDtypeStruct((half, width), jnp.bfloat16)
    pieces = call(split_kernel, [piece] * 2, [first], "h", 1, [pltpu.SemaphoreType.DMA((2,))])
    across = [swapped(part, 2, devices) for part in pieces]
    second_across = swapped(second, 2, devices)
    beside = swapped(first, 1, devices)
    second_beside = swapped(second, 1, devices)
    first_acc, second_acc, turned, sorted_sigma, lower = call(
        near_kernel,
        [wide, wide, jax.ShapeDtypeStruct((2 * size, width), jnp.bfloat16),
         jax.ShapeDtypeStruct((3, size, width), jnp.bfloat16), narrow],
        [where, listed, count, sigma, lower_panel, *pieces, second, beside, second_beside],
        "ssshhvvvvv",
        4 * one,
        [pltpu.VMEM((2, size, width), jnp.bfloat16), pltpu.SemaphoreType.DMA((6,))],
    )
    far = [far_of(part, devices) for part in across]
    second_parts = [second_across[: half // 2], second_across[half // 2 :]]
    second_far = [far_of(second_parts[0], devices, closed=True), far_of(second_parts[1], devices)]
    far, second_across, turned = barrier((far, second_across, turned))
    rest = rest_of(across, far, give_across, devices)
    column_first, column_again, give, keep = call(
        first_kernel,
        [narrow, narrow] + parts(2),
        [where, first_acc, *across, *far, rest, sorted_sigma, turned],
        "svvvvvvvv",
        5 * one,
        scratch,
    )
    give, second_far[0] = barrier((give, second_far[0]))
    give, keep = core_summed(give, keep, uppers, devices)
    total = chip_summed(give, keep, devices)
    second_parts, total = barrier((second_parts, total))
    second_rest = rest_of(second_parts, second_far, give_across, devices)
    (second_acc,) = call(
        across_kernel, [wide], [second_acc, column_again, lower, second_across, sorted_sigma], "vvvvv", 2 * one
    )
    column_second, second_give, second_keep = call(
        second_kernel,
        [narrow] + parts(1),
        [where, second_acc, *second_far, second_rest, sorted_sigma, turned],
        "svvvvvv",
        3 * one,
        scratch,
    )
    second_give, second_keep = core_summed(second_give, second_keep, uppers, devices)
    mine, other = summed(total, uppers, devices)
    second_total = chip_summed(second_give, second_keep, devices)
    second_mine, second_other = summed(second_total, uppers, devices)
    block_first, block_link, base = call(
        link_kernel, [wide] * 3, [where, mine, other, lower, first_diag, second_diag], "svvvvv", 4 * one, scratch
    )
    (block_second,) = call(last_kernel, [wide], [where, second_mine, second_other, base], "svvv", size * width)
    shape = first_panel.shape
    return column_first.reshape(shape), block_first, block_link, column_second.reshape(shape), block_second


def solution(mesh):
    return jax.shard_map(
        shards,
        mesh=mesh,
        in_specs=(
            P("groups", "row", None, None, None),
            P("groups", "row", None, None),
            P("groups", "row", None, None),
            P("groups", None),
            P("groups", None),
            P("groups", None),
            P("groups", "row", None),
            P("groups", "row"),
        ),
        out_specs=(
            P("groups", "row", None, None),
            P("groups", None),
            P("groups", None),
            P("groups", "row", None, None),
            P("groups", None),
        ),
        check_vma=False,
    )
```

```python
import functools

import jax
import jax.numpy as jnp
from jax import lax
from jax.experimental import pallas as pl
from jax.experimental.pallas import tpu as pltpu
from jax.sharding import PartitionSpec as P

VMEM_BYTES = 14 * 1024 * 1024


def call(body, outs, args, spaces, flops, scratch=(), out_space="v"):
    kinds = {"s": pltpu.SMEM, "v": pltpu.VMEM, "h": pltpu.HBM}
    moved = sum(a.size * a.dtype.itemsize for a in args) + sum(o.size * o.dtype.itemsize for o in outs)
    return pl.pallas_call(
        body,
        out_shape=outs,
        in_specs=[pl.BlockSpec(memory_space=kinds[c]) for c in spaces],
        out_specs=[pl.BlockSpec(memory_space=kinds[out_space])] * len(outs),
        scratch_shapes=list(scratch),
        compiler_params=pltpu.CompilerParams(vmem_limit_bytes=VMEM_BYTES),
        cost_estimate=pl.CostEstimate(flops=flops, bytes_accessed=moved, transcendentals=0),
    )(*args)


def dot(a, b):
    return lax.dot_general(a, b, (((1,), (0,)), ((), ())), preferred_element_type=jnp.float32)


def dot_t(a, b):
    return lax.dot_general(a, b, (((0,), (0,)), ((), ())), preferred_element_type=jnp.float32)


def offsets_of(where_ref):
    member = where_ref[0] % 4
    across = jnp.where(member < 2, 2, -2)
    beside = jnp.where(member % 2 == 0, 1, -1)
    return jnp.int32(0), beside, across, -across, -beside


def split_kernel(panel_hbm, low, high, sems):
    half = low.shape[0]
    copies = [
        pltpu.make_async_copy(panel_hbm.at[pl.ds(index * half, half)], target, sems.at[index])
        for index, target in enumerate((low, high))
    ]
    for copy in copies:
        copy.start()
    for copy in copies:
        copy.wait()


def near_kernel(where_ref, list_ref, count_ref, sigma_hbm, lower_hbm, first_0, first_1, second,
                first_beside, second_beside,
                first_acc, second_acc, turned_ref, sigma_ref, lower_ref, lower_turned_ref, near_ref, sems):
    lives = []
    copies = []
    for index, offset in enumerate(offsets_of(where_ref)):
        slot = jnp.int32(0)
        live = jnp.int32(0)
        for s in range(sigma_hbm.shape[0]):
            hit = (list_ref[s] == offset) & (s < count_ref[0])
            slot = jnp.where(hit, s, slot)
            live = jnp.where(hit, 1, live)
        target = near_ref.at[index] if index < 2 else sigma_ref.at[index - 2]
        lives.append((live, target))
        copies.append(pltpu.make_async_copy(sigma_hbm.at[slot], target, sems.at[index]))
    copies.append(pltpu.make_async_copy(lower_hbm, lower_ref, sems.at[5]))
    for copy in copies:
        copy.start()

    def arrived(index):
        copies[index].wait()
        live, target = lives[index]

        @pl.when(live == 0)
        def _():
            target[...] = jnp.zeros(target.shape, target.dtype)

    half = first_0.shape[0]
    size = 2 * half
    turned_ref[:size, :half] = first_0[...].T
    turned_ref[:size, half:] = first_1[...].T
    turned_ref[size:] = second[...].T
    arrived(0)
    first_acc[...] = dot(near_ref[0, :, :half], first_0[...])
    first_acc[...] += dot(near_ref[0, :, half:], first_1[...])
    second_acc[...] = dot(near_ref[0], second[...])
    arrived(1)
    first_acc[...] += dot(near_ref[1], first_beside[...])
    second_acc[...] += dot(near_ref[1], second_beside[...])
    for index in (2, 3, 4):
        arrived(index)
    copies[5].wait()
    lower_turned_ref[...] = lower_ref[...].T


def halves(value, where_ref, scratch_ref, give_ref, keep_ref, index):
    scratch_ref[...] = value
    half = value.shape[0] // 2
    core = where_ref[0] % 2
    keep_ref[index] = scratch_ref[pl.ds(pl.multiple_of(core * half, half), half)]
    give_ref[index] = scratch_ref[pl.ds(pl.multiple_of((1 - core) * half, half), half)].astype(jnp.bfloat16)


def first_kernel(where_ref, acc_in, across_0, across_1, far_0, far_1, rest, sigma_ref, turned_ref,
                 column_ref, again_ref, give_ref, keep_ref, acc_ref):
    half = far_0.shape[0]
    acc_ref[...] = acc_in[...]
    acc_ref[...] += dot(sigma_ref[0, :, :half], across_0[...])
    acc_ref[...] += dot(sigma_ref[0, :, half:], across_1[...])
    acc_ref[...] += dot(sigma_ref[1, :, :half], far_0[...])
    acc_ref[...] += dot(sigma_ref[1, :, half:], far_1[...])
    acc_ref[...] += dot(sigma_ref[2], rest[...])
    column = (-acc_ref[...]).astype(jnp.bfloat16)
    column_ref[...] = column
    again_ref[...] = column
    size = column.shape[0]
    halves(-dot(turned_ref[:size], column), where_ref, acc_ref, give_ref, keep_ref, 0)
    halves(dot(turned_ref[size:], column), where_ref, acc_ref, give_ref, keep_ref, 1)


def across_kernel(acc_in, column_ref, lower_ref, across, sigma_ref, acc_ref):
    acc_ref[...] = acc_in[...] + dot(column_ref[...], lower_ref[...])
    acc_ref[...] += dot(sigma_ref[0], across[...])


def second_kernel(where_ref, acc_in, far, rest, sigma_ref, turned_ref,
                  column_ref, give_ref, keep_ref, acc_ref):
    acc_ref[...] = acc_in[...]
    acc_ref[...] += dot(sigma_ref[1], far[...])
    acc_ref[...] += dot(sigma_ref[2], rest[...])
    column = (-acc_ref[...]).astype(jnp.bfloat16)
    column_ref[...] = column
    size = column.shape[0]
    halves(-dot(turned_ref[size:], column), where_ref, acc_ref, give_ref, keep_ref, 0)


def split(value):
    high = value.astype(jnp.bfloat16)
    low = (value - high.astype(jnp.float32)).astype(jnp.bfloat16)
    return high, low


def place(where_ref, mine_ref, other_ref, index, out_ref):
    half = mine_ref.shape[1]
    core = where_ref[0] % 2
    out_ref[pl.ds(pl.multiple_of(core * half, half), half)] = mine_ref[index].astype(jnp.float32)
    out_ref[pl.ds(pl.multiple_of((1 - core) * half, half), half)] = other_ref[index].astype(jnp.float32)


def final_kernel(where_ref, mine_ref, other_ref, second_mine_ref, second_other_ref, lower_ref, lower_turned_ref,
                 first_diag_ref, second_diag_ref, first_hbm, link_hbm, second_hbm,
                 sum_ref, first_ref, link_ref, second_ref, sems):
    copies = [
        pltpu.make_async_copy(source, target, sems.at[index])
        for index, (source, target) in enumerate(((first_ref, first_hbm), (link_ref, link_hbm), (second_ref, second_hbm)))
    ]
    lower = lower_ref[...]
    turned = lower_turned_ref[...]
    place(where_ref, mine_ref, other_ref, 0, sum_ref)
    block_first = first_diag_ref[...] + sum_ref[...]
    first_ref[...] = block_first
    copies[0].start()
    place(where_ref, mine_ref, other_ref, 1, sum_ref)
    place(where_ref, second_mine_ref, second_other_ref, 0, second_ref)
    high, low = split(block_first)
    link = dot(high, lower) + dot(low, lower) + sum_ref[...].T
    link_ref[...] = -link
    copies[1].start()
    high, low = split(link)
    second_ref[...] += second_diag_ref[...] + dot(turned, high) + dot(turned, low)
    copies[2].start()
    for copy in copies:
        copy.wait()


def swapped(value, bit, devices):
    return lax.ppermute(value, "row", [(i, i ^ bit) for i in range(devices)])


def far_of(across, devices, closed=False):
    hops = [(i, i + 4 if i % 4 < 2 else i - 4) for i in range(devices)]
    pairs = [(a, b if 0 <= b < devices else a ^ 2) for a, b in hops]
    if not closed:
        pairs = [(a, b) for a, b in hops if 0 <= b < devices]
    return lax.ppermute(across, "row", pairs)


def rest_of(across, far, give_across, devices):
    pieces = [jnp.where(give_across, a, f) for a, f in zip(across, far)]
    return swapped(jnp.concatenate(pieces, axis=0), 1, devices)


def core_summed(give, keep, uppers, devices):
    return halved(keep + swapped(give, 1, devices).astype(jnp.float32), uppers[1])


def chip_summed(give, keep, devices):
    return keep + swapped(give, 2, devices).astype(jnp.float32)


def halved(total, upper):
    half = total.shape[1] // 2
    low, high = total[:, :half], total[:, half:]
    return jnp.where(upper, low, high).astype(jnp.bfloat16), jnp.where(upper, high, low)


def summed(total, uppers, devices):
    last = len(uppers) - 1
    for b in range(2, last):
        give, keep = halved(total, uppers[b])
        total = keep + swapped(give, 2 ** b, devices).astype(jnp.float32)
    own = total.astype(jnp.bfloat16)
    gathered = (own.astype(jnp.float32) + swapped(own, 2 ** last, devices).astype(jnp.float32)).astype(jnp.bfloat16)
    for b in range(last - 1, 0, -1):
        other = swapped(gathered, 2 ** b, devices)
        low = jnp.where(uppers[b], other, gathered)
        high = jnp.where(uppers[b], gathered, other)
        gathered = jnp.concatenate([low, high], axis=1)
    return gathered, swapped(gathered, 1, devices)


def shards(sigma_blocks, first_panel, second_panel, lower_panel, first_diag, second_diag, task_list, task_count):
    barrier = lax.optimization_barrier
    devices = lax.axis_size("row")
    position = lax.axis_index("row").astype(jnp.int32)
    slots, size, width = sigma_blocks.shape[-3:]
    sigma = sigma_blocks.reshape((slots, size, width))
    first = first_panel.reshape((size, width))
    second = second_panel.reshape((size, width))
    where = position.reshape((1,))
    bits = [(position >> b) & 1 for b in range(devices.bit_length() - 1)]
    uppers = [bit == 1 for bit in bits]
    give_across = bits[0] == bits[1]
    where, uppers, give_across, first, second = barrier((where, uppers, give_across, first, second))
    listed = task_list.reshape((slots,))
    count = task_count.reshape((1,))
    one = 2 * size * size * width
    half = size // 2
    narrow = jax.ShapeDtypeStruct((size, width), jnp.bfloat16)
    wide = jax.ShapeDtypeStruct((size, width), jnp.float32)
    scratch = [pltpu.VMEM((size, width), jnp.float32)]

    def parts(k):
        return [jax.ShapeDtypeStruct((k, half, width), t) for t in (jnp.bfloat16, jnp.float32)]

    piece = jax.ShapeDtypeStruct((half, width), jnp.bfloat16)
    pieces = call(split_kernel, [piece] * 2, [first], "h", 1, [pltpu.SemaphoreType.DMA((2,))])
    across = [swapped(part, 2, devices) for part in pieces]
    second_across = swapped(second, 2, devices)
    beside = swapped(first, 1, devices)
    second_beside = swapped(second, 1, devices)
    first_acc, second_acc, turned, sorted_sigma, lower, lower_turned = call(
        near_kernel,
        [wide, wide, jax.ShapeDtypeStruct((2 * size, width), jnp.bfloat16),
         jax.ShapeDtypeStruct((3, size, width), jnp.bfloat16), narrow, narrow],
        [where, listed, count, sigma, lower_panel, *pieces, second, beside, second_beside],
        "ssshhvvvvv",
        4 * one,
        [pltpu.VMEM((2, size, width), jnp.bfloat16), pltpu.SemaphoreType.DMA((6,))],
    )
    far = [far_of(part, devices) for part in across]
    second_far = far_of(second_across, devices, closed=True)
    far, second_across, turned = barrier((far, second_across, turned))
    rest = rest_of(across, far, give_across, devices)
    column_first, column_again, give, keep = call(
        first_kernel,
        [narrow, narrow] + parts(2),
        [where, first_acc, *across, *far, rest, sorted_sigma, turned],
        "svvvvvvvv",
        5 * one,
        scratch,
    )
    give, second_across = barrier((give, second_across))
    give, keep = core_summed(give, keep, uppers, devices)
    second_rest = rest_of([second_across], [second_far], give_across, devices)
    total = chip_summed(give, keep, devices)
    (second_acc,) = call(
        across_kernel, [wide], [second_acc, column_again, lower, second_across, sorted_sigma], "vvvvv", 2 * one
    )
    column_second, second_give, second_keep = call(
        second_kernel,
        [narrow] + parts(1),
        [where, second_acc, second_far, second_rest, sorted_sigma, turned],
        "svvvvv",
        3 * one,
        scratch,
    )
    second_give, total = barrier((second_give, total))
    second_give, second_keep = core_summed(second_give, second_keep, uppers, devices)
    mine, other = summed(total, uppers, devices)
    second_total = chip_summed(second_give, second_keep, devices)
    second_mine, second_other = summed(second_total, uppers, devices)
    block_first, block_link, block_second = call(
        final_kernel,
        [wide] * 3,
        [where, mine, other, second_mine, second_other, lower, lower_turned, first_diag, second_diag],
        "svvvvvvvv",
        4 * one,
        scratch * 4 + [pltpu.SemaphoreType.DMA((3,))],
        "h",
    )
    shape = first_panel.shape
    return column_first.reshape(shape), block_first, block_link, column_second.reshape(shape), block_second


def solution(mesh):
    return jax.shard_map(
        shards,
        mesh=mesh,
        in_specs=(
            P("groups", "row", None, None, None),
            P("groups", "row", None, None),
            P("groups", "row", None, None),
            P("groups", None),
            P("groups", None),
            P("groups", None),
            P("groups", "row", None),
            P("groups", "row"),
        ),
        out_specs=(
            P("groups", "row", None, None),
            P("groups", None),
            P("groups", None),
            P("groups", "row", None, None),
            P("groups", None),
        ),
        check_vma=False,
    )
```

```python
import functools

import jax
import jax.numpy as jnp
from jax import lax
from jax.experimental import pallas as pl
from jax.experimental.pallas import tpu as pltpu
from jax.sharding import PartitionSpec as P

VMEM_BYTES = 14 * 1024 * 1024


def call(body, outs, args, spaces, flops, scratch=(), out_space="v"):
    kinds = {"s": pltpu.SMEM, "v": pltpu.VMEM, "h": pltpu.HBM}
    moved = sum(a.size * a.dtype.itemsize for a in args) + sum(o.size * o.dtype.itemsize for o in outs)
    return pl.pallas_call(
        body,
        out_shape=outs,
        in_specs=[pl.BlockSpec(memory_space=kinds[c]) for c in spaces],
        out_specs=[pl.BlockSpec(memory_space=kinds[out_space])] * len(outs),
        scratch_shapes=list(scratch),
        compiler_params=pltpu.CompilerParams(vmem_limit_bytes=VMEM_BYTES),
        cost_estimate=pl.CostEstimate(flops=flops, bytes_accessed=moved, transcendentals=0),
    )(*args)


def dot(a, b):
    return lax.dot_general(a, b, (((1,), (0,)), ((), ())), preferred_element_type=jnp.float32)


def dot_t(a, b):
    return lax.dot_general(a, b, (((0,), (0,)), ((), ())), preferred_element_type=jnp.float32)


def offsets_of(where_ref):
    member = where_ref[0] % 4
    across = jnp.where(member < 2, 2, -2)
    beside = jnp.where(member % 2 == 0, 1, -1)
    return jnp.int32(0), beside, across, -across, -beside


def split_kernel(panel_hbm, low, high, sems):
    half = low.shape[0]
    copies = [
        pltpu.make_async_copy(panel_hbm.at[pl.ds(index * half, half)], target, sems.at[index])
        for index, target in enumerate((low, high))
    ]
    for copy in copies:
        copy.start()
    for copy in copies:
        copy.wait()


def near_kernel(where_ref, list_ref, count_ref, sigma_hbm, lower_hbm, first_0, first_1, second,
                first_beside, second_beside,
                first_acc, second_acc, turned_ref, sigma_ref, lower_ref, lower_turned_ref, near_ref, sems):
    lives = []
    copies = []
    for index, offset in enumerate(offsets_of(where_ref)):
        slot = jnp.int32(0)
        live = jnp.int32(0)
        for s in range(sigma_hbm.shape[0]):
            hit = (list_ref[s] == offset) & (s < count_ref[0])
            slot = jnp.where(hit, s, slot)
            live = jnp.where(hit, 1, live)
        target = near_ref.at[index] if index < 2 else sigma_ref.at[index - 2]
        lives.append((live, target))
        copies.append(pltpu.make_async_copy(sigma_hbm.at[slot], target, sems.at[index]))
    copies.append(pltpu.make_async_copy(lower_hbm, lower_ref, sems.at[5]))
    for copy in copies:
        copy.start()

    def arrived(index):
        copies[index].wait()
        live, target = lives[index]

        @pl.when(live == 0)
        def _():
            target[...] = jnp.zeros(target.shape, target.dtype)

    half = first_0.shape[0]
    size = 2 * half
    turned_ref[:size, :half] = first_0[...].T
    turned_ref[:size, half:] = first_1[...].T
    turned_ref[size:] = second[...].T
    arrived(0)
    first_acc[...] = dot(near_ref[0, :, :half], first_0[...])
    first_acc[...] += dot(near_ref[0, :, half:], first_1[...])
    second_acc[...] = dot(near_ref[0], second[...])
    arrived(1)
    first_acc[...] += dot(near_ref[1], first_beside[...])
    second_acc[...] += dot(near_ref[1], second_beside[...])
    for index in (2, 3, 4):
        arrived(index)
    copies[5].wait()
    lower_turned_ref[...] = lower_ref[...].T


def halves(value, where_ref, scratch_ref, give_ref, keep_ref, index):
    scratch_ref[...] = value
    half = value.shape[0] // 2
    core = where_ref[0] % 2
    keep_ref[index] = scratch_ref[pl.ds(pl.multiple_of(core * half, half), half)]
    give_ref[index] = scratch_ref[pl.ds(pl.multiple_of((1 - core) * half, half), half)].astype(jnp.bfloat16)


def first_kernel(where_ref, acc_in, across_0, across_1, far_0, far_1, rest, sigma_ref, turned_ref,
                 column_ref, again_ref, give_ref, keep_ref, acc_ref):
    half = far_0.shape[0]
    acc_ref[...] = acc_in[...]
    acc_ref[...] += dot(sigma_ref[0, :, :half], across_0[...])
    acc_ref[...] += dot(sigma_ref[0, :, half:], across_1[...])
    acc_ref[...] += dot(sigma_ref[1, :, :half], far_0[...])
    acc_ref[...] += dot(sigma_ref[1, :, half:], far_1[...])
    acc_ref[...] += dot(sigma_ref[2], rest[...])
    column = (-acc_ref[...]).astype(jnp.bfloat16)
    column_ref[...] = column
    again_ref[...] = column
    size = column.shape[0]
    halves(-dot(turned_ref[:size], column), where_ref, acc_ref, give_ref, keep_ref, 0)
    halves(dot(turned_ref[size:], column), where_ref, acc_ref, give_ref, keep_ref, 1)


def across_kernel(acc_in, column_ref, lower_ref, across, sigma_ref, acc_ref):
    acc_ref[...] = acc_in[...] + dot(column_ref[...], lower_ref[...])
    acc_ref[...] += dot(sigma_ref[0], across[...])


def second_kernel(where_ref, acc_in, far, rest, sigma_ref, turned_ref,
                  column_ref, give_ref, keep_ref, acc_ref):
    acc_ref[...] = acc_in[...]
    acc_ref[...] += dot(sigma_ref[1], far[...])
    acc_ref[...] += dot(sigma_ref[2], rest[...])
    column = (-acc_ref[...]).astype(jnp.bfloat16)
    column_ref[...] = column
    size = column.shape[0]
    halves(-dot(turned_ref[size:], column), where_ref, acc_ref, give_ref, keep_ref, 0)


def split(value):
    high = value.astype(jnp.bfloat16)
    low = (value - high.astype(jnp.float32)).astype(jnp.bfloat16)
    return high, low


def place(where_ref, mine_ref, other_ref, index, out_ref):
    half = mine_ref.shape[1]
    core = where_ref[0] % 2
    out_ref[pl.ds(pl.multiple_of(core * half, half), half)] = mine_ref[index].astype(jnp.float32)
    out_ref[pl.ds(pl.multiple_of((1 - core) * half, half), half)] = other_ref[index].astype(jnp.float32)


def final_kernel(where_ref, mine_ref, other_ref, second_mine_ref, second_other_ref, lower_ref, lower_turned_ref,
                 first_diag_ref, second_diag_ref, first_hbm, link_hbm, second_hbm,
                 sum_ref, first_ref, link_ref, second_ref, sems):
    copies = [
        pltpu.make_async_copy(source, target, sems.at[index])
        for index, (source, target) in enumerate(((first_ref, first_hbm), (link_ref, link_hbm), (second_ref, second_hbm)))
    ]
    lower = lower_ref[...]
    turned = lower_turned_ref[...]
    place(where_ref, mine_ref, other_ref, 0, sum_ref)
    block_first = first_diag_ref[...] + sum_ref[...]
    first_ref[...] = block_first
    copies[0].start()
    place(where_ref, mine_ref, other_ref, 1, sum_ref)
    place(where_ref, second_mine_ref, second_other_ref, 0, second_ref)
    high, low = split(block_first)
    link = dot(high, lower) + dot(low, lower) + sum_ref[...].T
    link_ref[...] = -link
    copies[1].start()
    high, low = split(link)
    second_ref[...] += second_diag_ref[...] + dot(turned, high) + dot(turned, low)
    copies[2].start()
    for copy in copies:
        copy.wait()


def swapped(value, bit, devices):
    return lax.ppermute(value, "row", [(i, i ^ bit) for i in range(devices)])


def far_of(across, devices, closed=False):
    hops = [(i, i + 4 if i % 4 < 2 else i - 4) for i in range(devices)]
    pairs = [(a, b if 0 <= b < devices else a ^ 2) for a, b in hops]
    if not closed:
        pairs = [(a, b) for a, b in hops if 0 <= b < devices]
    return lax.ppermute(across, "row", pairs)


def rest_of(across, far, give_across, devices):
    pieces = [jnp.where(give_across, a, f) for a, f in zip(across, far)]
    return swapped(jnp.concatenate(pieces, axis=0), 1, devices)


def core_summed(give, keep, devices):
    return keep + swapped(give, 1, devices).astype(jnp.float32)


def step_summed(total, b, uppers, devices):
    give, keep = halved(total, uppers[b])
    return keep + swapped(give, 2 ** b, devices).astype(jnp.float32)


def halved(total, upper):
    half = total.shape[1] // 2
    low, high = total[:, :half], total[:, half:]
    return jnp.where(upper, low, high).astype(jnp.bfloat16), jnp.where(upper, high, low)


def summed(total, order, uppers, devices):
    halve, swap, double = order
    for b in halve:
        total = step_summed(total, b, uppers, devices)
    own = total.astype(jnp.bfloat16)
    gathered = (own.astype(jnp.float32) + swapped(own, 2 ** swap, devices).astype(jnp.float32)).astype(jnp.bfloat16)
    for b in double:
        other = swapped(gathered, 2 ** b, devices)
        low = jnp.where(uppers[b], other, gathered)
        high = jnp.where(uppers[b], gathered, other)
        gathered = jnp.concatenate([low, high], axis=1)
    return gathered, swapped(gathered, 1, devices)


def shards(sigma_blocks, first_panel, second_panel, lower_panel, first_diag, second_diag, task_list, task_count):
    barrier = lax.optimization_barrier
    devices = lax.axis_size("row")
    position = lax.axis_index("row").astype(jnp.int32)
    slots, size, width = sigma_blocks.shape[-3:]
    sigma = sigma_blocks.reshape((slots, size, width))
    first = first_panel.reshape((size, width))
    second = second_panel.reshape((size, width))
    where = position.reshape((1,))
    bits = [(position >> b) & 1 for b in range(devices.bit_length() - 1)]
    uppers = [bit == 1 for bit in bits]
    give_across = bits[0] == bits[1]
    where, uppers, give_across, first, second = barrier((where, uppers, give_across, first, second))
    listed = task_list.reshape((slots,))
    count = task_count.reshape((1,))
    one = 2 * size * size * width
    half = size // 2
    narrow = jax.ShapeDtypeStruct((size, width), jnp.bfloat16)
    wide = jax.ShapeDtypeStruct((size, width), jnp.float32)
    scratch = [pltpu.VMEM((size, width), jnp.float32)]

    def parts(k):
        return [jax.ShapeDtypeStruct((k, half, width), t) for t in (jnp.bfloat16, jnp.float32)]

    piece = jax.ShapeDtypeStruct((half, width), jnp.bfloat16)
    pieces = call(split_kernel, [piece] * 2, [first], "h", 1, [pltpu.SemaphoreType.DMA((2,))])
    across = [swapped(part, 2, devices) for part in pieces]
    second_across = swapped(second, 2, devices)
    beside = swapped(first, 1, devices)
    second_beside = swapped(second, 1, devices)
    first_acc, second_acc, turned, sorted_sigma, lower, lower_turned = call(
        near_kernel,
        [wide, wide, jax.ShapeDtypeStruct((2 * size, width), jnp.bfloat16),
         jax.ShapeDtypeStruct((3, size, width), jnp.bfloat16), narrow, narrow],
        [where, listed, count, sigma, lower_panel, *pieces, second, beside, second_beside],
        "ssshhvvvvv",
        4 * one,
        [pltpu.VMEM((2, size, width), jnp.bfloat16), pltpu.SemaphoreType.DMA((6,))],
    )
    far = [far_of(part, devices) for part in across]
    second_far = far_of(second_across, devices, closed=True)
    far, second_across, turned = barrier((far, second_across, turned))
    rest = rest_of(across, far, give_across, devices)
    column_first, column_again, give, keep = call(
        first_kernel,
        [narrow, narrow] + parts(2),
        [where, first_acc, *across, *far, rest, sorted_sigma, turned],
        "svvvvvvvv",
        5 * one,
        scratch,
    )
    give, second_across = barrier((give, second_across))
    total = core_summed(give, keep, devices)
    second_rest = rest_of([second_across], [second_far], give_across, devices)
    total = step_summed(total, 1, uppers, devices)
    (second_acc,) = call(
        across_kernel, [wide], [second_acc, column_again, lower, second_across, sorted_sigma], "vvvvv", 2 * one
    )
    column_second, second_give, second_keep = call(
        second_kernel,
        [narrow] + parts(1),
        [where, second_acc, second_far, second_rest, sorted_sigma, turned],
        "svvvvv",
        3 * one,
        scratch,
    )
    last = len(uppers) - 1
    second_total = core_summed(second_give, second_keep, devices)
    mine, other = summed(total, (range(2, last), last, range(last - 1, 0, -1)), uppers, devices)
    second_mine, second_other = summed(
        second_total, (range(2, last + 1), 1, range(last, 1, -1)), uppers, devices
    )
    block_first, block_link, block_second = call(
        final_kernel,
        [wide] * 3,
        [where, mine, other, second_mine, second_other, lower, lower_turned, first_diag, second_diag],
        "svvvvvvvv",
        4 * one,
        scratch * 4 + [pltpu.SemaphoreType.DMA((3,))],
        "h",
    )
    shape = first_panel.shape
    return column_first.reshape(shape), block_first, block_link, column_second.reshape(shape), block_second


def solution(mesh):
    return jax.shard_map(
        shards,
        mesh=mesh,
        in_specs=(
            P("groups", "row", None, None, None),
            P("groups", "row", None, None),
            P("groups", "row", None, None),
            P("groups", None),
            P("groups", None),
            P("groups", None),
            P("groups", "row", None),
            P("groups", "row"),
        ),
        out_specs=(
            P("groups", "row", None, None),
            P("groups", None),
            P("groups", None),
            P("groups", "row", None, None),
            P("groups", None),
        ),
        check_vma=False,
    )
```

```python
import functools

import jax
import jax.numpy as jnp
from jax import lax
from jax.experimental import pallas as pl
from jax.experimental.pallas import tpu as pltpu
from jax.sharding import PartitionSpec as P

VMEM_BYTES = 14 * 1024 * 1024


def call(body, outs, args, spaces, flops, scratch=(), out_space="v"):
    kinds = {"s": pltpu.SMEM, "v": pltpu.VMEM, "h": pltpu.HBM}
    moved = sum(a.size * a.dtype.itemsize for a in args) + sum(o.size * o.dtype.itemsize for o in outs)
    return pl.pallas_call(
        body,
        out_shape=outs,
        in_specs=[pl.BlockSpec(memory_space=kinds[c]) for c in spaces],
        out_specs=[pl.BlockSpec(memory_space=kinds[out_space])] * len(outs),
        scratch_shapes=list(scratch),
        compiler_params=pltpu.CompilerParams(vmem_limit_bytes=VMEM_BYTES),
        cost_estimate=pl.CostEstimate(flops=flops, bytes_accessed=moved, transcendentals=0),
    )(*args)


def dot(a, b):
    return lax.dot_general(a, b, (((1,), (0,)), ((), ())), preferred_element_type=jnp.float32)


def dot_t(a, b):
    return lax.dot_general(a, b, (((0,), (0,)), ((), ())), preferred_element_type=jnp.float32)


def offsets_of(where_ref):
    member = where_ref[0] % 4
    across = jnp.where(member < 2, 2, -2)
    beside = jnp.where(member % 2 == 0, 1, -1)
    return jnp.int32(0), beside, across, -across, -beside


def split_kernel(panel_hbm, low, high, sems):
    half = low.shape[0]
    copies = [
        pltpu.make_async_copy(panel_hbm.at[pl.ds(index * half, half)], target, sems.at[index])
        for index, target in enumerate((low, high))
    ]
    for copy in copies:
        copy.start()
    for copy in copies:
        copy.wait()


def near_kernel(where_ref, list_ref, count_ref, sigma_hbm, lower_hbm, first_0, first_1, second,
                first_beside, second_beside,
                first_acc, second_acc, turned_ref, sigma_ref, lower_ref, lower_turned_ref, near_ref, sems):
    lives = []
    copies = []
    for index, offset in enumerate(offsets_of(where_ref)):
        slot = jnp.int32(0)
        live = jnp.int32(0)
        for s in range(sigma_hbm.shape[0]):
            hit = (list_ref[s] == offset) & (s < count_ref[0])
            slot = jnp.where(hit, s, slot)
            live = jnp.where(hit, 1, live)
        target = near_ref.at[index] if index < 2 else sigma_ref.at[index - 2]
        lives.append((live, target))
        copies.append(pltpu.make_async_copy(sigma_hbm.at[slot], target, sems.at[index]))
    copies.append(pltpu.make_async_copy(lower_hbm, lower_ref, sems.at[5]))
    for copy in copies:
        copy.start()

    def arrived(index):
        copies[index].wait()
        live, target = lives[index]

        @pl.when(live == 0)
        def _():
            target[...] = jnp.zeros(target.shape, target.dtype)

    half = first_0.shape[0]
    size = 2 * half
    turned_ref[:size, :half] = first_0[...].T
    turned_ref[:size, half:] = first_1[...].T
    turned_ref[size:] = second[...].T
    arrived(0)
    first_acc[...] = dot(near_ref[0, :, :half], first_0[...])
    first_acc[...] += dot(near_ref[0, :, half:], first_1[...])
    second_acc[...] = dot(near_ref[0], second[...])
    arrived(1)
    first_acc[...] += dot(near_ref[1], first_beside[...])
    second_acc[...] += dot(near_ref[1], second_beside[...])
    for index in (2, 3, 4):
        arrived(index)
    copies[5].wait()
    lower_turned_ref[...] = lower_ref[...].T


def halves(value, where_ref, scratch_ref, give_ref, keep_ref, index):
    scratch_ref[...] = value
    half = value.shape[0] // 2
    core = where_ref[0] % 2
    keep_ref[index] = scratch_ref[pl.ds(pl.multiple_of(core * half, half), half)]
    give_ref[index] = scratch_ref[pl.ds(pl.multiple_of((1 - core) * half, half), half)].astype(jnp.bfloat16)


def first_kernel(where_ref, acc_in, across_0, across_1, far_0, far_1, rest, sigma_ref, turned_ref,
                 column_ref, again_ref, give_ref, keep_ref, acc_ref):
    half = far_0.shape[0]
    acc_ref[...] = acc_in[...]
    acc_ref[...] += dot(sigma_ref[0, :, :half], across_0[...])
    acc_ref[...] += dot(sigma_ref[0, :, half:], across_1[...])
    acc_ref[...] += dot(sigma_ref[1, :, :half], far_0[...])
    acc_ref[...] += dot(sigma_ref[1, :, half:], far_1[...])
    acc_ref[...] += dot(sigma_ref[2], rest[...])
    column = (-acc_ref[...]).astype(jnp.bfloat16)
    column_ref[...] = column
    again_ref[...] = column
    size = column.shape[0]
    halves(-dot(turned_ref[:size], column), where_ref, acc_ref, give_ref, keep_ref, 0)
    halves(dot(turned_ref[size:], column), where_ref, acc_ref, give_ref, keep_ref, 1)


def across_kernel(acc_in, column_ref, lower_ref, across, sigma_ref, acc_ref):
    acc_ref[...] = acc_in[...] + dot(column_ref[...], lower_ref[...])
    acc_ref[...] += dot(sigma_ref[0], across[...])


def second_kernel(where_ref, acc_in, far, rest, sigma_ref, turned_ref,
                  column_ref, give_ref, keep_ref, acc_ref):
    acc_ref[...] = acc_in[...]
    acc_ref[...] += dot(sigma_ref[1], far[...])
    acc_ref[...] += dot(sigma_ref[2], rest[...])
    column = (-acc_ref[...]).astype(jnp.bfloat16)
    column_ref[...] = column
    size = column.shape[0]
    halves(-dot(turned_ref[size:], column), where_ref, acc_ref, give_ref, keep_ref, 0)


def split(value):
    high = value.astype(jnp.bfloat16)
    low = (value - high.astype(jnp.float32)).astype(jnp.bfloat16)
    return high, low


def place(where_ref, mine_ref, other_ref, index, out_ref):
    half = mine_ref.shape[1]
    core = where_ref[0] % 2
    out_ref[pl.ds(pl.multiple_of(core * half, half), half)] = mine_ref[index].astype(jnp.float32)
    out_ref[pl.ds(pl.multiple_of((1 - core) * half, half), half)] = other_ref[index].astype(jnp.float32)


def final_kernel(where_ref, mine_ref, other_ref, second_mine_ref, second_other_ref, lower_ref, lower_turned_ref,
                 first_diag_ref, second_diag_ref, first_hbm, link_hbm, second_hbm,
                 sum_ref, first_ref, link_ref, second_ref, sems):
    copies = [
        pltpu.make_async_copy(source, target, sems.at[index])
        for index, (source, target) in enumerate(((first_ref, first_hbm), (link_ref, link_hbm), (second_ref, second_hbm)))
    ]
    lower = lower_ref[...]
    turned = lower_turned_ref[...]
    place(where_ref, mine_ref, other_ref, 0, sum_ref)
    block_first = first_diag_ref[...] + sum_ref[...]
    first_ref[...] = block_first
    copies[0].start()
    place(where_ref, mine_ref, other_ref, 1, sum_ref)
    place(where_ref, second_mine_ref, second_other_ref, 0, second_ref)
    high, low = split(block_first)
    link = dot(high, lower) + dot(low, lower) + sum_ref[...].T
    link_ref[...] = -link
    copies[1].start()
    high, low = split(link)
    second_ref[...] += second_diag_ref[...] + dot(turned, high) + dot(turned, low)
    copies[2].start()
    for copy in copies:
        copy.wait()


def swapped(value, bit, devices):
    return lax.ppermute(value, "row", [(i, i ^ bit) for i in range(devices)])


def far_of(across, devices, closed=False):
    hops = [(i, i + 4 if i % 4 < 2 else i - 4) for i in range(devices)]
    pairs = [(a, b if 0 <= b < devices else a ^ 2) for a, b in hops]
    if not closed:
        pairs = [(a, b) for a, b in hops if 0 <= b < devices]
    return lax.ppermute(across, "row", pairs)


def rest_of(across, far, give_across, devices):
    pieces = [jnp.where(give_across, a, f) for a, f in zip(across, far)]
    return swapped(jnp.concatenate(pieces, axis=0), 1, devices)


def core_summed(give, keep, devices):
    return keep + swapped(give, 1, devices).astype(jnp.float32)


def step_summed(total, b, uppers, devices):
    give, keep = halved(total, uppers[b])
    return keep + swapped(give, 2 ** b, devices).astype(jnp.float32)


def halved(total, upper):
    half = total.shape[1] // 2
    low, high = total[:, :half], total[:, half:]
    return jnp.where(upper, low, high).astype(jnp.bfloat16), jnp.where(upper, high, low)


def summed(total, order, uppers, devices):
    halve, swap, double = order
    for b in halve:
        total = step_summed(total, b, uppers, devices)
    own = total.astype(jnp.bfloat16)
    gathered = (own.astype(jnp.float32) + swapped(own, 2 ** swap, devices).astype(jnp.float32)).astype(jnp.bfloat16)
    for b in double:
        other = swapped(gathered, 2 ** b, devices)
        low = jnp.where(uppers[b], other, gathered)
        high = jnp.where(uppers[b], gathered, other)
        gathered = jnp.concatenate([low, high], axis=1)
    return gathered, swapped(gathered, 1, devices)


def shards(sigma_blocks, first_panel, second_panel, lower_panel, first_diag, second_diag, task_list, task_count):
    barrier = lax.optimization_barrier
    devices = lax.axis_size("row")
    position = lax.axis_index("row").astype(jnp.int32)
    slots, size, width = sigma_blocks.shape[-3:]
    sigma = sigma_blocks.reshape((slots, size, width))
    first = first_panel.reshape((size, width))
    second = second_panel.reshape((size, width))
    where = position.reshape((1,))
    bits = [(position >> b) & 1 for b in range(devices.bit_length() - 1)]
    uppers = [bit == 1 for bit in bits]
    give_across = bits[0] == bits[1]
    where, uppers, give_across, first, second = barrier((where, uppers, give_across, first, second))
    listed = task_list.reshape((slots,))
    count = task_count.reshape((1,))
    one = 2 * size * size * width
    half = size // 2
    narrow = jax.ShapeDtypeStruct((size, width), jnp.bfloat16)
    wide = jax.ShapeDtypeStruct((size, width), jnp.float32)
    scratch = [pltpu.VMEM((size, width), jnp.float32)]

    def parts(k):
        return [jax.ShapeDtypeStruct((k, half, width), t) for t in (jnp.bfloat16, jnp.float32)]

    piece = jax.ShapeDtypeStruct((half, width), jnp.bfloat16)
    pieces = call(split_kernel, [piece] * 2, [first], "h", 1, [pltpu.SemaphoreType.DMA((2,))])
    across = [swapped(part, 2, devices) for part in pieces]
    second_across = swapped(second, 2, devices)
    beside = swapped(first, 1, devices)
    second_beside = swapped(second, 1, devices)
    first_acc, second_acc, turned, sorted_sigma, lower, lower_turned = call(
        near_kernel,
        [wide, wide, jax.ShapeDtypeStruct((2 * size, width), jnp.bfloat16),
         jax.ShapeDtypeStruct((3, size, width), jnp.bfloat16), narrow, narrow],
        [where, listed, count, sigma, lower_panel, *pieces, second, beside, second_beside],
        "ssshhvvvvv",
        4 * one,
        [pltpu.VMEM((2, size, width), jnp.bfloat16), pltpu.SemaphoreType.DMA((6,))],
    )
    far = [far_of(part, devices) for part in across]
    second_far = far_of(second_across, devices, closed=True)
    far, second_across, turned = barrier((far, second_across, turned))
    rest = rest_of(across, far, give_across, devices)
    column_first, column_again, give, keep = call(
        first_kernel,
        [narrow, narrow] + parts(2),
        [where, first_acc, *across, *far, rest, sorted_sigma, turned],
        "svvvvvvvv",
        5 * one,
        scratch,
    )
    give, second_across = barrier((give, second_across))
    total = core_summed(give, keep, devices)
    second_rest = rest_of([second_across], [second_far], give_across, devices)
    total = step_summed(total, 1, uppers, devices)
    (second_acc,) = call(
        across_kernel, [wide], [second_acc, column_again, lower, second_across, sorted_sigma], "vvvvv", 2 * one
    )
    column_second, second_give, second_keep = call(
        second_kernel,
        [narrow] + parts(1),
        [where, second_acc, second_far, second_rest, sorted_sigma, turned],
        "svvvvv",
        3 * one,
        scratch,
    )
    last = len(uppers) - 1
    second_total = core_summed(second_give, second_keep, devices)
    halve = [1, *range(2, last)]
    second_halve = [2, 1, *range(3, last)]
    mine, other = summed(total, (halve[1:], last, halve[::-1]), uppers, devices)
    second_mine, second_other = summed(second_total, (second_halve, last, second_halve[::-1]), uppers, devices)
    block_first, block_link, block_second = call(
        final_kernel,
        [wide] * 3,
        [where, mine, other, second_mine, second_other, lower, lower_turned, first_diag, second_diag],
        "svvvvvvvv",
        4 * one,
        scratch * 4 + [pltpu.SemaphoreType.DMA((3,))],
        "h",
    )
    shape = first_panel.shape
    return column_first.reshape(shape), block_first, block_link, column_second.reshape(shape), block_second


def solution(mesh):
    return jax.shard_map(
        shards,
        mesh=mesh,
        in_specs=(
            P("groups", "row", None, None, None),
            P("groups", "row", None, None),
            P("groups", "row", None, None),
            P("groups", None),
            P("groups", None),
            P("groups", None),
            P("groups", "row", None),
            P("groups", "row"),
        ),
        out_specs=(
            P("groups", "row", None, None),
            P("groups", None),
            P("groups", None),
            P("groups", "row", None, None),
            P("groups", None),
        ),
        check_vma=False,
    )
```

```python
import functools

import jax
import jax.numpy as jnp
from jax import lax
from jax.experimental import pallas as pl
from jax.experimental.pallas import tpu as pltpu
from jax.sharding import PartitionSpec as P

VMEM_BYTES = 14 * 1024 * 1024


def call(body, outs, args, spaces, flops, scratch=(), out_spaces=None):
    kinds = {"s": pltpu.SMEM, "v": pltpu.VMEM, "h": pltpu.HBM}
    moved = sum(a.size * a.dtype.itemsize for a in args) + sum(o.size * o.dtype.itemsize for o in outs)
    return pl.pallas_call(
        body,
        out_shape=outs,
        in_specs=[pl.BlockSpec(memory_space=kinds[c]) for c in spaces],
        out_specs=[pl.BlockSpec(memory_space=kinds[c]) for c in out_spaces or "v" * len(outs)],
        scratch_shapes=list(scratch),
        compiler_params=pltpu.CompilerParams(vmem_limit_bytes=VMEM_BYTES),
        cost_estimate=pl.CostEstimate(flops=flops, bytes_accessed=moved, transcendentals=0),
    )(*args)


def dot(a, b):
    return lax.dot_general(a, b, (((1,), (0,)), ((), ())), preferred_element_type=jnp.float32)


def dot_t(a, b):
    return lax.dot_general(a, b, (((0,), (0,)), ((), ())), preferred_element_type=jnp.float32)


def offsets_of(where_ref):
    member = where_ref[0] % 4
    across = jnp.where(member < 2, 2, -2)
    beside = jnp.where(member % 2 == 0, 1, -1)
    return jnp.int32(0), beside, across, -across, -beside


def split_kernel(panel_hbm, low, high, sems):
    half = low.shape[0]
    copies = [
        pltpu.make_async_copy(panel_hbm.at[pl.ds(index * half, half)], target, sems.at[index])
        for index, target in enumerate((low, high))
    ]
    for copy in copies:
        copy.start()
    for copy in copies:
        copy.wait()


def near_kernel(where_ref, list_ref, count_ref, sigma_hbm, lower_hbm, first_0, first_1, second,
                first_beside, second_beside,
                first_acc, second_acc, turned_ref, sigma_ref, lower_ref, lower_turned_ref, near_ref, sems):
    lives = []
    copies = []
    for index, offset in enumerate(offsets_of(where_ref)):
        slot = jnp.int32(0)
        live = jnp.int32(0)
        for s in range(sigma_hbm.shape[0]):
            hit = (list_ref[s] == offset) & (s < count_ref[0])
            slot = jnp.where(hit, s, slot)
            live = jnp.where(hit, 1, live)
        target = near_ref.at[index] if index < 2 else sigma_ref.at[index - 2]
        lives.append((live, target))
        copies.append(pltpu.make_async_copy(sigma_hbm.at[slot], target, sems.at[index]))
    copies.append(pltpu.make_async_copy(lower_hbm, lower_ref, sems.at[5]))
    for copy in copies:
        copy.start()

    def arrived(index):
        copies[index].wait()
        live, target = lives[index]

        @pl.when(live == 0)
        def _():
            target[...] = jnp.zeros(target.shape, target.dtype)

    half = first_0.shape[0]
    size = 2 * half
    turned_ref[:size, :half] = first_0[...].T
    turned_ref[:size, half:] = first_1[...].T
    turned_ref[size:] = second[...].T
    arrived(0)
    first_acc[...] = dot(near_ref[0, :, :half], first_0[...])
    first_acc[...] += dot(near_ref[0, :, half:], first_1[...])
    second_acc[...] = dot(near_ref[0], second[...])
    arrived(1)
    first_acc[...] += dot(near_ref[1], first_beside[...])
    second_acc[...] += dot(near_ref[1], second_beside[...])
    for index in (2, 3, 4):
        arrived(index)
    copies[5].wait()
    lower_turned_ref[...] = lower_ref[...].T


def halves(value, where_ref, scratch_ref, give_ref, keep_ref, index):
    scratch_ref[...] = value
    half = value.shape[0] // 2
    core = where_ref[0] % 2
    keep_ref[index] = scratch_ref[pl.ds(pl.multiple_of(core * half, half), half)]
    give_ref[index] = scratch_ref[pl.ds(pl.multiple_of((1 - core) * half, half), half)].astype(jnp.bfloat16)


def first_kernel(where_ref, acc_in, across_0, across_1, far_0, far_1, rest, sigma_ref, turned_ref,
                 column_ref, again_ref, give_ref, keep_ref, acc_ref):
    half = far_0.shape[0]
    acc_ref[...] = acc_in[...]
    acc_ref[...] += dot(sigma_ref[0, :, :half], across_0[...])
    acc_ref[...] += dot(sigma_ref[0, :, half:], across_1[...])
    acc_ref[...] += dot(sigma_ref[1, :, :half], far_0[...])
    acc_ref[...] += dot(sigma_ref[1, :, half:], far_1[...])
    acc_ref[...] += dot(sigma_ref[2], rest[...])
    column = (-acc_ref[...]).astype(jnp.bfloat16)
    column_ref[...] = column
    again_ref[...] = column
    size = column.shape[0]
    halves(-dot(turned_ref[:size], column), where_ref, acc_ref, give_ref, keep_ref, 0)
    halves(dot(turned_ref[size:], column), where_ref, acc_ref, give_ref, keep_ref, 1)


def across_kernel(acc_in, column_ref, lower_ref, across, sigma_ref, acc_ref):
    acc_ref[...] = acc_in[...] + dot(column_ref[...], lower_ref[...])
    acc_ref[...] += dot(sigma_ref[0], across[...])


def second_kernel(where_ref, acc_in, far, rest, sigma_ref, turned_ref,
                  column_ref, give_ref, keep_ref, acc_ref):
    acc_ref[...] = acc_in[...]
    acc_ref[...] += dot(sigma_ref[1], far[...])
    acc_ref[...] += dot(sigma_ref[2], rest[...])
    column = (-acc_ref[...]).astype(jnp.bfloat16)
    column_ref[...] = column
    size = column.shape[0]
    halves(-dot(turned_ref[size:], column), where_ref, acc_ref, give_ref, keep_ref, 0)


def split(value):
    high = value.astype(jnp.bfloat16)
    low = (value - high.astype(jnp.float32)).astype(jnp.bfloat16)
    return high, low


def place(where_ref, mine_ref, other_ref, index, out_ref):
    half = mine_ref.shape[1]
    core = where_ref[0] % 2
    out_ref[pl.ds(pl.multiple_of(core * half, half), half)] = mine_ref[index].astype(jnp.float32)
    out_ref[pl.ds(pl.multiple_of((1 - core) * half, half), half)] = other_ref[index].astype(jnp.float32)


def link_kernel(where_ref, mine_ref, other_ref, lower_ref, lower_turned_ref, first_diag_ref, second_diag_ref,
                first_hbm, link_hbm, base_ref, sum_ref, first_ref, link_ref, sems):
    copies = [
        pltpu.make_async_copy(first_ref, first_hbm, sems.at[0]),
        pltpu.make_async_copy(link_ref, link_hbm, sems.at[1]),
    ]
    lower = lower_ref[...]
    turned = lower_turned_ref[...]
    place(where_ref, mine_ref, other_ref, 0, sum_ref)
    block_first = first_diag_ref[...] + sum_ref[...]
    first_ref[...] = block_first
    copies[0].start()
    place(where_ref, mine_ref, other_ref, 1, sum_ref)
    high, low = split(block_first)
    link = dot(high, lower) + dot(low, lower) + sum_ref[...].T
    link_ref[...] = -link
    copies[1].start()
    high, low = split(link)
    base_ref[...] = second_diag_ref[...] + dot(turned, high) + dot(turned, low)
    for copy in copies:
        copy.wait()


def last_kernel(where_ref, mine_ref, other_ref, base_ref, second_ref):
    place(where_ref, mine_ref, other_ref, 0, second_ref)
    second_ref[...] += base_ref[...]


def swapped(value, bit, devices):
    return lax.ppermute(value, "row", [(i, i ^ bit) for i in range(devices)])


def far_of(across, devices, closed=False):
    hops = [(i, i + 4 if i % 4 < 2 else i - 4) for i in range(devices)]
    pairs = [(a, b if 0 <= b < devices else a ^ 2) for a, b in hops]
    if not closed:
        pairs = [(a, b) for a, b in hops if 0 <= b < devices]
    return lax.ppermute(across, "row", pairs)


def rest_of(across, far, give_across, devices):
    pieces = [jnp.where(give_across, a, f) for a, f in zip(across, far)]
    return swapped(jnp.concatenate(pieces, axis=0), 1, devices)


def core_summed(give, keep, devices):
    return keep + swapped(give, 1, devices).astype(jnp.float32)


def step_summed(total, b, uppers, devices):
    give, keep = halved(total, uppers[b])
    return keep + swapped(give, 2 ** b, devices).astype(jnp.float32)


def halved(total, upper):
    half = total.shape[1] // 2
    low, high = total[:, :half], total[:, half:]
    return jnp.where(upper, low, high).astype(jnp.bfloat16), jnp.where(upper, high, low)


def summed(total, order, uppers, devices):
    halve, swap, double = order
    for b in halve:
        total = step_summed(total, b, uppers, devices)
    own = total.astype(jnp.bfloat16)
    gathered = (own.astype(jnp.float32) + swapped(own, 2 ** swap, devices).astype(jnp.float32)).astype(jnp.bfloat16)
    for b in double:
        other = swapped(gathered, 2 ** b, devices)
        low = jnp.where(uppers[b], other, gathered)
        high = jnp.where(uppers[b], gathered, other)
        gathered = jnp.concatenate([low, high], axis=1)
    return gathered, swapped(gathered, 1, devices)


def shards(sigma_blocks, first_panel, second_panel, lower_panel, first_diag, second_diag, task_list, task_count):
    barrier = lax.optimization_barrier
    devices = lax.axis_size("row")
    position = lax.axis_index("row").astype(jnp.int32)
    slots, size, width = sigma_blocks.shape[-3:]
    sigma = sigma_blocks.reshape((slots, size, width))
    first = first_panel.reshape((size, width))
    second = second_panel.reshape((size, width))
    where = position.reshape((1,))
    bits = [(position >> b) & 1 for b in range(devices.bit_length() - 1)]
    uppers = [bit == 1 for bit in bits]
    give_across = bits[0] == bits[1]
    where, uppers, give_across, first, second = barrier((where, uppers, give_across, first, second))
    listed = task_list.reshape((slots,))
    count = task_count.reshape((1,))
    one = 2 * size * size * width
    half = size // 2
    narrow = jax.ShapeDtypeStruct((size, width), jnp.bfloat16)
    wide = jax.ShapeDtypeStruct((size, width), jnp.float32)
    scratch = [pltpu.VMEM((size, width), jnp.float32)]

    def parts(k):
        return [jax.ShapeDtypeStruct((k, half, width), t) for t in (jnp.bfloat16, jnp.float32)]

    piece = jax.ShapeDtypeStruct((half, width), jnp.bfloat16)
    pieces = call(split_kernel, [piece] * 2, [first], "h", 1, [pltpu.SemaphoreType.DMA((2,))])
    across = [swapped(part, 2, devices) for part in pieces]
    second_across = swapped(second, 2, devices)
    beside = swapped(first, 1, devices)
    second_beside = swapped(second, 1, devices)
    first_acc, second_acc, turned, sorted_sigma, lower, lower_turned = call(
        near_kernel,
        [wide, wide, jax.ShapeDtypeStruct((2 * size, width), jnp.bfloat16),
         jax.ShapeDtypeStruct((3, size, width), jnp.bfloat16), narrow, narrow],
        [where, listed, count, sigma, lower_panel, *pieces, second, beside, second_beside],
        "ssshhvvvvv",
        4 * one,
        [pltpu.VMEM((2, size, width), jnp.bfloat16), pltpu.SemaphoreType.DMA((6,))],
    )
    far = [far_of(part, devices) for part in across]
    second_far = far_of(second_across, devices, closed=True)
    far, second_across, turned = barrier((far, second_across, turned))
    rest = rest_of(across, far, give_across, devices)
    column_first, column_again, give, keep = call(
        first_kernel,
        [narrow, narrow] + parts(2),
        [where, first_acc, *across, *far, rest, sorted_sigma, turned],
        "svvvvvvvv",
        5 * one,
        scratch,
    )
    give, second_across = barrier((give, second_across))
    total = core_summed(give, keep, devices)
    second_rest = rest_of([second_across], [second_far], give_across, devices)
    total = step_summed(total, 1, uppers, devices)
    (second_acc,) = call(
        across_kernel, [wide], [second_acc, column_again, lower, second_across, sorted_sigma], "vvvvv", 2 * one
    )
    column_second, second_give, second_keep = call(
        second_kernel,
        [narrow] + parts(1),
        [where, second_acc, second_far, second_rest, sorted_sigma, turned],
        "svvvvv",
        3 * one,
        scratch,
    )
    last = len(uppers) - 1
    second_total = core_summed(second_give, second_keep, devices)
    mine, other = summed(total, (range(2, last), last, range(last - 1, 0, -1)), uppers, devices)
    second_mine, second_other = summed(
        second_total, (range(2, last + 1), 1, range(last, 1, -1)), uppers, devices
    )
    block_first, block_link, base = call(
        link_kernel,
        [wide] * 3,
        [where, mine, other, lower, lower_turned, first_diag, second_diag],
        "svvvvvv",
        4 * one,
        scratch * 3 + [pltpu.SemaphoreType.DMA((2,))],
        "hhv",
    )
    (block_second,) = call(last_kernel, [wide], [where, second_mine, second_other, base], "svvv", size * width)
    shape = first_panel.shape
    return column_first.reshape(shape), block_first, block_link, column_second.reshape(shape), block_second


def solution(mesh):
    return jax.shard_map(
        shards,
        mesh=mesh,
        in_specs=(
            P("groups", "row", None, None, None),
            P("groups", "row", None, None),
            P("groups", "row", None, None),
            P("groups", None),
            P("groups", None),
            P("groups", None),
            P("groups", "row", None),
            P("groups", "row"),
        ),
        out_specs=(
            P("groups", "row", None, None),
            P("groups", None),
            P("groups", None),
            P("groups", "row", None, None),
            P("groups", None),
        ),
        check_vma=False,
    )
```
